32 devices in a mesh: fsdp: 16 (over z, y, core), tp: 2 (over x).
Axes of the slice: x: 2, y: 2, z: 4, core: 2. Of those that a mesh axis runs over, the one named last changes fastest.
Arguments:
- tokens: bfloat16 [16384, 768], P(('fsdp', 'tp')), may hold values from -6 to 6
- segments: int32 [16, 1024], P('fsdp'), may hold values from 0 to 15, never falling along the last dimension, each value on 1 to 768 neighbouring positions
- qkv_weight: bfloat16 [1, 3, 768, 768], P(None, None, 'fsdp', 'tp'), may hold values from -0.21875 to 0.21875
- out_weight: bfloat16 [1, 768, 768], P(None, 'tp', 'fsdp'), may hold values from -0.875 to 0.875
- gate_up_weight: bfloat16 [1, 2, 768, 3072], P(None, None, 'fsdp', 'tp'), may hold values from -0.21875 to 0.21875
- down_weight: bfloat16 [1, 3072, 768], P(None, 'tp', 'fsdp'), may hold values from -0.109375 to 0.109375
- norm_gain: bfloat16 [1, 2, 768], P(None, None, 'fsdp'), may hold values from 0.5 to 1.5
- norm_shift: bfloat16 [1, 2, 768], P(None, None, 'fsdp'), may hold values from -1.5 to 1.5
- cotangent: bfloat16 [16384, 768], P(('fsdp', 'tp')), may hold values from -6 to 6
Outputs:
- activations: bfloat16 [16384, 768], P(('fsdp', 'tp'))
- grad_tokens: float32 [16384, 768], P(('fsdp', 'tp'))
- grad_qkv: float32 [1, 3, 768, 768], P(None, None, 'fsdp', 'tp')
- grad_out: float32 [1, 768, 768], P(None, 'tp', 'fsdp')
- grad_gate_up: float32 [1, 2, 768, 3072], P(None, None, 'fsdp', 'tp')
- grad_down: float32 [1, 3072, 768], P(None, 'tp', 'fsdp')
- grad_norm_gain: float32 [1, 2, 768], P(None, None, 'fsdp')
- grad_norm_shift: float32 [1, 2, 768], P(None, None, 'fsdp')
The draws below stay inside these ranges and needn't reach their ends.
Inputs may be any that keep to these rules, and one draw needn't show every extreme that they name: `segments`: within each sequence the numbers never fall; a document is a run of equal numbers.
All inputs are finite; a program needn't handle non-finite values.
Results may differ from the reference program's by a relative error of at most 0.018.
Values may be sent and summed in bfloat16 or wider, within the bound.
A program may use at most 128 MiB of HBM per device.

```python
import math
import jax
import jax.numpy as jnp
import numpy as np
from jax import lax

D = 768
HEADS = 12
FF = 3072
HEAD_DIM = 64
LAYERS = 1
LEN = 1024
SEQS = 16
TOKENS = 16384
QBLOCK = 512
DOCS = 16
MOST_DOC = 768


def with_spikes(drawn, key, source, target, shards_of, factor):
    def block_of(position):
        return (jnp.arange(drawn.shape[position]) // (drawn.shape[position] // shards_of)).reshape((-1,) + (1,) * (drawn.ndim - 1 - position))

    near = jax.random.permutation(key, shards_of)[block_of(target)]
    far = (block_of(target) + shards_of // 2) % shards_of
    return jnp.where((block_of(source) == near) | (block_of(source) == far), factor * drawn, drawn)


def shard_levels(key, dims, shards, low, largest):
    level, own = 1.0, jax.random.fold_in(key, 6)
    for axis_at, blocks in shards:
        steps = jnp.exp(jax.random.uniform(jax.random.fold_in(own, axis_at), (blocks,), jnp.float32, low / len(shards), largest / len(shards)))
        level = level * jnp.repeat(steps, dims[axis_at] // blocks).reshape([-1 if axis == axis_at else 1 for axis in range(len(dims))])
    return level


def split_up(number_of, total, bound, slope):
    loads = [(1 << 20) // math.isqrt(grade ** slope) + 1 for grade in range(2, number_of + 1)]
    spare, counts = total - bound - (number_of - 1), [1] * (number_of - 1)
    while spare > 0:
        movable = [i for i in range(number_of - 1) if counts[i] < bound]
        mass, left = sum([loads[i] for i in movable]), spare
        for i in movable:
            extra = min(bound - counts[i], max(1, left * loads[i] // mass), spare)
            counts[i] = counts[i] + extra
            spare = spare - extra
    return np.array([bound] + counts)


def ragged(stream_key, number_of, total, reach, lean):
    if number_of == 2:
        one = jax.random.randint(stream_key, (), max(1, total - reach), min(reach, total - 1) + 1)
        return jnp.stack([one, total - one])
    lengths = jnp.asarray(split_up(number_of, total, reach, lean), jnp.int32)
    pairs = (number_of - 1) // 2
    source_of, receiver = lengths[1:1 + 2 * pairs:2], lengths[2:2 + 2 * pairs:2]
    slack = jnp.minimum(source_of - 1, reach - receiver)
    shifted = jax.random.randint(jax.random.fold_in(stream_key, 1), (pairs,), 0, 1 << 20) % (slack + 1)
    lengths = lengths.at[1:1 + 2 * pairs:2].set(source_of - shifted).at[2:2 + 2 * pairs:2].set(receiver + shifted)
    return lengths[jax.random.permutation(jax.random.fold_in(stream_key, 2), number_of)]


def noise(own_key, shape, deviation, reach, shards=(), held_as=jnp.bfloat16):
    entries = deviation * jax.random.normal(own_key, shape, jnp.float32)
    if shards:
        entries = entries * shard_levels(own_key, shape, shards, -0.22, 0.18)
    return jnp.clip(entries, -reach, reach).astype(held_as)


def gaussian_with(own_key, dims, spread, bound, cuts, heavy, held_as=jnp.bfloat16):
    entries = spread * jax.random.normal(own_key, dims, jnp.float32)
    if cuts:
        entries = entries * shard_levels(own_key, dims, cuts, -0.22, 0.18)
    return jnp.clip(with_spikes(entries, jax.random.fold_in(own_key, 3), *heavy), -bound, bound).astype(held_as)


def setup_inputs(seed: int = 0) -> dict:
    splits = jax.random.split(jax.random.key(seed), 10)
    return {
        "tokens": noise(splits[0], (TOKENS, D), 1.0, 6.0, ((0, 32),)),
        "segments": jax.vmap(lambda own: jnp.searchsorted(jnp.cumsum(ragged(own, DOCS, LEN, MOST_DOC, 2)), jnp.arange(LEN), side="right"))(jax.random.split(splits[1], SEQS)).reshape((SEQS, LEN)).astype(jnp.int32),
        "qkv_weight": noise(splits[2], (LAYERS, 3, D, D), D ** -0.5, 0.21875, ((2, 16), (3, 2))),
        "out_weight": noise(splits[3], (LAYERS, D, D), (D // 16) ** -0.5, 0.875, ((1, 2), (2, 16))),
        "gate_up_weight": noise(splits[4], (LAYERS, 2, D, FF), D ** -0.5, 0.21875, ((2, 16), (3, 2))),
        "down_weight": noise(splits[5], (LAYERS, FF, D), FF ** -0.5, 0.109375, ((1, 2), (2, 16))),
        "norm_gain": jnp.clip(0.5 + 1.0 * jax.random.uniform(splits[6], (LAYERS, 2, D), jnp.float32) ** shard_levels(splits[6], (LAYERS, 2, D), ((2, 16),), -0.2, 0.2), 0.5, 1.5).astype(jnp.bfloat16),
        "norm_shift": noise(splits[7], (LAYERS, 2, D), 0.3, 1.5, ((2, 16),)),
        "cotangent": gaussian_with(splits[8], (TOKENS, D), 1.0, 6.0, ((0, 32),), (0, 1, 32, 2.75)),
    }


@jax.custom_vjp
def low(v):
    return lax.optimization_barrier(v.astype(jnp.bfloat16)).astype(jnp.float32)

@jax.custom_vjp
def low_back(v):
    return v

def low_keep(v):
    return (low(v), None)

def low_pass(kept, grad):
    return (grad,)

def back_keep(v):
    return (v, None)

def back_low(kept, grad):
    return (low(grad),)
low.defvjp(low_keep, low_pass)
low_back.defvjp(back_keep, back_low)
highest = lax.Precision.HIGHEST
epsilon = 1e-05

def rope_tables(length):
    half_dim = HEAD_DIM // 2
    inv_freq = 1000.0 ** (-jnp.arange(half_dim, dtype=jnp.float32) * 2.0 / HEAD_DIM)
    angles = jnp.arange(length, dtype=jnp.float32)[:, None] * inv_freq[None, :]
    cosine = jnp.concatenate([jnp.cos(angles), jnp.cos(angles)], axis=-1)[:, None, :]
    sine_table = jnp.concatenate([jnp.sin(angles), jnp.sin(angles)], axis=-1)[:, None, :]
    return (cosine, sine_table)

def rotate(values_in, cosine, sine_table):
    half_dim = values_in.shape[-1] // 2
    turned = jnp.concatenate([-values_in[..., half_dim:], values_in[..., :half_dim]], axis=-1)
    return values_in * cosine + turned * sine_table

def norm_rows(stream, scale_vec, shift_vec):
    row_mean = lax.optimization_barrier(jnp.mean(stream, axis=-1, keepdims=True))
    centred = stream - row_mean
    row_var = lax.optimization_barrier(jnp.mean(centred * centred, axis=-1, keepdims=True))
    return centred * lax.rsqrt(row_var + epsilon) * scale_vec + shift_vec

def attention(queries, keys_rot, values, seg_row):

    def one_block(block_item):
        query_blk, seg_blk = block_item
        scores = jnp.einsum('qhd,khd->hqk', query_blk, keys_rot, precision=highest) * HEAD_DIM ** (-0.5)
        joined = seg_blk[:, None] == seg_row[None, :]
        scores = low_back(jnp.where(joined[None], scores, -1e+30))
        attn_probs = low(jax.nn.softmax(scores, axis=-1))
        return jnp.einsum('hqk,khd->qhd', attn_probs, values, precision=highest)
    block_count = LEN // QBLOCK
    block_items = (queries.reshape(block_count, QBLOCK, HEADS, HEAD_DIM), seg_row.reshape(block_count, QBLOCK))
    return lax.map(jax.checkpoint(one_block), block_items).reshape(LEN, D)

def layer_apply(stream, weights, seg_row, tables):
    qkv_w, out_w, gate_up_w, down_w, gain_vals, shift_vals = weights
    cosine, sine_table = tables
    shaped = (LEN, HEADS, HEAD_DIM)
    inputs = low(stream)
    query_pre = low_back(jnp.dot(inputs, qkv_w[0], precision=highest)).reshape(shaped)
    key_pre = low_back(jnp.dot(inputs, qkv_w[1], precision=highest)).reshape(shaped)
    queries = low(rotate(query_pre, cosine, sine_table))
    keys_rot = low(rotate(key_pre, cosine, sine_table))
    values = low(low_back(jnp.dot(inputs, qkv_w[2], precision=highest))).reshape(shaped)
    attended = low(low_back(attention(queries, keys_rot, values, seg_row)))
    branch = low_back(jnp.dot(attended, out_w, precision=highest))
    first_norm = norm_rows(stream + branch, gain_vals[0], shift_vals[0])
    middle = low(first_norm)
    gate_pre = low_back(jnp.dot(middle, gate_up_w[0], precision=highest))
    up_proj = low_back(jnp.dot(middle, gate_up_w[1], precision=highest))
    hidden = low(low_back(jax.nn.silu(gate_pre) * up_proj))
    branch_two = low_back(jnp.dot(hidden, down_w, precision=highest))
    return norm_rows(first_norm + branch_two, gain_vals[1], shift_vals[1])

def reference(tokens, segments, qkv_weight, out_weight, gate_up_weight, down_weight, norm_gain, norm_shift, cotangent):
    params = tuple((weight_part.astype(jnp.float32) for weight_part in (qkv_weight, out_weight, gate_up_weight, down_weight, norm_gain, norm_shift)))
    tables = rope_tables(LEN)
    streams = tokens.astype(jnp.float32).reshape(SEQS, LEN, D)
    cot_rows = cotangent.astype(jnp.float32).reshape(SEQS, LEN, D)

    def one_sequence(running, seq_item):
        stream, seg_row, cot_row = seq_item

        def forward(stream_in, layer_params):
            for layer_index in range(LAYERS):
                stream_in = layer_apply(stream_in, tuple((weight_part[layer_index] for weight_part in layer_params)), seg_row, tables)
            return stream_in
        final, pullback = jax.vjp(forward, stream, params)
        grad_stream, grad_params = pullback(cot_row)
        running = tuple((run_total + grad_part for run_total, grad_part in zip(running, grad_params)))
        return (running, (final.astype(jnp.bfloat16), grad_stream))
    zero_grads = tuple((jnp.zeros(weight_part.shape, jnp.float32) for weight_part in params))
    grad_sums, (finals, grad_rows) = lax.scan(one_sequence, zero_grads, (streams, segments, cot_rows))
    return (finals.reshape(TOKENS, D), grad_rows.reshape(TOKENS, D), grad_sums[0], grad_sums[1], grad_sums[2], grad_sums[3], grad_sums[4], grad_sums[5])
```

```python
import functools

import jax
import jax.numpy as jnp
import numpy as np
from jax import lax
from jax.experimental import pallas as pl
from jax.experimental.pallas import tpu as pltpu
from jax.sharding import PartitionSpec as P

HEAD_DIM = 64


epsilon = 1e-05


def for_sending(value):

    def short(part):
        return part.astype(jnp.bfloat16) if part.dtype == jnp.float32 else part

    return jax.tree.map(short, value)


def rope_tables(length):
    half_dim = HEAD_DIM // 2
    inv_freq = 1000.0 ** (-jnp.arange(half_dim, dtype=jnp.float32) * 2.0 / HEAD_DIM)
    angles = jnp.arange(length, dtype=jnp.float32)[:, None] * inv_freq[None, :]
    cosine = jnp.concatenate([jnp.cos(angles), jnp.cos(angles)], axis=-1)[:, None, :]
    sine_table = jnp.concatenate([jnp.sin(angles), jnp.sin(angles)], axis=-1)[:, None, :]
    return (cosine, sine_table)


def rotate(values_in, cosine, sine_table):
    half_dim = values_in.shape[-1] // 2
    turned = jnp.concatenate([-values_in[..., half_dim:], values_in[..., :half_dim]], axis=-1)
    return values_in * cosine + turned * sine_table


def unrotate(grads_in, cosine, sine_table):
    half_dim = grads_in.shape[-1] // 2
    moved_part = grads_in * sine_table
    return grads_in * cosine + jnp.concatenate(
        [moved_part[..., half_dim:], -moved_part[..., :half_dim]], axis=-1
    )


def norm_rows(stream, scale_vec, shift_vec):
    row_mean = jnp.mean(stream, axis=-1, keepdims=True)
    centred = stream - row_mean
    row_var = jnp.mean(centred * centred, axis=-1, keepdims=True)
    return centred * lax.rsqrt(row_var + epsilon) * scale_vec + shift_vec


def swiglu(gate_pre, up_proj):
    return jax.nn.silu(gate_pre) * up_proj


def spread(stream_low):
    return lax.all_gather(stream_low, "tp", axis=0, tiled=True)


def collect(partial_rows):
    return lax.psum_scatter(
        partial_rows.astype(jnp.bfloat16), "tp", scatter_dimension=0, tiled=True
    ).astype(jnp.float32)


def spread_grads(grads_low):
    return lax.all_gather(grads_low, "tp", axis=0, tiled=True)


def collect_grads(partial_rows):
    return lax.psum_scatter(
        partial_rows.astype(jnp.bfloat16), "tp", scatter_dimension=0, tiled=True
    ).astype(jnp.float32)


def layer_shards(arrays, layer_index):
    return tuple((weight_part[layer_index] for weight_part in arrays))


def block_scores(query_blk, keys_seq, seg_blk, seg_seq):
    scores = jnp.einsum(
        "qhd,khd->hqk", query_blk, keys_seq, preferred_element_type=jnp.float32
    ) * HEAD_DIM ** (-0.5)
    joined = seg_blk[:, None] == seg_seq[None, :]
    return jnp.where(joined[None], scores, -1e30)


def attend_forward(queries, keys_rot, values, segments):
    seq_count, length = segments.shape
    block_rows = min(512, length)
    block_count = length // block_rows

    def attend_one_block(flat_index):
        sequence = flat_index // block_count
        row_start = flat_index % block_count * block_rows
        query_seq = lax.dynamic_index_in_dim(queries, sequence, 0, False)
        keys_seq = lax.dynamic_index_in_dim(keys_rot, sequence, 0, False)
        values_seq = lax.dynamic_index_in_dim(values, sequence, 0, False)
        seg_seq = lax.dynamic_index_in_dim(segments, sequence, 0, False)
        query_blk = lax.dynamic_slice_in_dim(query_seq, row_start, block_rows, 0)
        seg_blk = lax.dynamic_slice_in_dim(seg_seq, row_start, block_rows, 0)
        scores = block_scores(query_blk, keys_seq, seg_blk, seg_seq)
        row_max = jnp.max(scores, axis=-1, keepdims=True)
        exp_terms = jnp.exp(scores - row_max)
        row_total = jnp.sum(exp_terms, axis=-1, keepdims=True)
        probs_low = (exp_terms / row_total).astype(jnp.bfloat16)
        attended = jnp.einsum(
            "hqk,khd->qhd", probs_low, values_seq, preferred_element_type=jnp.float32
        )
        return (attended, row_max + jnp.log(row_total))

    attended, log_total = lax.map(
        attend_one_block, jnp.arange(seq_count * block_count, dtype=jnp.int32)
    )
    return (attended.reshape(seq_count * length, -1), log_total)


def attend_backward(queries, keys_rot, values, d_attended, log_total, segments):
    seq_count, length = segments.shape
    block_rows = min(512, length)
    block_count = length // block_rows
    scale_value = HEAD_DIM ** (-0.5)

    def one_sequence(sequence):
        query_seq = lax.dynamic_index_in_dim(queries, sequence, 0, False)
        keys_seq = lax.dynamic_index_in_dim(keys_rot, sequence, 0, False)
        values_seq = lax.dynamic_index_in_dim(values, sequence, 0, False)
        d_out_seq = lax.dynamic_index_in_dim(d_attended, sequence, 0, False)
        seg_seq = lax.dynamic_index_in_dim(segments, sequence, 0, False)

        def one_one_block(running, block_index):
            row_start = block_index * block_rows
            query_blk = lax.dynamic_slice_in_dim(query_seq, row_start, block_rows, 0)
            d_out_blk = lax.dynamic_slice_in_dim(d_out_seq, row_start, block_rows, 0)
            seg_blk = lax.dynamic_slice_in_dim(seg_seq, row_start, block_rows, 0)
            block_total = lax.dynamic_index_in_dim(
                log_total, sequence * block_count + block_index, 0, False
            )
            scores = block_scores(query_blk, keys_seq, seg_blk, seg_seq)
            attn_probs = jnp.exp(scores - block_total)
            probs_low = attn_probs.astype(jnp.bfloat16)
            d_probs = jnp.einsum(
                "qhd,khd->hqk", d_out_blk, values_seq, preferred_element_type=jnp.float32
            )
            inner_sum = jnp.sum(attn_probs * d_probs, axis=-1, keepdims=True)
            d_scores = (attn_probs * (d_probs - inner_sum)).astype(jnp.bfloat16)
            d_query = (
                jnp.einsum("hqk,khd->qhd", d_scores, keys_seq, preferred_element_type=jnp.float32)
                * scale_value
            )
            d_key = (
                running[0]
                + jnp.einsum(
                    "hqk,qhd->khd", d_scores, query_blk, preferred_element_type=jnp.float32
                )
                * scale_value
            )
            d_value = running[1] + jnp.einsum(
                "hqk,qhd->khd", probs_low, d_out_blk, preferred_element_type=jnp.float32
            )
            return ((d_key, d_value), d_query)

        zero_keys = jnp.zeros(keys_seq.shape, jnp.float32)
        (d_keys, d_values), d_queries = lax.scan(
            one_one_block, (zero_keys, zero_keys), jnp.arange(block_count, dtype=jnp.int32)
        )
        return (d_queries.reshape(keys_seq.shape), d_keys, d_values)

    return lax.map(one_sequence, jnp.arange(seq_count, dtype=jnp.int32))


def layer_forward(stream, segments, weights, tables):
    qkv_w, out_w, gate_up_w, down_w, gain_rows, shift_rows = weights
    cosine, sine_table = tables
    seq_count, length = segments.shape
    head_count = qkv_w.shape[2] // HEAD_DIM
    shaped = (seq_count, length, head_count, HEAD_DIM)
    gain_vals = gain_rows.astype(jnp.float32)
    shift_vals = shift_rows.astype(jnp.float32)
    inputs = spread(stream.astype(jnp.bfloat16))
    query_pre = jnp.dot(inputs, qkv_w[0], preferred_element_type=jnp.float32).reshape(shaped)
    key_pre = jnp.dot(inputs, qkv_w[1], preferred_element_type=jnp.float32).reshape(shaped)
    queries = rotate(query_pre, cosine, sine_table).astype(jnp.bfloat16)
    keys_rot = rotate(key_pre, cosine, sine_table).astype(jnp.bfloat16)
    values = (
        jnp.dot(inputs, qkv_w[2], preferred_element_type=jnp.float32)
        .astype(jnp.bfloat16)
        .reshape(shaped)
    )
    attended, log_total = attend_forward(queries, keys_rot, values, segments)
    attended_low = attended.astype(jnp.bfloat16)
    branch = collect(jnp.dot(attended_low, out_w, preferred_element_type=jnp.float32))
    mixed = stream + branch
    first_norm = norm_rows(mixed, gain_vals[0], shift_vals[0])
    middle = spread(first_norm.astype(jnp.bfloat16))
    gate_pre = jnp.dot(middle, gate_up_w[0], preferred_element_type=jnp.float32)
    up_proj = jnp.dot(middle, gate_up_w[1], preferred_element_type=jnp.float32)
    hidden = swiglu(gate_pre, up_proj).astype(jnp.bfloat16)
    branch_two = collect(jnp.dot(hidden, down_w, preferred_element_type=jnp.float32))
    second_in = first_norm + branch_two
    saved_state = (
        inputs,
        queries,
        keys_rot,
        values,
        log_total,
        attended_low,
        mixed,
        middle,
        gate_pre,
        up_proj,
        hidden,
        second_in,
    )
    return (norm_rows(second_in, gain_vals[1], shift_vals[1]), saved_state)


def layer_backward(grad_out, saved_state, segments, weights, tables):
    qkv_w, out_w, gate_up_w, down_w, gain_rows, shift_rows = weights
    (
        inputs,
        queries,
        keys_rot,
        values,
        log_total,
        attended_low,
        mixed,
        middle,
        gate_pre,
        up_proj,
        hidden,
        second_in,
    ) = saved_state
    cosine, sine_table = tables
    gain_vals = gain_rows.astype(jnp.float32)
    shift_vals = shift_rows.astype(jnp.float32)
    unused_two, norm_two_back = jax.vjp(norm_rows, second_in, gain_vals[1], shift_vals[1])
    d_second, d_gain_two, d_shift_two = norm_two_back(grad_out)
    d_branch_two = spread_grads(d_second.astype(jnp.bfloat16))
    grad_down = jnp.einsum("rf,rd->fd", hidden, d_branch_two, preferred_element_type=jnp.float32)
    d_hidden_low = jnp.einsum(
        "rd,fd->rf", d_branch_two, down_w, preferred_element_type=jnp.float32
    ).astype(jnp.bfloat16)
    d_hidden = lax.optimization_barrier(d_hidden_low).astype(jnp.float32)
    unused_swish, swish_back = jax.vjp(swiglu, gate_pre, up_proj)
    d_gate, d_up = swish_back(d_hidden)
    d_gate_low = d_gate.astype(jnp.bfloat16)
    d_up_low = d_up.astype(jnp.bfloat16)
    grad_gate_up = jnp.stack(
        [
            jnp.einsum("rd,rf->df", middle, d_gate_low, preferred_element_type=jnp.float32),
            jnp.einsum("rd,rf->df", middle, d_up_low, preferred_element_type=jnp.float32),
        ]
    )
    d_middle = jnp.einsum("rf,df->rd", d_gate_low, gate_up_w[0], preferred_element_type=jnp.float32)
    d_middle = d_middle + jnp.einsum(
        "rf,df->rd", d_up_low, gate_up_w[1], preferred_element_type=jnp.float32
    )
    d_first = d_second + collect_grads(d_middle)
    unused_one, norm_one_back = jax.vjp(norm_rows, mixed, gain_vals[0], shift_vals[0])
    d_mixed, d_gain_one, d_shift_one = norm_one_back(d_first)
    d_branch = spread_grads(d_mixed.astype(jnp.bfloat16))
    grad_out_w = jnp.einsum("rc,rd->cd", attended_low, d_branch, preferred_element_type=jnp.float32)
    d_attended = (
        jnp.einsum("rd,cd->rc", d_branch, out_w, preferred_element_type=jnp.float32)
        .astype(jnp.bfloat16)
        .reshape(queries.shape)
    )
    d_queries, d_keys, d_values = attend_backward(
        queries, keys_rot, values, d_attended, log_total, segments
    )
    flat_shape = (-1, queries.shape[2] * queries.shape[3])
    d_query_low = unrotate(d_queries, cosine, sine_table).astype(jnp.bfloat16).reshape(flat_shape)
    d_key_low = unrotate(d_keys, cosine, sine_table).astype(jnp.bfloat16).reshape(flat_shape)
    d_value_low = d_values.astype(jnp.bfloat16).reshape(flat_shape)
    grad_parts = (d_query_low, d_key_low, d_value_low)
    grad_qkv = jnp.stack(
        [
            jnp.einsum("rd,rc->dc", inputs, grad_part, preferred_element_type=jnp.float32)
            for grad_part in grad_parts
        ]
    )
    d_inputs = jnp.einsum("rc,dc->rd", d_query_low, qkv_w[0], preferred_element_type=jnp.float32)
    d_inputs = d_inputs + jnp.einsum(
        "rc,dc->rd", d_key_low, qkv_w[1], preferred_element_type=jnp.float32
    )
    d_inputs = d_inputs + jnp.einsum(
        "rc,dc->rd", d_value_low, qkv_w[2], preferred_element_type=jnp.float32
    )
    d_stream = d_mixed + collect_grads(d_inputs)
    weight_grads = (
        grad_qkv,
        grad_out_w,
        grad_gate_up,
        grad_down,
        jnp.stack([d_gain_one, d_gain_two]),
        jnp.stack([d_shift_one, d_shift_two]),
    )
    return (d_stream, weight_grads)


def on_device(
    tokens,
    segments,
    qkv_weight,
    out_weight,
    gate_up_weight,
    down_weight,
    norm_gain,
    norm_shift,
    cotangent,
):
    arrays = (qkv_weight, out_weight, gate_up_weight, down_weight, norm_gain, norm_shift)
    layer_total = qkv_weight.shape[0]
    tables = rope_tables(segments.shape[1])
    stream = tokens.astype(jnp.float32)
    kept_weights = []
    layer_index = 0
    weights = lax.all_gather(
        for_sending(layer_shards(arrays, layer_index)), "fsdp", axis=1, tiled=True
    )
    stream, saved_state = layer_forward(stream, segments, weights, tables)
    kept_weights.append(weights)
    saved_states = [saved_state]
    activations = stream.astype(jnp.bfloat16)
    grad_stream = cotangent.astype(jnp.float32)
    grad_layers = [None] * layer_total
    for layer_index in reversed(range(layer_total)):
        weights = lax.all_gather(
            for_sending(layer_shards(arrays, layer_index)), "fsdp", axis=1, tiled=True
        )
        grad_stream, weight_grads = layer_backward(
            grad_stream, saved_states[layer_index], segments, weights, tables
        )
        grad_layers[layer_index] = (
            lax.psum_scatter(weight_grads[0], "fsdp", scatter_dimension=1, tiled=True),
            lax.psum_scatter(weight_grads[1], "fsdp", scatter_dimension=1, tiled=True),
            lax.psum_scatter(weight_grads[2], "fsdp", scatter_dimension=1, tiled=True),
            lax.psum_scatter(weight_grads[3], "fsdp", scatter_dimension=1, tiled=True),
            lax.psum_scatter(weight_grads[4], "fsdp", scatter_dimension=1, tiled=True),
            lax.psum_scatter(weight_grads[5], "fsdp", scatter_dimension=1, tiled=True),
        )
    stacked = [jnp.stack([grad_layers[0][member]]) for member in range(6)]
    gain_sum, shift_sum = lax.psum((stacked[4], stacked[5]), "tp")
    return (
        activations,
        grad_stream,
        stacked[0],
        stacked[1],
        stacked[2],
        stacked[3],
        gain_sum,
        shift_sum,
    )


MESH_ID = pl.DeviceIdType.MESH
BF = jnp.bfloat16
F32 = jnp.float32
NZ, NY = 4, 2
PQ, PK, PV, PO, PG0, PG1, PG2, PD0, PD1, PD2 = range(10)
NPARTS = 10
PAIRS = 3
NEG = -1e30


def nt(a, b):
    return lax.dot_general(a, b, (((1,), (1,)), ((), ())), preferred_element_type=F32)


def nn(a, b):
    return jnp.dot(a, b, preferred_element_type=F32)


def rope_numpy(length):
    half = HEAD_DIM // 2
    inv = 1000.0 ** (-np.arange(half, dtype=np.float64) * 2.0 / HEAD_DIM)
    angles = np.arange(length, dtype=np.float64)[:, None] * inv[None, :]
    cosine, sine = np.cos(angles), np.sin(angles)
    cos_rows = np.concatenate([cosine, cosine, cosine, cosine], axis=1)
    sin_rows = np.concatenate([-sine, sine, -sine, sine], axis=1)
    return cos_rows.astype(np.float32), sin_rows.astype(np.float32)


def layer_kernel(
    dims,
    tok_ref, cot_ref, seg_ref, cos_ref, sin_ref, qkv_in, o_in, gu_in, d_in,
    act_out, gtok_out, gq_out, go_out, ggu_out, gd_out,
    W, G, Ly, Lz, Lx, F, X, XT, Q, K, V, A, M, MT, DT, GT, UP, H, R, C, N1, N2, RS1, RS2,
    DQT, LSE, LST, DEL, DLT, SEGR, SEGC, NV, NG, NGR, NGT, GL,
    sLC, sCR, rCR, sB, rB, sY, rY, sZ, rZ, sX, rX, sF, rF, sO, sM, rM, cred,
):
    LEN, D, HC, FC = dims
    HALF = LEN // 2
    SH = D // 16
    BR = 2 * SH
    CH = FC // 3
    OW = HC + 128
    cols = {PQ: (0, HC), PK: (HC, HC), PV: (2 * HC, HC), PO: (3 * HC, OW)}
    at = 3 * HC + OW
    for p in (PG0, PG1, PG2):
        cols[p] = (at, 2 * CH)
        at += 2 * CH
    for p in (PD0, PD1, PD2):
        cols[p] = (at, CH)
        at += CH

    f = lax.axis_index("fsdp")
    t = lax.axis_index("tp")
    c = lax.rem(f, 2)
    y = lax.rem(f // 2, 2)
    z = f // 4
    oc = 1 - c
    native = c == t
    away = c != t
    dev_x = (f, 1 - t)
    dev_y = ((z * 2 + (1 - y)) * 2 + c, t)
    dev_c = ((z * 2 + y) * 2 + oc, t)
    dev_d = ((z * 2 + y) * 2 + oc, 1 - t)

    def zof(dz):
        return lax.rem(z + dz, NZ)

    def dev_z(dz):
        return ((zof(dz) * 2 + y) * 2 + c, t)

    def rows_of(zz, yy):
        return pl.ds(pl.multiple_of((zz * 2 + yy) * BR, 16), BR)

    def blk(ref, p, zz, yy):
        return ref.at[rows_of(zz, yy), pl.ds(cols[p][0], cols[p][1])]

    def bid(zz, yy):
        return zz * 2 + yy

    def rc(src, dst, ss, rs, dev):
        return pltpu.make_async_remote_copy(
            src_ref=src, dst_ref=dst, send_sem=ss, recv_sem=rs, device_id=dev, device_id_type=MESH_ID
        )

    def got(dst, rs, ss):
        rc(dst, dst, ss, rs, dev_x).wait_recv()

    own_r = pl.multiple_of(c * HALF, HALF)
    oth_r = pl.multiple_of(oc * HALF, HALF)
    own_rows = pl.ds(own_r, HALF)
    oth_rows = pl.ds(oth_r, HALF)

    bar = pltpu.get_barrier_semaphore()
    partners = [dev_x, dev_y, dev_c, dev_d, dev_z(1), dev_z(2), dev_z(3)]
    for dev in partners:
        pl.semaphore_signal(bar, inc=1, device_id=dev, device_id_type=MESH_ID)
    pl.semaphore_wait(bar, len(partners))

    def shard_copies(p):
        c0, n = cols[p]
        if p in (PQ, PK, PV):
            return [(qkv_in.at[p], c0, n)]
        if p == PO:
            return [(o_in, c0, n)]
        if p in (PG0, PG1, PG2):
            j = p - PG0
            return [(gu_in.at[i, :, pl.ds(j * CH, CH)], c0 + i * CH, CH) for i in range(2)]
        j = p - PD0
        return [(d_in.at[:, pl.ds(j * CH, CH)], c0, CH)]

    shard_rows = pl.ds(pl.multiple_of((z * 2 + y) * BR + c * SH, 16), SH)
    oshard_rows = pl.ds(pl.multiple_of((z * 2 + y) * BR + oc * SH, 16), SH)

    def shard_local(p):
        return [
            pltpu.make_async_copy(src, W.at[shard_rows, pl.ds(c0, n)], sLC.at[p, i])
            for i, (src, c0, n) in enumerate(shard_copies(p))
        ]

    def shard_remote(p):
        return [
            rc(src, W.at[shard_rows, pl.ds(c0, n)], sCR.at[p, i], rCR.at[p, i], dev_c)
            for i, (src, c0, n) in enumerate(shard_copies(p))
        ]

    def shard_arrivals(p):
        return [
            rc(W.at[oshard_rows, pl.ds(c0, n)], W.at[oshard_rows, pl.ds(c0, n)], sCR.at[p, i], rCR.at[p, i], dev_c)
            for i, (src, c0, n) in enumerate(shard_copies(p))
        ]

    seg_home = pltpu.make_async_copy(seg_ref, SEGR, sM.at[0])
    seg_send = rc(seg_ref, SEGR, sM.at[1], rM.at[1], dev_c)
    tok_home = pltpu.make_async_copy(tok_ref, X.at[own_rows], sM.at[2])
    tok_core = rc(tok_ref, X.at[own_rows], sM.at[3], rM.at[3], dev_c)
    tok_away = rc(tok_ref, X.at[oth_rows], sM.at[4], rM.at[4], dev_d)
    tok_pass = rc(X.at[own_rows], X.at[own_rows], sM.at[3], rM.at[3], dev_c)
    cot_home = pltpu.make_async_copy(cot_ref, C, sM.at[5])
    cot_away = rc(cot_ref, C, sM.at[5], rM.at[5], dev_d)

    @pl.when(native)
    def _():
        for p in range(NPARTS):
            for cp in shard_local(p):
                cp.start()
        seg_home.start()
        seg_send.start()
        tok_home.start()
        tok_core.start()
        cot_home.start()

    @pl.when(away)
    def _():
        for p in range(NPARTS):
            for cp in shard_remote(p):
                cp.start()
            if p == PQ:
                tok_away.start()
        cot_away.start()

    MODE_FIRST = (PQ, PV, PG1, PD1)
    sends = {}

    def send_b(p, k, zz, yy, dev):
        b = blk(W, p, zz, yy)
        return rc(b, b, sB.at[p, k], rB.at[p, bid(zz, yy)], dev)

    def first_sends(p):
        return [send_b(p, dz - 1, z, y, dev_z(dz)) for dz in (1, 2, 3)] + [send_b(p, 3, z, y, dev_y)]

    def x_own(p):
        return send_b(p, 4, z, y, dev_x)

    def y_fwd(p, dz):
        return send_b(p, 4 + dz, zof(dz), y, dev_y)

    def x_fwd(p, dz):
        return send_b(p, 7 + dz, zof(dz), y, dev_x)

    def x_fwd_y(p, dz):
        return send_b(p, 11 + dz, zof(dz), 1 - y, dev_x)

    def ag1(p):
        @pl.when(native)
        def _():
            for cp in shard_local(p):
                cp.wait()
            for cp in shard_arrivals(p):
                cp.wait_recv()
            x_own(p).start()
            for cp in first_sends(p):
                cp.start()

        @pl.when(away)
        def _():
            got(blk(W, p, z, y), rB.at[p, bid(z, y)], sB.at[p, 4])
            if p in MODE_FIRST:
                for cp in first_sends(p):
                    cp.start()

    def ag2(p):
        for dz in (1, 2, 3):
            got(blk(W, p, zof(dz), y), rB.at[p, bid(zof(dz), y)], sB.at[p, 0])
            if p in MODE_FIRST:
                y_fwd(p, dz).start()
            else:
                @pl.when(native)
                def _():
                    y_fwd(p, dz).start()
                    x_fwd(p, dz).start()

    def ag3(p):
        for dz in range(4):
            got(blk(W, p, zof(dz), 1 - y), rB.at[p, bid(zof(dz), 1 - y)], sB.at[p, 0])
            if p not in MODE_FIRST:
                @pl.when(native)
                def _():
                    x_fwd_y(p, dz).start()

    def ag_sent(p):
        if p in MODE_FIRST:
            for cp in first_sends(p):
                cp.wait_send()
            for dz in (1, 2, 3):
                y_fwd(p, dz).wait_send()

            @pl.when(native)
            def _():
                x_own(p).wait_send()
        else:
            @pl.when(native)
            def _():
                for cp in first_sends(p):
                    cp.wait_send()
                for dz in (1, 2, 3):
                    y_fwd(p, dz).wait_send()
                    x_fwd(p, dz).wait_send()
                x_own(p).wait_send()
                for dz in range(4):
                    x_fwd_y(p, dz).wait_send()

        @pl.when(away)
        def _():
            for cp in shard_remote(p):
                cp.wait_send()

    queue = []
    LOOK = 4
    for p in range(min(LOOK, NPARTS)):
        queue.append(("ag1", p))
    for i in range(NPARTS + 1):
        if i < NPARTS:
            queue.append(("ag2", i))
        if i + LOOK < NPARTS:
            queue.append(("ag1", i + LOOK))
        if i >= 1:
            queue.append(("ag3", i - 1))
    kinds = {"ag1": ag1, "ag2": ag2, "ag3": ag3}

    def step():
        if queue:
            name, p = queue.pop(0)
            kinds[name](p)

    def until(name, p):
        while (name, p) in queue:
            step()

    lane = lax.broadcasted_iota(jnp.int32, (1, 128), 1)
    low_half = lax.rem(lane, HEAD_DIM) < HEAD_DIM // 2
    head0 = lane < HEAD_DIM

    def swap(v):
        return jnp.where(low_half, pltpu.roll(v, 128 - HEAD_DIM // 2, 1), pltpu.roll(v, HEAD_DIM // 2, 1))

    def rot(v, r, n):
        return v * cos_ref[pl.ds(r, n), :] + swap(v) * sin_ref[pl.ds(r, n), :]

    def unrot(v, r, n):
        return v * cos_ref[pl.ds(r, n), :] - swap(v) * sin_ref[pl.ds(r, n), :]

    def wcols(p, a=0, n=None):
        c0, m = cols[p]
        return pl.ds(c0 + a, m if n is None else n)

    def loop(n, body):
        def go(i, carry):
            body(i)
            return carry
        lax.fori_loop(0, n, go, 0)

    TR = 256

    def transpose_into(src, dst):
        def body(i):
            r = pl.multiple_of(i * TR, TR)
            dst[:, pl.ds(r, TR)] = src[pl.ds(r, TR), :].T
        loop(LEN // TR, body)

    def core_send(src, dst, k):
        return rc(src, dst, sM.at[k], rM.at[k], dev_c)

    step()

    @pl.when(native)
    def _():
        tok_home.wait()
        seg_home.wait()

    @pl.when(away)
    def _():
        rc(tok_ref, X.at[own_rows], sM.at[4], rM.at[4], dev_d).wait_recv()
        tok_pass.start()
        rc(seg_ref, SEGR, sM.at[1], rM.at[1], dev_c).wait_recv()

    rc(X.at[oth_rows], X.at[oth_rows], sM.at[3], rM.at[3], dev_c).wait_recv()

    def seg_cols(i):
        r = pl.multiple_of(i * 128, 128)
        SEGC[pl.ds(r, 128), :] = jnp.broadcast_to(SEGR[0:1, pl.ds(r, 128)], (128, 128)).T
    loop(LEN // 128, seg_cols)

    def project(p, dst, turn):
        def body(i):
            r = pl.multiple_of(i * TR, TR)
            v = nn(X[pl.ds(r, TR), :], W[:, wcols(p)])
            for k in range(PAIRS):
                part = v[:, 128 * k : 128 * (k + 1)]
                if turn:
                    part = rot(part, r, TR)
                dst[pl.ds(r, TR), 128 * k : 128 * (k + 1)] = part.astype(BF)
        loop(LEN // TR, body)

    transpose_into(X, XT)
    until("ag3", PQ)
    project(PQ, Q, True)
    until("ag3", PK)
    project(PK, K, True)
    until("ag3", PV)
    project(PV, V, False)

    scale = HEAD_DIM ** -0.5
    LSE[...] = jnp.zeros(LSE.shape, F32)

    def attend_pair(k):
        def body(i):
            r = pl.multiple_of(i * TR, TR)
            rows = pl.ds(r, TR)
            pair = slice(128 * k, 128 * (k + 1))
            q = Q[rows, pair]
            keys = K[:, pair]
            vals = V[:, pair]
            same = SEGC[rows, 0:1] == SEGR[0:1, :]
            outs, lses = [], []
            for s in range(2):
                mine = head0 if s == 0 else jnp.logical_not(head0)
                qm = jnp.where(mine, q.astype(F32) * scale, 0.0).astype(BF)
                sc = jnp.where(same, nt(qm, keys), NEG)
                top = jnp.max(sc, axis=1, keepdims=True)
                e = jnp.exp(sc - top)
                total = jnp.sum(e, axis=1, keepdims=True)
                outs.append(nn(e.astype(BF), vals) / total)
                lses.append(top + jnp.log(total))
            A[rows, pair] = jnp.where(head0, outs[0], outs[1]).astype(BF)
            LSE[rows, :] = jnp.where(lane == 2 * k, lses[0], jnp.where(lane == 2 * k + 1, lses[1], LSE[rows, :]))
        loop(LEN // TR, body)

    attend_pair(0)
    until("ag3", PO)
    attend_pair(1)
    until("ag2", PG0)
    attend_pair(2)
    until("ag2", PG1)

    norm_cols = pl.ds(cols[PO][0] + HC, 128)
    NV[...] = W[:, norm_cols].astype(F32).T[0:8, :]

    tok_pass_done = rc(X.at[own_rows], X.at[own_rows], sM.at[3], rM.at[3], dev_c)

    @pl.when(native)
    def _():
        tok_core.wait_send()

    @pl.when(away)
    def _():
        tok_pass_done.wait_send()

    def partial(lhs, weights, dst_rows_at, finish):
        def body(i):
            r = pl.multiple_of(i * TR, TR)
            acc = None
            for ref, a, n, w0 in lhs:
                term = nt(ref[pl.ds(dst_rows_at + r, TR), pl.ds(a, n)], weights[:, pl.ds(w0, n)])
                acc = term if acc is None else acc + term
            finish(r, acc)
        loop(HALF // TR, body)

    def to_x(r, acc):
        X[pl.ds(oth_r + r, TR), :] = acc.astype(BF)

    def to_n2(r, acc):
        N2[pl.ds(r, TR), :] = acc

    out_terms = [(A, 0, HC, cols[PO][0])]
    partial(out_terms, W, oth_r, to_x)
    part0 = core_send(X.at[oth_rows], R, 6)
    part0.start()
    partial(out_terms, W, own_r, to_n2)
    part0.wait_recv()

    TN = 64
    inv_d = 1.0 / D

    def norm1(i):
        r = pl.multiple_of(i * TN, TN)
        rows = pl.ds(r, TN)
        mix = X[pl.ds(own_r + r, TN), :].astype(F32) + N2[rows, :] + R[rows, :].astype(F32)
        mean = jnp.sum(mix, axis=1, keepdims=True) * inv_d
        cen = mix - mean
        var = jnp.sum(cen * cen, axis=1, keepdims=True) * inv_d
        rs = lax.rsqrt(var + epsilon)
        n = cen * rs
        N1[rows, :] = n
        RS1[rows, :] = jnp.broadcast_to(rs, (TN, 128))
        M[pl.ds(own_r + r, TN), :] = (n * NV[0:1, :] + NV[2:3, :]).astype(BF)
    loop(HALF // TN, norm1)
    mid = core_send(M.at[own_rows], M.at[own_rows], 7)
    mid.start()
    until("ag3", PG0)
    rc(M.at[oth_rows], M.at[oth_rows], sM.at[7], rM.at[7], dev_c).wait_recv()

    def sigmoid(v):
        return 1.0 / (1.0 + jnp.exp(-v))

    def hidden_chunk(j):
        def body(i):
            r = pl.multiple_of(i * TR, TR)
            rows = pl.ds(r, TR)
            both = nn(M[rows, :], W[:, wcols(PG0 + j)])
            gate, up = both[:, :CH], both[:, CH:]
            GT[rows, pl.ds(j * CH, CH)] = gate.astype(BF)
            UP[rows, pl.ds(j * CH, CH)] = up.astype(BF)
            H[rows, pl.ds(j * CH, CH)] = (gate * sigmoid(gate) * up).astype(BF)
        loop(LEN // TR, body)

    hidden_chunk(0)
    until("ag2", PG2)
    transpose_into(M, MT)
    until("ag3", PG1)
    hidden_chunk(1)
    until("ag3", PG2)
    hidden_chunk(2)
    until("ag3", PD2)
    part0.wait_send()
    mid.wait_send()

    down_terms = [(H, j * CH, CH, cols[PD0 + j][0]) for j in range(3)]
    partial(down_terms, W, oth_r, to_x)
    part1 = core_send(X.at[oth_rows], R, 8)
    part1.start()
    partial(down_terms, W, own_r, to_n2)

    @pl.when(native)
    def _():
        cot_home.wait()

    @pl.when(away)
    def _():
        rc(cot_ref, C, sM.at[5], rM.at[5], dev_d).wait_recv()

    part1.wait_recv()

    def norm2(i, carry):
        dg, db = carry
        r = pl.multiple_of(i * TN, TN)
        rows = pl.ds(r, TN)
        first = N1[rows, :] * NV[0:1, :] + NV[2:3, :]
        v = first + N2[rows, :] + R[rows, :].astype(F32)
        mean = jnp.sum(v, axis=1, keepdims=True) * inv_d
        cen = v - mean
        var = jnp.sum(cen * cen, axis=1, keepdims=True) * inv_d
        rs = lax.rsqrt(var + epsilon)
        n = cen * rs
        e = C[rows, :].astype(F32)
        C[rows, :] = (n * NV[1:2, :] + NV[3:4, :]).astype(BF)
        eg = e * NV[1:2, :]
        m1 = jnp.sum(eg, axis=1, keepdims=True) * inv_d
        m2 = jnp.sum(eg * n, axis=1, keepdims=True) * inv_d
        d = rs * (eg - m1 - n * m2)
        N2[rows, :] = d
        M[pl.ds(own_r + r, TN), :] = d.astype(BF)
        return dg + jnp.sum(e * n, axis=0, keepdims=True), db + jnp.sum(e, axis=0, keepdims=True)

    zero_row = jnp.zeros((1, D), F32)
    dg1, db1 = lax.fori_loop(0, HALF // TN, norm2, (zero_row, zero_row))
    NG[...] = jnp.zeros(NG.shape, F32)
    NG[1:2, :] = dg1
    NG[3:4, :] = db1
    d2 = core_send(M.at[own_rows], M.at[own_rows], 9)
    d2.start()

    act_home = pltpu.make_async_copy(C, act_out, sM.at[10])
    act_away = rc(C, act_out, sM.at[10], rM.at[10], dev_d)

    @pl.when(native)
    def _():
        act_home.start()

    @pl.when(away)
    def _():
        act_away.start()

    for p in range(NPARTS):
        ag_sent(p)

    rc(M.at[oth_rows], M.at[oth_rows], sM.at[9], rM.at[9], dev_c).wait_recv()

    XF = (PD0, PD2, PG0, PG2, PO, PK)
    land = {p: cols[p][0] for p in XF}
    land[PK] = cols[PD1][0]

    def wland(p, zz, yy):
        return W.at[rows_of(zz, yy), pl.ds(land[p], cols[p][1])]

    def credit(p):
        @pl.when(native)
        def _():
            pl.semaphore_signal(cred.at[p], inc=1, device_id=dev_x, device_id_type=MESH_ID)

    def cslice(p):
        return pl.ds(cols[p][0], cols[p][1])

    def x_block(p, dz, dy):
        yy = 1 - y if dy == 0 else y
        return rc(blk(G, p, zof(dz), yy), wland(p, zof(dz), yy), sX.at[p, 2 * dz + dy], rX.at[p, 2 * dz + dy], dev_x)

    def y_block(p, dz):
        return rc(blk(G, p, zof(dz), 1 - y), Ly.at[zof(dz), :, cslice(p)], sY.at[p, dz], rY.at[p, dz], dev_y)

    def y_arrival(p, dz):
        return rc(blk(G, p, zof(dz), y), Ly.at[zof(dz), :, cslice(p)], sY.at[p, dz], rY.at[p, dz], dev_y)

    def z_block(p, dz):
        return rc(blk(G, p, zof(dz), y), Lz.at[dz - 1, :, cslice(p)], sZ.at[p, dz - 1], rZ.at[p, dz - 1], dev_z(dz))

    def x_final(p):
        return rc(blk(G, p, z, y), Lx.at[:, cslice(p)], sX.at[p, 0], rX.at[p, 0], dev_x)

    def out_copies(p):
        lo = pl.multiple_of(c * SH, 16)
        c0, n = cols[p]
        if p in (PQ, PK, PV):
            pieces = [(c0, n, gq_out.at[p])]
        elif p == PO:
            pieces = [(c0, n, go_out)]
        elif p in (PG0, PG1, PG2):
            j = p - PG0
            pieces = [(c0 + i * CH, CH, ggu_out.at[i, :, pl.ds(j * CH, CH)]) for i in range(2)]
        else:
            pieces = [(c0, n, gd_out.at[:, pl.ds((p - PD0) * CH, CH)])]
        return [
            pltpu.make_async_copy(F.at[pl.ds(lo, SH), pl.ds(a, m)], dst, sO.at[p, i])
            for i, (a, m, dst) in enumerate(pieces)
        ]

    def f_send(p):
        part = F.at[pl.ds(pl.multiple_of(oc * SH, 16), SH), cslice(p)]
        return rc(part, part, sF.at[p], rF.at[p], dev_c)

    def f_arrival(p):
        part = F.at[pl.ds(pl.multiple_of(c * SH, 16), SH), cslice(p)]
        return rc(part, part, sF.at[p], rF.at[p], dev_c)

    def add_blocks(p, zz, yy, extra):
        rows = rows_of(zz, yy)
        total = G[rows, cslice(p)].astype(F32)
        for term in extra:
            total = total + term.astype(F32)
        return rows, total

    def rs1(p):
        if p in XF:
            @pl.when(away)
            def _():
                pl.semaphore_wait(cred.at[p], 1)
                for dy in range(2):
                    for dz in range(4):
                        x_block(p, dz, dy).start()
        else:
            for dz in range(4):
                y_block(p, dz).start()

    def rs1n(p):
        if p in XF:
            @pl.when(native)
            def _():
                for dz in range(4):
                    x_block(p, dz, 0).wait_recv()
                    rows, total = add_blocks(p, zof(dz), 1 - y, [W[rows_of(zof(dz), 1 - y), pl.ds(land[p], cols[p][1])]])
                    G[rows, cslice(p)] = total.astype(BF)
                    y_block(p, dz).start()

    def rs2(p):
        def work():
            for dz in (1, 2, 3, 0):
                terms = []
                if p in XF:
                    x_block(p, dz, 1).wait_recv()
                    terms.append(W[rows_of(zof(dz), y), pl.ds(land[p], cols[p][1])])
                y_arrival(p, dz).wait_recv()
                terms.append(Ly[zof(dz), :, cslice(p)])
                rows, total = add_blocks(p, zof(dz), y, terms)
                G[rows, cslice(p)] = total.astype(BF)
                if dz:
                    z_block(p, dz).start()
        if p in XF:
            pl.when(native)(work)
        else:
            work()

    def rs3(p):
        def total():
            for dz in (1, 2, 3):
                z_block(p, dz).wait_recv()
            return add_blocks(p, z, y, [Lz[dz - 1, :, cslice(p)] for dz in (1, 2, 3)])[1]

        @pl.when(native)
        def _():
            F[:, cslice(p)] = total()
            if p in XF:
                f_send(p).start()
                for cp in out_copies(p):
                    cp.start()

        if p not in XF:
            @pl.when(away)
            def _():
                G[rows_of(z, y), cslice(p)] = total().astype(BF)
                x_final(p).start()

    def rs4(p):
        if p in XF:
            @pl.when(away)
            def _():
                f_arrival(p).wait_recv()
                for cp in out_copies(p):
                    cp.start()
        else:
            @pl.when(native)
            def _():
                x_final(p).wait_recv()
                F[:, cslice(p)] = F[:, cslice(p)] + Lx[:, cslice(p)].astype(F32)
                f_send(p).start()
                for cp in out_copies(p):
                    cp.start()

            @pl.when(away)
            def _():
                x_final(p).wait_send()
                f_arrival(p).wait_recv()
                for cp in out_copies(p):
                    cp.start()

    def rs_sent(p):
        if p in XF:
            @pl.when(away)
            def _():
                for dy in range(2):
                    for dz in range(4):
                        x_block(p, dz, dy).wait_send()

            @pl.when(native)
            def _():
                for dz in range(4):
                    y_block(p, dz).wait_send()
                for dz in (1, 2, 3):
                    z_block(p, dz).wait_send()
        else:
            for dz in range(4):
                y_block(p, dz).wait_send()
            for dz in (1, 2, 3):
                z_block(p, dz).wait_send()

        @pl.when(native)
        def _():
            f_send(p).wait_send()

        for cp in out_copies(p):
            cp.wait()

    kinds.update({"rs1n": rs1n, "rs2": rs2, "rs3": rs3, "rs4": rs4})
    order = [PD1, PG1, PD0, PD2, PG0, PG2, PO, PV, PQ, PK]
    for i in range(NPARTS + 3):
        for lag, name in enumerate(("rs1n", "rs2", "rs3", "rs4")):
            if 0 <= i - lag < NPARTS:
                queue.append((name, order[i - lag]))

    transpose_into(M, DT)

    def back_chunk(j):
        hc = pl.ds(j * CH, CH)

        def body(i):
            r = pl.multiple_of(i * TR, TR)
            rows = pl.ds(r, TR)
            dh = nn(M[rows, :], W[:, wcols(PD0 + j)]).astype(BF).astype(F32)
            gate = GT[rows, hc].astype(F32)
            up = UP[rows, hc].astype(F32)
            sg = sigmoid(gate)
            GT[rows, hc] = (dh * up * (sg * (1.0 + gate * (1.0 - sg)))).astype(BF)
            UP[rows, hc] = (dh * gate * sg).astype(BF)
        loop(LEN // TR, body)

    def weight_grad(left, right, rcols, c0):
        def body(i):
            r = pl.multiple_of(i * TR, TR)
            G[pl.ds(r, TR), c0] = nn(left[pl.ds(r, TR), :], right[:, rcols]).astype(BF)
        loop(D // TR, body)

    def grads_chunk(j):
        hc = pl.ds(j * CH, CH)
        weight_grad(DT, H, hc, wcols(PD0 + j))

    def grads_gate_up(j):
        hc = pl.ds(j * CH, CH)
        weight_grad(MT, GT, hc, wcols(PG0 + j, 0, CH))
        weight_grad(MT, UP, hc, wcols(PG0 + j, CH, CH))

    back_chunk(1)
    grads_chunk(1)
    rs1(PD1)
    grads_gate_up(1)
    rs1(PG1)
    back_chunk(0)
    credit(PD0)
    grads_chunk(0)
    rs1(PD0)
    back_chunk(2)
    credit(PD2)
    grads_chunk(2)
    rs1(PD2)
    credit(PK)
    until("rs2", PD1)
    grads_gate_up(0)
    until("rs1n", PD0)
    grads_gate_up(2)
    until("rs2", PG1)

    mid_terms = []
    for j in range(3):
        mid_terms.append((GT, j * CH, CH, cols[PG0 + j][0]))
        mid_terms.append((UP, j * CH, CH, cols[PG0 + j][0] + CH))
    part1.wait_send()
    partial(mid_terms, W, oth_r, to_x)
    part2 = core_send(X.at[oth_rows], R, 11)
    part2.start()

    def to_n2_add(r, acc):
        N2[pl.ds(r, TR), :] = N2[pl.ds(r, TR), :] + acc
    partial(mid_terms, W, own_r, to_n2_add)
    credit(PG0)
    credit(PG2)
    rs1(PG0)
    rs1(PG2)
    d2.wait_send()
    part2.wait_recv()

    def norm1_back(i, carry):
        dg, db = carry
        r = pl.multiple_of(i * TN, TN)
        rows = pl.ds(r, TN)
        e = N2[rows, :] + R[rows, :].astype(F32)
        n = N1[rows, :]
        rs = RS1[rows, 0:1]
        eg = e * NV[0:1, :]
        m1 = jnp.sum(eg, axis=1, keepdims=True) * inv_d
        m2 = jnp.sum(eg * n, axis=1, keepdims=True) * inv_d
        d = rs * (eg - m1 - n * m2)
        N2[rows, :] = d
        M[pl.ds(own_r + r, TN), :] = d.astype(BF)
        return dg + jnp.sum(e * n, axis=0, keepdims=True), db + jnp.sum(e, axis=0, keepdims=True)

    dg0, db0 = lax.fori_loop(0, HALF // TN, norm1_back, (zero_row, zero_row))
    d1 = core_send(M.at[own_rows], M.at[own_rows], 12)
    d1.start()
    NG[0:1, :] = dg0
    NG[2:3, :] = db0
    ng = core_send(NG, NGR, 13)
    ng.start()
    until("rs2", PD0)
    rc(M.at[oth_rows], M.at[oth_rows], sM.at[12], rM.at[12], dev_c).wait_recv()
    transpose_into(M, DT)
    ng.wait_recv()
    NGT[...] = jnp.zeros(NGT.shape, F32)
    NGT[0:8, :] = NG[...] + NGR[...]
    G[:, norm_cols] = NGT[...].T.astype(BF)

    def d_att(i):
        r = pl.multiple_of(i * TR, TR)
        rows = pl.ds(r, TR)
        da = nn(M[rows, :], W[:, wcols(PO, 0, HC)]).astype(BF)
        UP[rows, pl.ds(0, HC)] = da
        prod = da.astype(F32) * A[rows, :].astype(F32)
        acc = jnp.zeros((TR, 128), F32)
        for k in range(PAIRS):
            piece = prod[:, 128 * k : 128 * (k + 1)]
            d0 = jnp.sum(jnp.where(head0, piece, 0.0), axis=1, keepdims=True)
            dall = jnp.sum(piece, axis=1, keepdims=True)
            acc = jnp.where(lane == 2 * k, d0, jnp.where(lane == 2 * k + 1, dall - d0, acc))
        DEL[rows, :] = acc
    loop(LEN // TR, d_att)
    credit(PO)
    weight_grad(DT, A, pl.ds(0, HC), wcols(PO, 0, HC))
    rs1(PO)
    LST[...] = LSE[...].T[0:8, :]
    DLT[...] = DEL[...].T[0:8, :]

    def attend_back(k):
        pair = slice(128 * k, 128 * (k + 1))
        DQT[...] = jnp.zeros(DQT.shape, F32)

        def body(i):
            r = pl.multiple_of(i * TR, TR)
            rows = pl.ds(r, TR)
            keys = K[rows, pair].astype(F32) * scale
            vals = V[rows, pair]
            qp = Q[:, pair]
            da = UP[:, pair]
            same = SEGC[rows, 0:1] == SEGR[0:1, :]
            dv, dk, kts, dss = [], [], [], []
            for s in range(2):
                h = 2 * k + s
                mine = head0 if s == 0 else jnp.logical_not(head0)
                km = jnp.where(mine, keys, 0.0)
                vm = jnp.where(mine, vals.astype(F32), 0.0).astype(BF)
                sc = nt(km.astype(BF), qp)
                pr = jnp.where(same, jnp.exp(sc - LST[h : h + 1, :]), 0.0)
                dp = nt(vm, da)
                ds = (pr * (dp - DLT[h : h + 1, :])).astype(BF)
                dv.append(nn(pr.astype(BF), da))
                dk.append(nn(ds, qp))
                DQT[...] = DQT[...] + nn(km.T.astype(BF), ds)
            GT[rows, 2 * HC + 128 * k : 2 * HC + 128 * (k + 1)] = jnp.where(head0, dv[0], dv[1]).astype(BF)
            GT[rows, HC + 128 * k : HC + 128 * (k + 1)] = unrot(jnp.where(head0, dk[0], dk[1]) * scale, r, TR).astype(BF)
        loop(LEN // TR, body)

        def finish(i):
            r = pl.multiple_of(i * 128, 128)
            GT[pl.ds(r, 128), pair] = unrot(DQT[:, pl.ds(r, 128)].T, r, 128).astype(BF)
        loop(LEN // 128, finish)

    attend_back(0)
    until("rs2", PD2)
    attend_back(1)
    until("rs2", PG0)
    attend_back(2)
    until("rs1n", PO)

    weight_grad(XT, GT, pl.ds(2 * HC, HC), wcols(PV))
    rs1(PV)
    weight_grad(XT, GT, pl.ds(0, HC), wcols(PQ))
    rs1(PQ)
    weight_grad(XT, GT, pl.ds(HC, HC), wcols(PK))
    rs1(PK)

    in_terms = [(GT, 0, 3 * HC, 0)]
    part2.wait_send()
    partial(in_terms, W, oth_r, to_x)
    part3 = core_send(X.at[oth_rows], R, 14)
    part3.start()
    partial(in_terms, W, own_r, to_n2_add)

    @pl.when(native)
    def _():
        act_home.wait()

    @pl.when(away)
    def _():
        act_away.wait_send()

    part3.wait_recv()

    gtok_home = pltpu.make_async_copy(N2, gtok_out, sM.at[15])
    gtok_away = rc(C, GL, sM.at[15], rM.at[15], dev_d)

    def add_rows(i):
        r = pl.multiple_of(i * TN, TN)
        rows = pl.ds(r, TN)
        total = N2[rows, :] + R[rows, :].astype(F32)
        N2[rows, :] = total
        C[rows, :] = total.astype(BF)
    loop(HALF // TN, add_rows)

    @pl.when(native)
    def _():
        gtok_home.start()

    @pl.when(away)
    def _():
        gtok_away.start()

    while queue:
        step()

    @pl.when(away)
    def _():
        rc(C, GL, sM.at[15], rM.at[15], dev_d).wait_recv()
        N1[...] = GL[...].astype(F32)
        out = pltpu.make_async_copy(N1, gtok_out, sM.at[16])
        out.start()
        out.wait()
        gtok_away.wait_send()
        rc(C, act_out, sM.at[10], rM.at[10], dev_d).wait_recv()
        tok_away.wait_send()
        cot_away.wait_send()

    @pl.when(native)
    def _():
        gtok_home.wait()
        seg_send.wait_send()

    d1.wait_send()
    ng.wait_send()
    part3.wait_send()
    for p in range(NPARTS):
        rs_sent(p)


def on_device_fused(
    tokens, segments, qkv_weight, out_weight, gate_up_weight, down_weight, norm_gain, norm_shift, cotangent
):
    length, width = segments.shape[1], tokens.shape[1]
    half = tokens.shape[0]
    hc, fc = qkv_weight.shape[3], gate_up_weight.shape[3]
    sh = qkv_weight.shape[2]
    nc = 4 * hc + 128 + 3 * fc
    cosine, sine = rope_numpy(length)
    norms = jnp.concatenate([norm_gain[0], norm_shift[0]], axis=0).T
    o_own = jnp.concatenate([out_weight[0].T, norms, jnp.zeros((sh, 128 - norms.shape[1]), BF)], axis=1)
    d_own = down_weight[0].T
    seg8 = jnp.broadcast_to(segments.astype(F32), (8, length))
    vm = pl.BlockSpec(memory_space=pltpu.VMEM)
    anyspec = pl.BlockSpec(memory_space=pl.ANY)
    V_ = pltpu.VMEM
    br = 2 * sh
    dma = pltpu.SemaphoreType.DMA
    scratch = [
        V_((width, nc), BF),
        V_((width, nc), BF),
        V_((NZ, br, nc), BF),
        V_((NZ - 1, br, nc), BF),
        V_((br, nc), BF),
        V_((br, nc), F32),
        V_((length, width), BF),
        V_((width, length), BF),
        V_((length, hc), BF),
        V_((length, hc), BF),
        V_((length, hc), BF),
        V_((length, hc), BF),
        V_((length, width), BF),
        V_((width, length), BF),
        V_((width, length), BF),
        V_((length, fc), BF),
        V_((length, fc), BF),
        V_((length, fc), BF),
        V_((half, width), BF),
        V_((half, width), BF),
        V_((half, width), F32),
        V_((half, width), F32),
        V_((half, 128), F32),
        V_((8, 128), F32),
        V_((128, length), F32),
        V_((length, 128), F32),
        V_((8, length), F32),
        V_((length, 128), F32),
        V_((8, length), F32),
        V_((8, length), F32),
        V_((length, 128), F32),
        V_((8, width), F32),
        V_((8, width), F32),
        V_((8, width), F32),
        V_((128, width), F32),
        V_((half, width), BF),
        dma((NPARTS, 2)), dma((NPARTS, 2)), dma((NPARTS, 2)),
        dma((NPARTS, 15)), dma((NPARTS, 8)),
        dma((NPARTS, 4)), dma((NPARTS, 4)),
        dma((NPARTS, 3)), dma((NPARTS, 3)),
        dma((NPARTS, 8)), dma((NPARTS, 8)),
        dma((NPARTS,)), dma((NPARTS,)), dma((NPARTS, 2)),
        dma((17,)), dma((17,)),
        pltpu.SemaphoreType.REGULAR((NPARTS,)),
    ]
    act, gtok, gq, go, ggu, gd = pl.pallas_call(
        functools.partial(layer_kernel, (length, width, hc, fc)),
        out_shape=(
            jax.ShapeDtypeStruct((half, width), BF),
            jax.ShapeDtypeStruct((half, width), F32),
            jax.ShapeDtypeStruct((3, sh, hc), F32),
            jax.ShapeDtypeStruct((sh, hc + 128), F32),
            jax.ShapeDtypeStruct((2, sh, fc), F32),
            jax.ShapeDtypeStruct((sh, fc), F32),
        ),
        in_specs=[anyspec, anyspec, vm, vm, vm, anyspec, anyspec, anyspec, anyspec],
        out_specs=tuple([anyspec] * 6),
        scratch_shapes=scratch,
        compiler_params=pltpu.CompilerParams(
            collective_id=1, has_side_effects=True, vmem_limit_bytes=VMEM_LIMIT
        ),
        name="layer",
    )(tokens, cotangent, seg8, jnp.asarray(cosine), jnp.asarray(sine), qkv_weight[0], o_own, gate_up_weight[0], d_own)
    ngrad = go[:, hc : hc + 4].T
    return (
        act,
        gtok,
        gq[None],
        go[:, :hc].T[None],
        ggu[None],
        gd.T[None],
        ngrad[0:2][None],
        ngrad[2:4][None],
    )


VMEM_LIMIT = 64 * 1024 * 1024


def solution(mesh):
    body = on_device_fused if dict(mesh.shape) == {"fsdp": 16, "tp": 2} else on_device
    placed = (
        P(("fsdp", "tp"), None),
        P("fsdp", None),
        P(None, None, "fsdp", "tp"),
        P(None, "tp", "fsdp"),
        P(None, None, "fsdp", "tp"),
        P(None, "tp", "fsdp"),
        P(None, None, "fsdp"),
        P(None, None, "fsdp"),
        P(("fsdp", "tp"), None),
    )
    return jax.shard_map(
        body,
        mesh=mesh,
        in_specs=placed,
        out_specs=(
            P(("fsdp", "tp"), None),
            P(("fsdp", "tp"), None),
            P(None, None, "fsdp", "tp"),
            P(None, "tp", "fsdp"),
            P(None, None, "fsdp", "tp"),
            P(None, "tp", "fsdp"),
            P(None, None, "fsdp"),
            P(None, None, "fsdp"),
        ),
        check_vma=False,
    )
```

```python
import functools

import jax
import jax.numpy as jnp
import numpy as np
from jax import lax
from jax.experimental import pallas as pl
from jax.experimental.pallas import tpu as pltpu
from jax.sharding import PartitionSpec as P

HEAD_DIM = 64


epsilon = 1e-05


def for_sending(value):

    def short(part):
        return part.astype(jnp.bfloat16) if part.dtype == jnp.float32 else part

    return jax.tree.map(short, value)


def rope_tables(length):
    half_dim = HEAD_DIM // 2
    inv_freq = 1000.0 ** (-jnp.arange(half_dim, dtype=jnp.float32) * 2.0 / HEAD_DIM)
    angles = jnp.arange(length, dtype=jnp.float32)[:, None] * inv_freq[None, :]
    cosine = jnp.concatenate([jnp.cos(angles), jnp.cos(angles)], axis=-1)[:, None, :]
    sine_table = jnp.concatenate([jnp.sin(angles), jnp.sin(angles)], axis=-1)[:, None, :]
    return (cosine, sine_table)


def rotate(values_in, cosine, sine_table):
    half_dim = values_in.shape[-1] // 2
    turned = jnp.concatenate([-values_in[..., half_dim:], values_in[..., :half_dim]], axis=-1)
    return values_in * cosine + turned * sine_table


def unrotate(grads_in, cosine, sine_table):
    half_dim = grads_in.shape[-1] // 2
    moved_part = grads_in * sine_table
    return grads_in * cosine + jnp.concatenate(
        [moved_part[..., half_dim:], -moved_part[..., :half_dim]], axis=-1
    )


def norm_rows(stream, scale_vec, shift_vec):
    row_mean = jnp.mean(stream, axis=-1, keepdims=True)
    centred = stream - row_mean
    row_var = jnp.mean(centred * centred, axis=-1, keepdims=True)
    return centred * lax.rsqrt(row_var + epsilon) * scale_vec + shift_vec


def swiglu(gate_pre, up_proj):
    return jax.nn.silu(gate_pre) * up_proj


def spread(stream_low):
    return lax.all_gather(stream_low, "tp", axis=0, tiled=True)


def collect(partial_rows):
    return lax.psum_scatter(
        partial_rows.astype(jnp.bfloat16), "tp", scatter_dimension=0, tiled=True
    ).astype(jnp.float32)


def spread_grads(grads_low):
    return lax.all_gather(grads_low, "tp", axis=0, tiled=True)


def collect_grads(partial_rows):
    return lax.psum_scatter(
        partial_rows.astype(jnp.bfloat16), "tp", scatter_dimension=0, tiled=True
    ).astype(jnp.float32)


def layer_shards(arrays, layer_index):
    return tuple((weight_part[layer_index] for weight_part in arrays))


def block_scores(query_blk, keys_seq, seg_blk, seg_seq):
    scores = jnp.einsum(
        "qhd,khd->hqk", query_blk, keys_seq, preferred_element_type=jnp.float32
    ) * HEAD_DIM ** (-0.5)
    joined = seg_blk[:, None] == seg_seq[None, :]
    return jnp.where(joined[None], scores, -1e30)


def attend_forward(queries, keys_rot, values, segments):
    seq_count, length = segments.shape
    block_rows = min(512, length)
    block_count = length // block_rows

    def attend_one_block(flat_index):
        sequence = flat_index // block_count
        row_start = flat_index % block_count * block_rows
        query_seq = lax.dynamic_index_in_dim(queries, sequence, 0, False)
        keys_seq = lax.dynamic_index_in_dim(keys_rot, sequence, 0, False)
        values_seq = lax.dynamic_index_in_dim(values, sequence, 0, False)
        seg_seq = lax.dynamic_index_in_dim(segments, sequence, 0, False)
        query_blk = lax.dynamic_slice_in_dim(query_seq, row_start, block_rows, 0)
        seg_blk = lax.dynamic_slice_in_dim(seg_seq, row_start, block_rows, 0)
        scores = block_scores(query_blk, keys_seq, seg_blk, seg_seq)
        row_max = jnp.max(scores, axis=-1, keepdims=True)
        exp_terms = jnp.exp(scores - row_max)
        row_total = jnp.sum(exp_terms, axis=-1, keepdims=True)
        probs_low = (exp_terms / row_total).astype(jnp.bfloat16)
        attended = jnp.einsum(
            "hqk,khd->qhd", probs_low, values_seq, preferred_element_type=jnp.float32
        )
        return (attended, row_max + jnp.log(row_total))

    attended, log_total = lax.map(
        attend_one_block, jnp.arange(seq_count * block_count, dtype=jnp.int32)
    )
    return (attended.reshape(seq_count * length, -1), log_total)


def attend_backward(queries, keys_rot, values, d_attended, log_total, segments):
    seq_count, length = segments.shape
    block_rows = min(512, length)
    block_count = length // block_rows
    scale_value = HEAD_DIM ** (-0.5)

    def one_sequence(sequence):
        query_seq = lax.dynamic_index_in_dim(queries, sequence, 0, False)
        keys_seq = lax.dynamic_index_in_dim(keys_rot, sequence, 0, False)
        values_seq = lax.dynamic_index_in_dim(values, sequence, 0, False)
        d_out_seq = lax.dynamic_index_in_dim(d_attended, sequence, 0, False)
        seg_seq = lax.dynamic_index_in_dim(segments, sequence, 0, False)

        def one_one_block(running, block_index):
            row_start = block_index * block_rows
            query_blk = lax.dynamic_slice_in_dim(query_seq, row_start, block_rows, 0)
            d_out_blk = lax.dynamic_slice_in_dim(d_out_seq, row_start, block_rows, 0)
            seg_blk = lax.dynamic_slice_in_dim(seg_seq, row_start, block_rows, 0)
            block_total = lax.dynamic_index_in_dim(
                log_total, sequence * block_count + block_index, 0, False
            )
            scores = block_scores(query_blk, keys_seq, seg_blk, seg_seq)
            attn_probs = jnp.exp(scores - block_total)
            probs_low = attn_probs.astype(jnp.bfloat16)
            d_probs = jnp.einsum(
                "qhd,khd->hqk", d_out_blk, values_seq, preferred_element_type=jnp.float32
            )
            inner_sum = jnp.sum(attn_probs * d_probs, axis=-1, keepdims=True)
            d_scores = (attn_probs * (d_probs - inner_sum)).astype(jnp.bfloat16)
            d_query = (
                jnp.einsum("hqk,khd->qhd", d_scores, keys_seq, preferred_element_type=jnp.float32)
                * scale_value
            )
            d_key = (
                running[0]
                + jnp.einsum(
                    "hqk,qhd->khd", d_scores, query_blk, preferred_element_type=jnp.float32
                )
                * scale_value
            )
            d_value = running[1] + jnp.einsum(
                "hqk,qhd->khd", probs_low, d_out_blk, preferred_element_type=jnp.float32
            )
            return ((d_key, d_value), d_query)

        zero_keys = jnp.zeros(keys_seq.shape, jnp.float32)
        (d_keys, d_values), d_queries = lax.scan(
            one_one_block, (zero_keys, zero_keys), jnp.arange(block_count, dtype=jnp.int32)
        )
        return (d_queries.reshape(keys_seq.shape), d_keys, d_values)

    return lax.map(one_sequence, jnp.arange(seq_count, dtype=jnp.int32))


def layer_forward(stream, segments, weights, tables):
    qkv_w, out_w, gate_up_w, down_w, gain_rows, shift_rows = weights
    cosine, sine_table = tables
    seq_count, length = segments.shape
    head_count = qkv_w.shape[2] // HEAD_DIM
    shaped = (seq_count, length, head_count, HEAD_DIM)
    gain_vals = gain_rows.astype(jnp.float32)
    shift_vals = shift_rows.astype(jnp.float32)
    inputs = spread(stream.astype(jnp.bfloat16))
    query_pre = jnp.dot(inputs, qkv_w[0], preferred_element_type=jnp.float32).reshape(shaped)
    key_pre = jnp.dot(inputs, qkv_w[1], preferred_element_type=jnp.float32).reshape(shaped)
    queries = rotate(query_pre, cosine, sine_table).astype(jnp.bfloat16)
    keys_rot = rotate(key_pre, cosine, sine_table).astype(jnp.bfloat16)
    values = (
        jnp.dot(inputs, qkv_w[2], preferred_element_type=jnp.float32)
        .astype(jnp.bfloat16)
        .reshape(shaped)
    )
    attended, log_total = attend_forward(queries, keys_rot, values, segments)
    attended_low = attended.astype(jnp.bfloat16)
    branch = collect(jnp.dot(attended_low, out_w, preferred_element_type=jnp.float32))
    mixed = stream + branch
    first_norm = norm_rows(mixed, gain_vals[0], shift_vals[0])
    middle = spread(first_norm.astype(jnp.bfloat16))
    gate_pre = jnp.dot(middle, gate_up_w[0], preferred_element_type=jnp.float32)
    up_proj = jnp.dot(middle, gate_up_w[1], preferred_element_type=jnp.float32)
    hidden = swiglu(gate_pre, up_proj).astype(jnp.bfloat16)
    branch_two = collect(jnp.dot(hidden, down_w, preferred_element_type=jnp.float32))
    second_in = first_norm + branch_two
    saved_state = (
        inputs,
        queries,
        keys_rot,
        values,
        log_total,
        attended_low,
        mixed,
        middle,
        gate_pre,
        up_proj,
        hidden,
        second_in,
    )
    return (norm_rows(second_in, gain_vals[1], shift_vals[1]), saved_state)


def layer_backward(grad_out, saved_state, segments, weights, tables):
    qkv_w, out_w, gate_up_w, down_w, gain_rows, shift_rows = weights
    (
        inputs,
        queries,
        keys_rot,
        values,
        log_total,
        attended_low,
        mixed,
        middle,
        gate_pre,
        up_proj,
        hidden,
        second_in,
    ) = saved_state
    cosine, sine_table = tables
    gain_vals = gain_rows.astype(jnp.float32)
    shift_vals = shift_rows.astype(jnp.float32)
    unused_two, norm_two_back = jax.vjp(norm_rows, second_in, gain_vals[1], shift_vals[1])
    d_second, d_gain_two, d_shift_two = norm_two_back(grad_out)
    d_branch_two = spread_grads(d_second.astype(jnp.bfloat16))
    grad_down = jnp.einsum("rf,rd->fd", hidden, d_branch_two, preferred_element_type=jnp.float32)
    d_hidden_low = jnp.einsum(
        "rd,fd->rf", d_branch_two, down_w, preferred_element_type=jnp.float32
    ).astype(jnp.bfloat16)
    d_hidden = lax.optimization_barrier(d_hidden_low).astype(jnp.float32)
    unused_swish, swish_back = jax.vjp(swiglu, gate_pre, up_proj)
    d_gate, d_up = swish_back(d_hidden)
    d_gate_low = d_gate.astype(jnp.bfloat16)
    d_up_low = d_up.astype(jnp.bfloat16)
    grad_gate_up = jnp.stack(
        [
            jnp.einsum("rd,rf->df", middle, d_gate_low, preferred_element_type=jnp.float32),
            jnp.einsum("rd,rf->df", middle, d_up_low, preferred_element_type=jnp.float32),
        ]
    )
    d_middle = jnp.einsum("rf,df->rd", d_gate_low, gate_up_w[0], preferred_element_type=jnp.float32)
    d_middle = d_middle + jnp.einsum(
        "rf,df->rd", d_up_low, gate_up_w[1], preferred_element_type=jnp.float32
    )
    d_first = d_second + collect_grads(d_middle)
    unused_one, norm_one_back = jax.vjp(norm_rows, mixed, gain_vals[0], shift_vals[0])
    d_mixed, d_gain_one, d_shift_one = norm_one_back(d_first)
    d_branch = spread_grads(d_mixed.astype(jnp.bfloat16))
    grad_out_w = jnp.einsum("rc,rd->cd", attended_low, d_branch, preferred_element_type=jnp.float32)
    d_attended = (
        jnp.einsum("rd,cd->rc", d_branch, out_w, preferred_element_type=jnp.float32)
        .astype(jnp.bfloat16)
        .reshape(queries.shape)
    )
    d_queries, d_keys, d_values = attend_backward(
        queries, keys_rot, values, d_attended, log_total, segments
    )
    flat_shape = (-1, queries.shape[2] * queries.shape[3])
    d_query_low = unrotate(d_queries, cosine, sine_table).astype(jnp.bfloat16).reshape(flat_shape)
    d_key_low = unrotate(d_keys, cosine, sine_table).astype(jnp.bfloat16).reshape(flat_shape)
    d_value_low = d_values.astype(jnp.bfloat16).reshape(flat_shape)
    grad_parts = (d_query_low, d_key_low, d_value_low)
    grad_qkv = jnp.stack(
        [
            jnp.einsum("rd,rc->dc", inputs, grad_part, preferred_element_type=jnp.float32)
            for grad_part in grad_parts
        ]
    )
    d_inputs = jnp.einsum("rc,dc->rd", d_query_low, qkv_w[0], preferred_element_type=jnp.float32)
    d_inputs = d_inputs + jnp.einsum(
        "rc,dc->rd", d_key_low, qkv_w[1], preferred_element_type=jnp.float32
    )
    d_inputs = d_inputs + jnp.einsum(
        "rc,dc->rd", d_value_low, qkv_w[2], preferred_element_type=jnp.float32
    )
    d_stream = d_mixed + collect_grads(d_inputs)
    weight_grads = (
        grad_qkv,
        grad_out_w,
        grad_gate_up,
        grad_down,
        jnp.stack([d_gain_one, d_gain_two]),
        jnp.stack([d_shift_one, d_shift_two]),
    )
    return (d_stream, weight_grads)


def on_device(
    tokens,
    segments,
    qkv_weight,
    out_weight,
    gate_up_weight,
    down_weight,
    norm_gain,
    norm_shift,
    cotangent,
):
    arrays = (qkv_weight, out_weight, gate_up_weight, down_weight, norm_gain, norm_shift)
    layer_total = qkv_weight.shape[0]
    tables = rope_tables(segments.shape[1])
    stream = tokens.astype(jnp.float32)
    kept_weights = []
    layer_index = 0
    weights = lax.all_gather(
        for_sending(layer_shards(arrays, layer_index)), "fsdp", axis=1, tiled=True
    )
    stream, saved_state = layer_forward(stream, segments, weights, tables)
    kept_weights.append(weights)
    saved_states = [saved_state]
    activations = stream.astype(jnp.bfloat16)
    grad_stream = cotangent.astype(jnp.float32)
    grad_layers = [None] * layer_total
    for layer_index in reversed(range(layer_total)):
        weights = lax.all_gather(
            for_sending(layer_shards(arrays, layer_index)), "fsdp", axis=1, tiled=True
        )
        grad_stream, weight_grads = layer_backward(
            grad_stream, saved_states[layer_index], segments, weights, tables
        )
        grad_layers[layer_index] = (
            lax.psum_scatter(weight_grads[0], "fsdp", scatter_dimension=1, tiled=True),
            lax.psum_scatter(weight_grads[1], "fsdp", scatter_dimension=1, tiled=True),
            lax.psum_scatter(weight_grads[2], "fsdp", scatter_dimension=1, tiled=True),
            lax.psum_scatter(weight_grads[3], "fsdp", scatter_dimension=1, tiled=True),
            lax.psum_scatter(weight_grads[4], "fsdp", scatter_dimension=1, tiled=True),
            lax.psum_scatter(weight_grads[5], "fsdp", scatter_dimension=1, tiled=True),
        )
    stacked = [jnp.stack([grad_layers[0][member]]) for member in range(6)]
    gain_sum, shift_sum = lax.psum((stacked[4], stacked[5]), "tp")
    return (
        activations,
        grad_stream,
        stacked[0],
        stacked[1],
        stacked[2],
        stacked[3],
        gain_sum,
        shift_sum,
    )


MESH_ID = pl.DeviceIdType.MESH
BF = jnp.bfloat16
F32 = jnp.float32
NZ, NY = 4, 2
PQ, PK, PV, PO, PG = range(5)
NG_PARTS = 6
PD = PG + NG_PARTS
NPARTS = PD + 3
PAIRS = 3
NEG = -1e30


def nt(a, b):
    return lax.dot_general(a, b, (((1,), (1,)), ((), ())), preferred_element_type=F32)


def nn(a, b):
    return jnp.dot(a, b, preferred_element_type=F32)


def rope_numpy(length):
    half = HEAD_DIM // 2
    inv = 1000.0 ** (-np.arange(half, dtype=np.float64) * 2.0 / HEAD_DIM)
    angles = np.arange(length, dtype=np.float64)[:, None] * inv[None, :]
    cosine, sine = np.cos(angles), np.sin(angles)
    cos_rows = np.concatenate([cosine, cosine, cosine, cosine], axis=1)
    sin_rows = np.concatenate([-sine, sine, -sine, sine], axis=1)
    return cos_rows.astype(np.float32), sin_rows.astype(np.float32)


def layer_kernel(
    dims,
    tok_ref, cot_ref, seg_ref, cos_ref, sin_ref, qkv_in, o_in, gu_in, d_in,
    act_out, gtok_out, gq_out, go_out, ggu_out, gd_out,
    W, G, Ly, Lz, Lx, F, X, XT, Q, K, V, A, M, MT, DT, GT, UP, H, R, C, N1, N2, RS1,
    DQT, LSE, LST, DEL, DLT, SEGR, SEGC, NV, NG, NGR, NGT, GL, LD,
    sLC, sCR, rCR, sA, sB, rB, sY, rY, sZ, rZ, sX, rX, sXF, rXF, sF, rF, sO, sM, rM, cred,
):
    LEN, D, HC, FC = dims
    HALF = LEN // 2
    SH = D // 16
    BR = 2 * SH
    CH = FC // 3
    GH = FC // NG_PARTS
    OW = HC + 128
    cols = {}
    at = 0
    for p in range(NPARTS):
        n = HC if p in (PQ, PK, PV) else OW if p == PO else 2 * GH if p < PD else CH
        cols[p] = (at, n)
        at += n

    f = lax.axis_index("fsdp")
    t = lax.axis_index("tp")
    c = lax.rem(f, 2)
    y = lax.rem(f // 2, 2)
    z = f // 4
    oc = 1 - c
    native = c == t
    away = c != t
    dev_x = (f, 1 - t)
    dev_y = ((z * 2 + (1 - y)) * 2 + c, t)
    dev_c = ((z * 2 + y) * 2 + oc, t)
    dev_d = ((z * 2 + y) * 2 + oc, 1 - t)

    def zof(d):
        return lax.rem(z + d, NZ)

    def dev_z(d):
        return ((zof(d) * 2 + y) * 2 + c, t)

    def rows_of(zz, yy):
        return pl.ds(pl.multiple_of((zz * 2 + yy) * BR, 16), BR)

    def cslice(p):
        return pl.ds(cols[p][0], cols[p][1])

    def blk(ref, p, zz, yy):
        return ref.at[rows_of(zz, yy), cslice(p)]

    def bid(zz, yy):
        return zz * 2 + yy

    def crosses_first(p, zz, yy):
        return lax.rem(zz + yy + p, 2) == 0

    def both(*conds):
        out = conds[0]
        for cond in conds[1:]:
            out = jnp.logical_and(out, cond)
        return out

    def when(cond, fn):
        pl.when(cond)(fn)

    def rc(src, dst, ss, rs, dev):
        return pltpu.make_async_remote_copy(
            src_ref=src, dst_ref=dst, send_sem=ss, recv_sem=rs, device_id=dev, device_id_type=MESH_ID
        )

    def wait_bytes(p, blocks, sem):
        ref = Ly.at[0, :, pl.ds(0, blocks * cols[p][1])]
        pltpu.make_async_copy(ref, ref, sem).wait()

    own_r = pl.multiple_of(c * HALF, HALF)
    oth_r = pl.multiple_of(oc * HALF, HALF)
    own_rows = pl.ds(own_r, HALF)
    oth_rows = pl.ds(oth_r, HALF)

    bar = pltpu.get_barrier_semaphore()
    partners = [dev_x, dev_y, dev_c, dev_d, dev_z(1), dev_z(2), dev_z(3)]
    for dev in partners:
        pl.semaphore_signal(bar, inc=1, device_id=dev, device_id_type=MESH_ID)
    pl.semaphore_wait(bar, len(partners))

    def shard_pieces(p):
        c0, n = cols[p]
        if p in (PQ, PK, PV):
            return [(qkv_in.at[p], c0, n)]
        if p == PO:
            return [(o_in, c0, n)]
        if p < PD:
            j = p - PG
            return [(gu_in.at[i, :, pl.ds(j * GH, GH)], c0 + i * GH, GH) for i in range(2)]
        j = p - PD
        return [(d_in.at[:, pl.ds(j * CH, CH)], c0, CH)]

    shard_rows = pl.ds(pl.multiple_of((z * 2 + y) * BR + c * SH, 16), SH)
    oshard_rows = pl.ds(pl.multiple_of((z * 2 + y) * BR + oc * SH, 16), SH)

    def start_shards(p):
        @pl.when(native)
        def _():
            for src, c0, n in shard_pieces(p):
                pltpu.make_async_copy(src, W.at[shard_rows, pl.ds(c0, n)], sLC.at[p]).start()

        @pl.when(away)
        def _():
            for src, c0, n in shard_pieces(p):
                rc(src, W.at[shard_rows, pl.ds(c0, n)], sCR.at[p], rCR.at[p], dev_c).start()

    def own_whole(p):
        return W.at[shard_rows, cslice(p)]

    tok_home = pltpu.make_async_copy(tok_ref, X.at[own_rows], sM.at[2])
    tok_core = rc(tok_ref, X.at[own_rows], sM.at[3], rM.at[3], dev_c)
    tok_away = rc(tok_ref, X.at[oth_rows], sM.at[4], rM.at[4], dev_d)
    tok_pass = rc(X.at[own_rows], X.at[own_rows], sM.at[3], rM.at[3], dev_c)
    seg_home = pltpu.make_async_copy(seg_ref, SEGR, sM.at[0])
    seg_send = rc(seg_ref, SEGR, sM.at[1], rM.at[1], dev_c)
    cot_home = pltpu.make_async_copy(cot_ref, C, sM.at[5])
    cot_away = rc(cot_ref, C, sM.at[5], rM.at[5], dev_d)

    start_shards(PQ)
    start_shards(PK)

    @pl.when(native)
    def _():
        seg_home.start()
        seg_send.start()
        tok_home.start()
        tok_core.start()
        cot_home.start()

    @pl.when(away)
    def _():
        tok_away.start()

    for p in range(2, NPARTS):
        start_shards(p)

    def ag_copy(p, zz, yy, dev, sem):
        b = blk(W, p, zz, yy)
        return rc(b, b, sem.at[p], rB.at[p, bid(zz, yy)], dev)

    def got(p, zz, yy):
        b = blk(W, p, zz, yy)
        rc(b, b, sA.at[p], rB.at[p, bid(zz, yy)], dev_x).wait_recv()

    def ag1(p):
        def spread_own():
            for d in (2, 1, 3):
                ag_copy(p, z, y, dev_z(d), sA).start()
            ag_copy(p, z, y, dev_y, sA).start()

        @pl.when(native)
        def _():
            pltpu.make_async_copy(own_whole(p), own_whole(p), sLC.at[p]).wait()
            o = W.at[oshard_rows, cslice(p)]
            rc(o, o, sCR.at[p], rCR.at[p], dev_c).wait_recv()
            ag_copy(p, z, y, dev_x, sA).start()
            spread_own()

        @pl.when(both(away, crosses_first(p, z, y)))
        def _():
            got(p, z, y)
            spread_own()

    def ag2(p, d):
        zz = zof(d)
        first = crosses_first(p, zz, y)

        def work():
            got(p, zz, y)
            ag_copy(p, zz, y, dev_y, sB).start()

            @pl.when(jnp.logical_not(first))
            def _():
                ag_copy(p, zz, y, dev_x, sB).start()

        when(both(d > 0, jnp.logical_or(native, first)), work)

    def ag3(p, d):
        zz = zof(d)
        first = crosses_first(p, zz, 1 - y)

        @pl.when(jnp.logical_or(native, first))
        def _():
            got(p, zz, 1 - y)

            @pl.when(jnp.logical_not(first))
            def _():
                ag_copy(p, zz, 1 - y, dev_x, sB).start()

    def ag4(p, d):
        zz = zof(d)
        yy = lax.rem(zz + p + 1, 2)

        @pl.when(away)
        def _():
            got(p, zz, yy)

    def ag_sent(p):
        own_first = crosses_first(p, z, y)

        @pl.when(native)
        def _():
            wait_bytes(p, 5, sA.at[p])
            when(own_first, lambda: wait_bytes(p, 7, sB.at[p]))
            when(jnp.logical_not(own_first), lambda: wait_bytes(p, 6, sB.at[p]))

        @pl.when(away)
        def _():
            @pl.when(own_first)
            def _():
                wait_bytes(p, 4, sA.at[p])
                wait_bytes(p, 1, sB.at[p])
            when(jnp.logical_not(own_first), lambda: wait_bytes(p, 2, sB.at[p]))
            pltpu.make_async_copy(own_whole(p), own_whole(p), sCR.at[p]).wait()

    def loop(n, body, *events):
        for ev in events:
            assert ev in queue and n == 4
            queue.remove(ev)

        def go(i, carry):
            body(i)
            for name, p in events:
                kinds[name](p, i)
            return carry
        lax.fori_loop(0, n, go, 0)

    queue = []
    for i in range(-2, NPARTS + 2):
        for name, lag in (("ag1", -2), ("ag2", 0), ("ag3", 1), ("ag4", 2)):
            if 0 <= i - lag < NPARTS:
                queue.append((name, i - lag))
    kinds = {"ag1": ag1, "ag2": ag2, "ag3": ag3, "ag4": ag4}
    whole = ("ag1", "rs1", "rs3", "rs4")

    def step():
        name, p = queue.pop(0)
        if name in whole:
            kinds[name](p)
        else:
            def go(i, carry):
                kinds[name](p, i)
                return carry
            lax.fori_loop(0, 4, go, 0)

    def until(name, p):
        while (name, p) in queue:
            step()

    def ready(p):
        until("ag3", p)
        if ("ag4", p) in queue:
            queue.remove(("ag4", p))
            queue.insert(0, ("ag4", p))
            step()

    lane = lax.broadcasted_iota(jnp.int32, (1, 128), 1)
    low_half = lax.rem(lane, HEAD_DIM) < HEAD_DIM // 2
    head0 = lane < HEAD_DIM

    def swap(v):
        return jnp.where(low_half, pltpu.roll(v, 128 - HEAD_DIM // 2, 1), pltpu.roll(v, HEAD_DIM // 2, 1))

    def rot(v, r, n):
        return v * cos_ref[pl.ds(r, n), :] + swap(v) * sin_ref[pl.ds(r, n), :]

    def unrot(v, r, n):
        return v * cos_ref[pl.ds(r, n), :] - swap(v) * sin_ref[pl.ds(r, n), :]

    def wcols(p, a=0, n=None):
        c0, m = cols[p]
        return pl.ds(c0 + a, m if n is None else n)

    TR = 256

    def transpose_into(src, dst, *events):
        def body(i):
            r = pl.multiple_of(i * TR, TR)
            dst[:, pl.ds(r, TR)] = src[pl.ds(r, TR), :].T
        loop(LEN // TR, body, *events)

    def core_send(src, dst, k):
        return rc(src, dst, sM.at[k], rM.at[k], dev_c)

    until("ag1", PK)

    @pl.when(native)
    def _():
        tok_home.wait()
        seg_home.wait()

    @pl.when(away)
    def _():
        rc(seg_ref, SEGR, sM.at[1], rM.at[1], dev_c).wait_recv()
    until("ag2", PQ)

    @pl.when(away)
    def _():
        rc(tok_ref, X.at[own_rows], sM.at[4], rM.at[4], dev_d).wait_recv()
        tok_pass.start()
    until("ag3", PQ)
    rc(X.at[oth_rows], X.at[oth_rows], sM.at[3], rM.at[3], dev_c).wait_recv()

    def seg_cols(i):
        r = pl.multiple_of(i * 128, 128)
        SEGC[pl.ds(r, 128), :] = jnp.broadcast_to(SEGR[0:1, pl.ds(r, 128)], (128, 128)).T
    loop(LEN // 128, seg_cols)

    def project(p, dst, turn, *events):
        def body(i):
            r = pl.multiple_of(i * TR, TR)
            v = nn(X[pl.ds(r, TR), :], W[:, wcols(p)])
            for k in range(PAIRS):
                part = v[:, 128 * k : 128 * (k + 1)]
                if turn:
                    part = rot(part, r, TR)
                dst[pl.ds(r, TR), 128 * k : 128 * (k + 1)] = part.astype(BF)
        loop(LEN // TR, body, *events)

    transpose_into(X, XT)
    ready(PQ)
    project(PQ, Q, True)
    ready(PK)
    project(PK, K, True)
    when(away, lambda: cot_away.start())
    ready(PV)
    project(PV, V, False)

    scale = HEAD_DIM ** -0.5
    LSE[...] = jnp.zeros(LSE.shape, F32)

    def attend_pair(k, *events):
        def body(i):
            r = pl.multiple_of(i * TR, TR)
            rows = pl.ds(r, TR)
            pair = slice(128 * k, 128 * (k + 1))
            q = Q[rows, pair]
            keys = K[:, pair]
            vals = V[:, pair]
            same = SEGC[rows, 0:1] == SEGR[0:1, :]
            outs, lses = [], []
            for s in range(2):
                mine = head0 if s == 0 else jnp.logical_not(head0)
                qm = jnp.where(mine, q.astype(F32) * scale, 0.0).astype(BF)
                sc = jnp.where(same, nt(qm, keys), NEG)
                top = jnp.max(sc, axis=1, keepdims=True)
                e = jnp.exp(sc - top)
                total = jnp.sum(e, axis=1, keepdims=True)
                outs.append(nn(e.astype(BF), vals) / total)
                lses.append(top + jnp.log(total))
            A[rows, pair] = jnp.where(head0, outs[0], outs[1]).astype(BF)
            LSE[rows, :] = jnp.where(lane == 2 * k, lses[0], jnp.where(lane == 2 * k + 1, lses[1], LSE[rows, :]))
        loop(LEN // TR, body, *events)

    for k in range(PAIRS):
        until("ag1", PO + 3 + k)
        attend_pair(k, ("ag2", PO + 1 + k), ("ag3", PO + k))

    ready(PO)
    norm_cols = pl.ds(cols[PO][0] + HC, 128)
    NV[...] = W[:, norm_cols].astype(F32).T[0:8, :]

    @pl.when(native)
    def _():
        tok_core.wait_send()

    @pl.when(away)
    def _():
        tok_pass.wait_send()

    def partial(lhs, dst_rows_at, finish):
        def body(i):
            r = pl.multiple_of(i * TR, TR)
            acc = None
            for ref, a, n, w0 in lhs:
                term = nt(ref[pl.ds(dst_rows_at + r, TR), pl.ds(a, n)], W[:, pl.ds(w0, n)])
                acc = term if acc is None else acc + term
            finish(r, acc)
        loop(HALF // TR, body)

    def to_x(r, acc):
        X[pl.ds(oth_r + r, TR), :] = acc.astype(BF)

    def to_n2(r, acc):
        N2[pl.ds(r, TR), :] = acc

    out_terms = [(A, 0, HC, cols[PO][0])]
    partial(out_terms, oth_r, to_x)
    part0 = core_send(X.at[oth_rows], R, 6)
    part0.start()
    partial(out_terms, own_r, to_n2)
    until("ag1", PG + 5)
    part0.wait_recv()

    TN = 64
    inv_d = 1.0 / D

    def norm1(i):
        r = pl.multiple_of(i * TN, TN)
        rows = pl.ds(r, TN)
        mix = X[pl.ds(own_r + r, TN), :].astype(F32) + N2[rows, :] + R[rows, :].astype(F32)
        mean = jnp.sum(mix, axis=1, keepdims=True) * inv_d
        cen = mix - mean
        var = jnp.sum(cen * cen, axis=1, keepdims=True) * inv_d
        rs = lax.rsqrt(var + epsilon)
        n = cen * rs
        N1[rows, :] = n
        RS1[rows, :] = jnp.broadcast_to(rs, (TN, 128))
        M[pl.ds(own_r + r, TN), :] = (n * NV[0:1, :] + NV[2:3, :]).astype(BF)
    loop(HALF // TN, norm1)
    mid = core_send(M.at[own_rows], M.at[own_rows], 7)
    mid.start()
    until("ag2", PG + 3)
    rc(M.at[oth_rows], M.at[oth_rows], sM.at[7], rM.at[7], dev_c).wait_recv()

    def sigmoid(v):
        return 1.0 / (1.0 + jnp.exp(-v))

    def hidden_chunk(g, *events):
        def body(i):
            r = pl.multiple_of(i * TR, TR)
            rows = pl.ds(r, TR)
            pre = nn(M[rows, :], W[:, wcols(PG + g)])
            gate, up = pre[:, :GH], pre[:, GH:]
            GT[rows, pl.ds(g * GH, GH)] = gate.astype(BF)
            UP[rows, pl.ds(g * GH, GH)] = up.astype(BF)
            H[rows, pl.ds(g * GH, GH)] = (gate * sigmoid(gate) * up).astype(BF)
        loop(LEN // TR, body, *events)

    for g in range(NG_PARTS):
        ready(PG + g)
        if g == 1:
            transpose_into(M, MT)
        hidden_chunk(g)
    for p in range(PD, NPARTS):
        ready(p)
    part0.wait_send()
    mid.wait_send()

    down_terms = [(H, j * CH, CH, cols[PD + j][0]) for j in range(3)]
    partial(down_terms, oth_r, to_x)
    part1 = core_send(X.at[oth_rows], R, 8)
    part1.start()
    partial(down_terms, own_r, to_n2)

    @pl.when(native)
    def _():
        cot_home.wait()

    @pl.when(away)
    def _():
        rc(cot_ref, C, sM.at[5], rM.at[5], dev_d).wait_recv()

    part1.wait_recv()

    def norm2(i, carry):
        dg, db = carry
        r = pl.multiple_of(i * TN, TN)
        rows = pl.ds(r, TN)
        first = N1[rows, :] * NV[0:1, :] + NV[2:3, :]
        v = first + N2[rows, :] + R[rows, :].astype(F32)
        mean = jnp.sum(v, axis=1, keepdims=True) * inv_d
        cen = v - mean
        var = jnp.sum(cen * cen, axis=1, keepdims=True) * inv_d
        rs = lax.rsqrt(var + epsilon)
        n = cen * rs
        e = C[rows, :].astype(F32)
        C[rows, :] = (n * NV[1:2, :] + NV[3:4, :]).astype(BF)
        eg = e * NV[1:2, :]
        m1 = jnp.sum(eg, axis=1, keepdims=True) * inv_d
        m2 = jnp.sum(eg * n, axis=1, keepdims=True) * inv_d
        d = rs * (eg - m1 - n * m2)
        N2[rows, :] = d
        M[pl.ds(own_r + r, TN), :] = d.astype(BF)
        return dg + jnp.sum(e * n, axis=0, keepdims=True), db + jnp.sum(e, axis=0, keepdims=True)

    zero_row = jnp.zeros((1, D), F32)
    dg1, db1 = lax.fori_loop(0, HALF // TN, norm2, (zero_row, zero_row))
    d2 = core_send(M.at[own_rows], M.at[own_rows], 9)
    d2.start()
    NG[...] = jnp.zeros(NG.shape, F32)
    NG[1:2, :] = dg1
    NG[3:4, :] = db1

    for p in range(NPARTS):
        ag_sent(p)

    act_home = pltpu.make_async_copy(C, act_out, sM.at[10])
    act_away = rc(C, act_out, sM.at[10], rM.at[10], dev_d)

    @pl.when(native)
    def _():
        act_home.start()

    @pl.when(away)
    def _():
        act_away.start()

    land = {p: p for p in range(NPARTS)}
    land[PG + 2] = PD + 1
    land[PG + 3] = PD
    land[PQ] = PG + 3
    land[PK] = PG + 2
    land[PO] = PG + 4
    land[PV] = PG + 5
    credits = {PD: [PD, PG + 3], PD + 1: [PG + 2], PD + 2: [PD + 2]}
    credits["mid"] = [PG, PG + 1, PG + 4, PG + 5, PQ, PK, PO, PV]

    def wland(p, zz, yy):
        if p == PD + 1:
            return LD.at[zz]
        return W.at[rows_of(zz, yy), pl.ds(cols[land[p]][0], cols[p][1])]

    def credit(k):
        @pl.when(native)
        def _():
            for p in credits[k]:
                pl.semaphore_signal(cred.at[p], inc=1, device_id=dev_x, device_id_type=MESH_ID)

    def x_block(p, d):
        zz = zof(d)
        yy = lax.rem(zz + p + 1, 2)
        return rc(blk(G, p, zz, yy), wland(p, zz, yy), sX.at[p], rX.at[p, d], dev_x)

    def y_block(p, d):
        return rc(blk(G, p, zof(d), 1 - y), Ly.at[zof(d), :, cslice(p)], sY.at[p], rY.at[p, d], dev_y)

    def y_arrival(p, d):
        return rc(blk(G, p, zof(d), y), Ly.at[zof(d), :, cslice(p)], sY.at[p], rY.at[p, d], dev_y)

    def z_block(p, d):
        return rc(blk(G, p, zof(d), y), Lz.at[d - 1, :, cslice(p)], sZ.at[p], rZ.at[p], dev_z(d))

    def x_final(p):
        return rc(blk(G, p, z, y), Lx.at[:, cslice(p)], sXF.at[p], rXF.at[p], dev_x)

    def out_copies(p):
        lo = pl.multiple_of(c * SH, 16)
        c0, n = cols[p]
        if p in (PQ, PK, PV):
            pieces = [(c0, n, gq_out.at[p])]
        elif p == PO:
            pieces = [(c0, n, go_out)]
        elif p < PD:
            j = p - PG
            pieces = [(c0 + i * GH, GH, ggu_out.at[i, :, pl.ds(j * GH, GH)]) for i in range(2)]
        else:
            pieces = [(c0, n, gd_out.at[:, pl.ds((p - PD) * CH, CH)])]
        return [
            pltpu.make_async_copy(F.at[pl.ds(lo, SH), pl.ds(a, m)], dst, sO.at[p])
            for a, m, dst in pieces
        ]

    def f_rows(core):
        return pl.ds(pl.multiple_of(core * SH, 16), SH)

    def f_send(p):
        part = F.at[f_rows(oc), cslice(p)]
        return rc(part, part, sF.at[p], rF.at[p], dev_c)

    def f_arrival(p):
        part = F.at[f_rows(c), cslice(p)]
        return rc(part, part, sF.at[p], rF.at[p], dev_c)

    def rs1(p):
        def gy(d, carry):
            when(crosses_first(p, zof(d), 1 - y), lambda: y_block(p, d).start())
            return carry
        lax.fori_loop(0, 4, gy, 0)

        @pl.when(away)
        def _():
            if p != PD + 1:
                pl.semaphore_wait(cred.at[p], 1)

            def go(d, carry):
                x_block(p, d).start()
                return carry
            lax.fori_loop(0, 4, go, 0)

    def rs1n(p, d):
        zz = zof(d)

        @pl.when(both(native, jnp.logical_not(crosses_first(p, zz, 1 - y))))
        def _():
            x_block(p, d).wait_recv()
            rows = rows_of(zz, 1 - y)
            G[rows, cslice(p)] = (G[rows, cslice(p)].astype(F32) + wland(p, zz, 1 - y)[...].astype(F32)).astype(BF)
            y_block(p, d).start()

    def rs2(p, i):
        d = lax.rem(i + 1, 4)
        zz = zof(d)
        rows = rows_of(zz, y)
        first = crosses_first(p, zz, y)

        def finish(total):
            G[rows, cslice(p)] = total.astype(BF)
            when(d > 0, lambda: z_block(p, d).start())

        @pl.when(both(native, jnp.logical_not(first)))
        def _():
            x_block(p, d).wait_recv()
            y_arrival(p, d).wait_recv()
            finish(G[rows, cslice(p)].astype(F32) + Ly[zz, :, cslice(p)].astype(F32) + wland(p, zz, y)[...].astype(F32))

        @pl.when(first)
        def _():
            y_arrival(p, d).wait_recv()
            finish(G[rows, cslice(p)].astype(F32) + Ly[zz, :, cslice(p)].astype(F32))

    def rs3(p):
        own_first = crosses_first(p, z, y)

        def total():
            three = Lz.at[:, :, cslice(p)]
            pltpu.make_async_copy(three, three, rZ.at[p]).wait()
            out = G[rows_of(z, y), cslice(p)].astype(F32)
            for k in range(3):
                out = out + Lz[k, :, cslice(p)].astype(F32)
            return out

        @pl.when(native)
        def _():
            F[:, cslice(p)] = total()

        @pl.when(both(away, own_first))
        def _():
            G[rows_of(z, y), cslice(p)] = total().astype(BF)
            x_final(p).start()

    def rs4(p):
        @pl.when(native)
        def _():
            @pl.when(crosses_first(p, z, y))
            def _():
                x_final(p).wait_recv()
                F[:, cslice(p)] = F[:, cslice(p)] + Lx[:, cslice(p)].astype(F32)
            f_send(p).start()

        when(away, lambda: f_arrival(p).wait_recv())
        for cp in out_copies(p):
            cp.start()

    def rs_sent(p):
        own_first = crosses_first(p, z, y)

        @pl.when(native)
        def _():
            wait_bytes(p, 4, sY.at[p])
            wait_bytes(p, 3, sZ.at[p])
            f_send(p).wait_send()

        @pl.when(away)
        def _():
            wait_bytes(p, 4, sX.at[p])
            wait_bytes(p, 2, sY.at[p])

            @pl.when(own_first)
            def _():
                wait_bytes(p, 1, sZ.at[p])
                x_final(p).wait_send()
            when(jnp.logical_not(own_first), lambda: wait_bytes(p, 2, sZ.at[p]))

        part = F.at[f_rows(c), cslice(p)]
        pltpu.make_async_copy(part, part, sO.at[p]).wait()

    kinds.update({"rs1": rs1, "rs1n": rs1n, "rs2": rs2, "rs3": rs3, "rs4": rs4})
    order = [PD + 1, PG + 2, PD, PG + 3, PD + 2, PG, PG + 1, PG + 4, PG + 5, PO, PV, PQ, PK]
    assert not queue
    for i in range(NPARTS + 4):
        for lag, name in enumerate(("rs1", "rs1n", "rs2", "rs3", "rs4")):
            if 0 <= i - lag < NPARTS:
                queue.append((name, order[i - lag]))

    def transpose_half(src, dst, first_row):
        def body(i):
            r = pl.multiple_of(first_row + i * TR, TR)
            dst[:, pl.ds(r, TR)] = src[pl.ds(r, TR), :].T
        loop(HALF // TR, body)

    transpose_half(M, DT, own_r)
    rc(M.at[oth_rows], M.at[oth_rows], sM.at[9], rM.at[9], dev_c).wait_recv()
    transpose_half(M, DT, oth_r)

    def back_chunk(j, *events):
        hc = pl.ds(j * CH, CH)

        def body(i):
            r = pl.multiple_of(i * TR, TR)
            rows = pl.ds(r, TR)
            dh = nn(M[rows, :], W[:, wcols(PD + j)]).astype(BF).astype(F32)
            gate = GT[rows, hc].astype(F32)
            up = UP[rows, hc].astype(F32)
            sg = sigmoid(gate)
            GT[rows, hc] = (dh * up * (sg * (1.0 + gate * (1.0 - sg)))).astype(BF)
            UP[rows, hc] = (dh * gate * sg).astype(BF)
        loop(LEN // TR, body, *events)

    WR = D // 4

    def weight_grad(left, pieces, *events):
        def body(i):
            r = pl.multiple_of(i * WR, 64)
            for right, a, n, c0 in pieces:
                G[pl.ds(r, WR), pl.ds(c0, n)] = nn(left[pl.ds(r, WR), :], right[:, pl.ds(a, n)]).astype(BF)
        loop(4, body, *events)

    def grads_down(j, *events):
        weight_grad(DT, [(H, j * CH, CH, cols[PD + j][0])], *events)

    def grads_gate_up(g, *events):
        c0 = cols[PG + g][0]
        weight_grad(MT, [(GT, g * GH, GH, c0), (UP, g * GH, GH, c0 + GH)], *events)

    def now(p):
        if ("rs1", p) in queue:
            queue.remove(("rs1", p))
        rs1(p)

    grads_down(1)
    now(PD + 1)
    back_chunk(1)
    credit(PD + 1)
    grads_gate_up(2)
    now(PG + 2)
    grads_gate_up(3)
    back_chunk(0, ("rs1n", PD + 1))
    credit(PD)
    grads_down(0)
    now(PD)
    grads_gate_up(0, ("rs1n", PG + 2))
    grads_gate_up(1, ("rs2", PD + 1))
    now(PG + 3)
    back_chunk(2, ("rs1n", PD))
    credit(PD + 2)
    grads_down(2, ("rs2", PG + 2))
    until("rs3", PD + 1)
    now(PD + 2)
    grads_gate_up(4, ("rs1n", PG + 3))
    grads_gate_up(5, ("rs2", PD))
    until("rs4", PD + 1)

    mid_terms = []
    for g in range(NG_PARTS):
        mid_terms.append((GT, g * GH, GH, cols[PG + g][0]))
        mid_terms.append((UP, g * GH, GH, cols[PG + g][0] + GH))
    part1.wait_send()
    partial(mid_terms, oth_r, to_x)
    part2 = core_send(X.at[oth_rows], R, 11)
    part2.start()

    def to_n2_add(r, acc):
        N2[pl.ds(r, TR), :] = N2[pl.ds(r, TR), :] + acc
    partial(mid_terms, own_r, to_n2_add)
    credit("mid")
    now(PG)
    d2.wait_send()
    part2.wait_recv()

    def norm1_back(i, carry):
        dg, db = carry
        r = pl.multiple_of(i * TN, TN)
        rows = pl.ds(r, TN)
        e = N2[rows, :] + R[rows, :].astype(F32)
        n = N1[rows, :]
        rs = RS1[rows, 0:1]
        eg = e * NV[0:1, :]
        m1 = jnp.sum(eg, axis=1, keepdims=True) * inv_d
        m2 = jnp.sum(eg * n, axis=1, keepdims=True) * inv_d
        d = rs * (eg - m1 - n * m2)
        N2[rows, :] = d
        M[pl.ds(own_r + r, TN), :] = d.astype(BF)
        return dg + jnp.sum(e * n, axis=0, keepdims=True), db + jnp.sum(e, axis=0, keepdims=True)

    dg0, db0 = lax.fori_loop(0, HALF // TN, norm1_back, (zero_row, zero_row))
    d1 = core_send(M.at[own_rows], M.at[own_rows], 12)
    d1.start()
    NG[0:1, :] = dg0
    NG[2:3, :] = db0
    ng = core_send(NG, NGR, 13)
    ng.start()
    until("rs3", PG + 2)
    rc(M.at[oth_rows], M.at[oth_rows], sM.at[12], rM.at[12], dev_c).wait_recv()
    transpose_into(M, DT, ("rs1n", PD + 2))
    ng.wait_recv()
    NGT[...] = jnp.zeros(NGT.shape, F32)
    NGT[0:8, :] = NG[...] + NGR[...]
    G[:, norm_cols] = NGT[...].T.astype(BF)

    def d_att(i):
        r = pl.multiple_of(i * TR, TR)
        rows = pl.ds(r, TR)
        da = nn(M[rows, :], W[:, wcols(PO, 0, HC)]).astype(BF)
        UP[rows, pl.ds(0, HC)] = da
        prod = da.astype(F32) * A[rows, :].astype(F32)
        acc = jnp.zeros((TR, 128), F32)
        for k in range(PAIRS):
            piece = prod[:, 128 * k : 128 * (k + 1)]
            d0 = jnp.sum(jnp.where(head0, piece, 0.0), axis=1, keepdims=True)
            dall = jnp.sum(piece, axis=1, keepdims=True)
            acc = jnp.where(lane == 2 * k, d0, jnp.where(lane == 2 * k + 1, dall - d0, acc))
        DEL[rows, :] = acc
    loop(LEN // TR, d_att, ("rs2", PG + 3))
    weight_grad(DT, [(A, 0, HC, cols[PO][0])])
    now(PG + 1)
    until("rs4", PG + 2)
    LST[...] = LSE[...].T[0:8, :]
    DLT[...] = DEL[...].T[0:8, :]

    def attend_back(k, *events):
        pair = slice(128 * k, 128 * (k + 1))
        DQT[...] = jnp.zeros(DQT.shape, F32)

        def body(i):
            r = pl.multiple_of(i * TR, TR)
            rows = pl.ds(r, TR)
            keys = K[rows, pair].astype(F32) * scale
            vals = V[rows, pair]
            qp = Q[:, pair]
            da = UP[:, pair]
            same = SEGC[rows, 0:1] == SEGR[0:1, :]
            dv, dk = [], []
            for s in range(2):
                h = 2 * k + s
                mine = head0 if s == 0 else jnp.logical_not(head0)
                km = jnp.where(mine, keys, 0.0)
                vm = jnp.where(mine, vals.astype(F32), 0.0).astype(BF)
                sc = nt(km.astype(BF), qp)
                pr = jnp.where(same, jnp.exp(sc - LST[h : h + 1, :]), 0.0)
                dp = nt(vm, da)
                ds = (pr * (dp - DLT[h : h + 1, :])).astype(BF)
                dv.append(nn(pr.astype(BF), da))
                dk.append(nn(ds, qp))
                DQT[...] = DQT[...] + nn(km.T.astype(BF), ds)
            GT[rows, 2 * HC + 128 * k : 2 * HC + 128 * (k + 1)] = jnp.where(head0, dv[0], dv[1]).astype(BF)
            GT[rows, HC + 128 * k : HC + 128 * (k + 1)] = unrot(jnp.where(head0, dk[0], dk[1]) * scale, r, TR).astype(BF)
        loop(LEN // TR, body, *events)

        def finish(i):
            r = pl.multiple_of(i * 128, 128)
            GT[pl.ds(r, 128), pair] = unrot(DQT[:, pl.ds(r, 128)].T, r, 128).astype(BF)
        loop(LEN // 128, finish)

    attend_back(0, ("rs1n", PG), ("rs2", PD + 2))
    until("rs3", PG + 3)
    now(PG + 4)
    attend_back(1, ("rs1n", PG + 1), ("rs2", PG))
    until("rs3", PD + 2)
    now(PG + 5)
    attend_back(2, ("rs1n", PG + 4), ("rs2", PG + 1))
    until("rs3", PG)
    now(PO)

    weight_grad(XT, [(GT, 2 * HC, HC, cols[PV][0])], ("rs1n", PG + 5))
    now(PV)
    weight_grad(XT, [(GT, 0, HC, cols[PQ][0])], ("rs2", PG + 4))
    now(PQ)
    weight_grad(XT, [(GT, HC, HC, cols[PK][0])], ("rs1n", PO))
    now(PK)

    in_terms = [(GT, 0, 3 * HC, 0)]
    part2.wait_send()
    partial(in_terms, oth_r, to_x)
    part3 = core_send(X.at[oth_rows], R, 14)
    part3.start()
    partial(in_terms, own_r, to_n2_add)

    @pl.when(native)
    def _():
        act_home.wait()

    @pl.when(away)
    def _():
        act_away.wait_send()

    part3.wait_recv()

    gtok_home = pltpu.make_async_copy(N2, gtok_out, sM.at[15])
    gtok_away = rc(C, GL, sM.at[15], rM.at[15], dev_d)

    def add_rows(i):
        r = pl.multiple_of(i * TN, TN)
        rows = pl.ds(r, TN)
        total = N2[rows, :] + R[rows, :].astype(F32)
        N2[rows, :] = total
        C[rows, :] = total.astype(BF)
    loop(HALF // TN, add_rows)

    @pl.when(native)
    def _():
        gtok_home.start()

    @pl.when(away)
    def _():
        gtok_away.start()

    while queue:
        step()

    @pl.when(away)
    def _():
        rc(C, GL, sM.at[15], rM.at[15], dev_d).wait_recv()
        N1[...] = GL[...].astype(F32)
        out = pltpu.make_async_copy(N1, gtok_out, sM.at[16])
        out.start()
        out.wait()
        gtok_away.wait_send()
        rc(C, act_out, sM.at[10], rM.at[10], dev_d).wait_recv()
        tok_away.wait_send()
        cot_away.wait_send()

    @pl.when(native)
    def _():
        gtok_home.wait()
        seg_send.wait_send()

    d1.wait_send()
    ng.wait_send()
    part3.wait_send()
    for p in range(NPARTS):
        rs_sent(p)


def on_device_fused(
    tokens, segments, qkv_weight, out_weight, gate_up_weight, down_weight, norm_gain, norm_shift, cotangent
):
    length, width = segments.shape[1], tokens.shape[1]
    half = tokens.shape[0]
    hc, fc = qkv_weight.shape[3], gate_up_weight.shape[3]
    sh = qkv_weight.shape[2]
    nc = 4 * hc + 128 + 3 * fc
    cosine, sine = rope_numpy(length)
    norms = jnp.concatenate([norm_gain[0], norm_shift[0]], axis=0).T
    o_own = jnp.concatenate([out_weight[0].T, norms, jnp.zeros((sh, 128 - norms.shape[1]), BF)], axis=1)
    d_own = down_weight[0].T
    seg8 = jnp.broadcast_to(segments.astype(F32), (8, length))
    vm = pl.BlockSpec(memory_space=pltpu.VMEM)
    anyspec = pl.BlockSpec(memory_space=pl.ANY)
    V_ = pltpu.VMEM
    br = 2 * sh
    dma = pltpu.SemaphoreType.DMA
    scratch = [
        V_((width, nc), BF),
        V_((width, nc), BF),
        V_((NZ, br, nc), BF),
        V_((NZ - 1, br, nc), BF),
        V_((br, nc), BF),
        V_((br, nc), F32),
        V_((length, width), BF),
        V_((width, length), BF),
        V_((length, hc), BF),
        V_((length, hc), BF),
        V_((length, hc), BF),
        V_((length, hc), BF),
        V_((length, width), BF),
        V_((width, length), BF),
        V_((width, length), BF),
        V_((length, fc), BF),
        V_((length, fc), BF),
        V_((length, fc), BF),
        V_((half, width), BF),
        V_((half, width), BF),
        V_((half, width), F32),
        V_((half, width), F32),
        V_((half, 128), F32),
        V_((128, length), F32),
        V_((length, 128), F32),
        V_((8, length), F32),
        V_((length, 128), F32),
        V_((8, length), F32),
        V_((8, length), F32),
        V_((length, 128), F32),
        V_((8, width), F32),
        V_((8, width), F32),
        V_((8, width), F32),
        V_((128, width), F32),
        V_((half, width), BF),
        V_((NZ, br, fc // 3), BF),
        dma((NPARTS,)), dma((NPARTS,)), dma((NPARTS,)), dma((NPARTS,)), dma((NPARTS,)), dma((NPARTS, 8)),
        dma((NPARTS,)), dma((NPARTS, 4)), dma((NPARTS,)), dma((NPARTS,)), dma((NPARTS,)), dma((NPARTS, 4)),
        dma((NPARTS,)), dma((NPARTS,)), dma((NPARTS,)), dma((NPARTS,)), dma((NPARTS,)),
        dma((17,)), dma((17,)),
        pltpu.SemaphoreType.REGULAR((NPARTS,)),
    ]
    act, gtok, gq, go, ggu, gd = pl.pallas_call(
        functools.partial(layer_kernel, (length, width, hc, fc)),
        out_shape=(
            jax.ShapeDtypeStruct((half, width), BF),
            jax.ShapeDtypeStruct((half, width), F32),
            jax.ShapeDtypeStruct((3, sh, hc), F32),
            jax.ShapeDtypeStruct((sh, hc + 128), F32),
            jax.ShapeDtypeStruct((2, sh, fc), F32),
            jax.ShapeDtypeStruct((sh, fc), F32),
        ),
        in_specs=[anyspec, anyspec, vm, vm, vm, anyspec, anyspec, anyspec, anyspec],
        out_specs=tuple([anyspec] * 6),
        scratch_shapes=scratch,
        compiler_params=pltpu.CompilerParams(
            collective_id=1, has_side_effects=True, vmem_limit_bytes=VMEM_LIMIT
        ),
        name="layer",
    )(tokens, cotangent, seg8, jnp.asarray(cosine), jnp.asarray(sine), qkv_weight[0], o_own, gate_up_weight[0], d_own)
    ngrad = go[:, hc : hc + 4].T
    return (
        act,
        gtok,
        gq[None],
        go[:, :hc].T[None],
        ggu[None],
        gd.T[None],
        ngrad[0:2][None],
        ngrad[2:4][None],
    )


VMEM_LIMIT = 64 * 1024 * 1024


def solution(mesh):
    body = on_device_fused if dict(mesh.shape) == {"fsdp": 16, "tp": 2} else on_device
    placed = (
        P(("fsdp", "tp"), None),
        P("fsdp", None),
        P(None, None, "fsdp", "tp"),
        P(None, "tp", "fsdp"),
        P(None, None, "fsdp", "tp"),
        P(None, "tp", "fsdp"),
        P(None, None, "fsdp"),
        P(None, None, "fsdp"),
        P(("fsdp", "tp"), None),
    )
    return jax.shard_map(
        body,
        mesh=mesh,
        in_specs=placed,
        out_specs=(
            P(("fsdp", "tp"), None),
            P(("fsdp", "tp"), None),
            P(None, None, "fsdp", "tp"),
            P(None, "tp", "fsdp"),
            P(None, None, "fsdp", "tp"),
            P(None, "tp", "fsdp"),
            P(None, None, "fsdp"),
            P(None, None, "fsdp"),
        ),
        check_vma=False,
    )
```

```python
import functools

import jax
import jax.numpy as jnp
import numpy as np
from jax import lax
from jax.experimental import pallas as pl
from jax.experimental.pallas import tpu as pltpu
from jax.sharding import PartitionSpec as P

HEAD_DIM = 64


epsilon = 1e-05


def for_sending(value):

    def short(part):
        return part.astype(jnp.bfloat16) if part.dtype == jnp.float32 else part

    return jax.tree.map(short, value)


def rope_tables(length):
    half_dim = HEAD_DIM // 2
    inv_freq = 1000.0 ** (-jnp.arange(half_dim, dtype=jnp.float32) * 2.0 / HEAD_DIM)
    angles = jnp.arange(length, dtype=jnp.float32)[:, None] * inv_freq[None, :]
    cosine = jnp.concatenate([jnp.cos(angles), jnp.cos(angles)], axis=-1)[:, None, :]
    sine_table = jnp.concatenate([jnp.sin(angles), jnp.sin(angles)], axis=-1)[:, None, :]
    return (cosine, sine_table)


def rotate(values_in, cosine, sine_table):
    half_dim = values_in.shape[-1] // 2
    turned = jnp.concatenate([-values_in[..., half_dim:], values_in[..., :half_dim]], axis=-1)
    return values_in * cosine + turned * sine_table


def unrotate(grads_in, cosine, sine_table):
    half_dim = grads_in.shape[-1] // 2
    moved_part = grads_in * sine_table
    return grads_in * cosine + jnp.concatenate(
        [moved_part[..., half_dim:], -moved_part[..., :half_dim]], axis=-1
    )


def norm_rows(stream, scale_vec, shift_vec):
    row_mean = jnp.mean(stream, axis=-1, keepdims=True)
    centred = stream - row_mean
    row_var = jnp.mean(centred * centred, axis=-1, keepdims=True)
    return centred * lax.rsqrt(row_var + epsilon) * scale_vec + shift_vec


def swiglu(gate_pre, up_proj):
    return jax.nn.silu(gate_pre) * up_proj


def spread(stream_low):
    return lax.all_gather(stream_low, "tp", axis=0, tiled=True)


def collect(partial_rows):
    return lax.psum_scatter(
        partial_rows.astype(jnp.bfloat16), "tp", scatter_dimension=0, tiled=True
    ).astype(jnp.float32)


def spread_grads(grads_low):
    return lax.all_gather(grads_low, "tp", axis=0, tiled=True)


def collect_grads(partial_rows):
    return lax.psum_scatter(
        partial_rows.astype(jnp.bfloat16), "tp", scatter_dimension=0, tiled=True
    ).astype(jnp.float32)


def layer_shards(arrays, layer_index):
    return tuple((weight_part[layer_index] for weight_part in arrays))


def block_scores(query_blk, keys_seq, seg_blk, seg_seq):
    scores = jnp.einsum(
        "qhd,khd->hqk", query_blk, keys_seq, preferred_element_type=jnp.float32
    ) * HEAD_DIM ** (-0.5)
    joined = seg_blk[:, None] == seg_seq[None, :]
    return jnp.where(joined[None], scores, -1e30)


def attend_forward(queries, keys_rot, values, segments):
    seq_count, length = segments.shape
    block_rows = min(512, length)
    block_count = length // block_rows

    def attend_one_block(flat_index):
        sequence = flat_index // block_count
        row_start = flat_index % block_count * block_rows
        query_seq = lax.dynamic_index_in_dim(queries, sequence, 0, False)
        keys_seq = lax.dynamic_index_in_dim(keys_rot, sequence, 0, False)
        values_seq = lax.dynamic_index_in_dim(values, sequence, 0, False)
        seg_seq = lax.dynamic_index_in_dim(segments, sequence, 0, False)
        query_blk = lax.dynamic_slice_in_dim(query_seq, row_start, block_rows, 0)
        seg_blk = lax.dynamic_slice_in_dim(seg_seq, row_start, block_rows, 0)
        scores = block_scores(query_blk, keys_seq, seg_blk, seg_seq)
        row_max = jnp.max(scores, axis=-1, keepdims=True)
        exp_terms = jnp.exp(scores - row_max)
        row_total = jnp.sum(exp_terms, axis=-1, keepdims=True)
        probs_low = (exp_terms / row_total).astype(jnp.bfloat16)
        attended = jnp.einsum(
            "hqk,khd->qhd", probs_low, values_seq, preferred_element_type=jnp.float32
        )
        return (attended, row_max + jnp.log(row_total))

    attended, log_total = lax.map(
        attend_one_block, jnp.arange(seq_count * block_count, dtype=jnp.int32)
    )
    return (attended.reshape(seq_count * length, -1), log_total)


def attend_backward(queries, keys_rot, values, d_attended, log_total, segments):
    seq_count, length = segments.shape
    block_rows = min(512, length)
    block_count = length // block_rows
    scale_value = HEAD_DIM ** (-0.5)

    def one_sequence(sequence):
        query_seq = lax.dynamic_index_in_dim(queries, sequence, 0, False)
        keys_seq = lax.dynamic_index_in_dim(keys_rot, sequence, 0, False)
        values_seq = lax.dynamic_index_in_dim(values, sequence, 0, False)
        d_out_seq = lax.dynamic_index_in_dim(d_attended, sequence, 0, False)
        seg_seq = lax.dynamic_index_in_dim(segments, sequence, 0, False)

        def one_one_block(running, block_index):
            row_start = block_index * block_rows
            query_blk = lax.dynamic_slice_in_dim(query_seq, row_start, block_rows, 0)
            d_out_blk = lax.dynamic_slice_in_dim(d_out_seq, row_start, block_rows, 0)
            seg_blk = lax.dynamic_slice_in_dim(seg_seq, row_start, block_rows, 0)
            block_total = lax.dynamic_index_in_dim(
                log_total, sequence * block_count + block_index, 0, False
            )
            scores = block_scores(query_blk, keys_seq, seg_blk, seg_seq)
            attn_probs = jnp.exp(scores - block_total)
            probs_low = attn_probs.astype(jnp.bfloat16)
            d_probs = jnp.einsum(
                "qhd,khd->hqk", d_out_blk, values_seq, preferred_element_type=jnp.float32
            )
            inner_sum = jnp.sum(attn_probs * d_probs, axis=-1, keepdims=True)
            d_scores = (attn_probs * (d_probs - inner_sum)).astype(jnp.bfloat16)
            d_query = (
                jnp.einsum("hqk,khd->qhd", d_scores, keys_seq, preferred_element_type=jnp.float32)
                * scale_value
            )
            d_key = (
                running[0]
                + jnp.einsum(
                    "hqk,qhd->khd", d_scores, query_blk, preferred_element_type=jnp.float32
                )
                * scale_value
            )
            d_value = running[1] + jnp.einsum(
                "hqk,qhd->khd", probs_low, d_out_blk, preferred_element_type=jnp.float32
            )
            return ((d_key, d_value), d_query)

        zero_keys = jnp.zeros(keys_seq.shape, jnp.float32)
        (d_keys, d_values), d_queries = lax.scan(
            one_one_block, (zero_keys, zero_keys), jnp.arange(block_count, dtype=jnp.int32)
        )
        return (d_queries.reshape(keys_seq.shape), d_keys, d_values)

    return lax.map(one_sequence, jnp.arange(seq_count, dtype=jnp.int32))


def layer_forward(stream, segments, weights, tables):
    qkv_w, out_w, gate_up_w, down_w, gain_rows, shift_rows = weights
    cosine, sine_table = tables
    seq_count, length = segments.shape
    head_count = qkv_w.shape[2] // HEAD_DIM
    shaped = (seq_count, length, head_count, HEAD_DIM)
    gain_vals = gain_rows.astype(jnp.float32)
    shift_vals = shift_rows.astype(jnp.float32)
    inputs = spread(stream.astype(jnp.bfloat16))
    query_pre = jnp.dot(inputs, qkv_w[0], preferred_element_type=jnp.float32).reshape(shaped)
    key_pre = jnp.dot(inputs, qkv_w[1], preferred_element_type=jnp.float32).reshape(shaped)
    queries = rotate(query_pre, cosine, sine_table).astype(jnp.bfloat16)
    keys_rot = rotate(key_pre, cosine, sine_table).astype(jnp.bfloat16)
    values = (
        jnp.dot(inputs, qkv_w[2], preferred_element_type=jnp.float32)
        .astype(jnp.bfloat16)
        .reshape(shaped)
    )
    attended, log_total = attend_forward(queries, keys_rot, values, segments)
    attended_low = attended.astype(jnp.bfloat16)
    branch = collect(jnp.dot(attended_low, out_w, preferred_element_type=jnp.float32))
    mixed = stream + branch
    first_norm = norm_rows(mixed, gain_vals[0], shift_vals[0])
    middle = spread(first_norm.astype(jnp.bfloat16))
    gate_pre = jnp.dot(middle, gate_up_w[0], preferred_element_type=jnp.float32)
    up_proj = jnp.dot(middle, gate_up_w[1], preferred_element_type=jnp.float32)
    hidden = swiglu(gate_pre, up_proj).astype(jnp.bfloat16)
    branch_two = collect(jnp.dot(hidden, down_w, preferred_element_type=jnp.float32))
    second_in = first_norm + branch_two
    saved_state = (
        inputs,
        queries,
        keys_rot,
        values,
        log_total,
        attended_low,
        mixed,
        middle,
        gate_pre,
        up_proj,
        hidden,
        second_in,
    )
    return (norm_rows(second_in, gain_vals[1], shift_vals[1]), saved_state)


def layer_backward(grad_out, saved_state, segments, weights, tables):
    qkv_w, out_w, gate_up_w, down_w, gain_rows, shift_rows = weights
    (
        inputs,
        queries,
        keys_rot,
        values,
        log_total,
        attended_low,
        mixed,
        middle,
        gate_pre,
        up_proj,
        hidden,
        second_in,
    ) = saved_state
    cosine, sine_table = tables
    gain_vals = gain_rows.astype(jnp.float32)
    shift_vals = shift_rows.astype(jnp.float32)
    unused_two, norm_two_back = jax.vjp(norm_rows, second_in, gain_vals[1], shift_vals[1])
    d_second, d_gain_two, d_shift_two = norm_two_back(grad_out)
    d_branch_two = spread_grads(d_second.astype(jnp.bfloat16))
    grad_down = jnp.einsum("rf,rd->fd", hidden, d_branch_two, preferred_element_type=jnp.float32)
    d_hidden_low = jnp.einsum(
        "rd,fd->rf", d_branch_two, down_w, preferred_element_type=jnp.float32
    ).astype(jnp.bfloat16)
    d_hidden = lax.optimization_barrier(d_hidden_low).astype(jnp.float32)
    unused_swish, swish_back = jax.vjp(swiglu, gate_pre, up_proj)
    d_gate, d_up = swish_back(d_hidden)
    d_gate_low = d_gate.astype(jnp.bfloat16)
    d_up_low = d_up.astype(jnp.bfloat16)
    grad_gate_up = jnp.stack(
        [
            jnp.einsum("rd,rf->df", middle, d_gate_low, preferred_element_type=jnp.float32),
            jnp.einsum("rd,rf->df", middle, d_up_low, preferred_element_type=jnp.float32),
        ]
    )
    d_middle = jnp.einsum("rf,df->rd", d_gate_low, gate_up_w[0], preferred_element_type=jnp.float32)
    d_middle = d_middle + jnp.einsum(
        "rf,df->rd", d_up_low, gate_up_w[1], preferred_element_type=jnp.float32
    )
    d_first = d_second + collect_grads(d_middle)
    unused_one, norm_one_back = jax.vjp(norm_rows, mixed, gain_vals[0], shift_vals[0])
    d_mixed, d_gain_one, d_shift_one = norm_one_back(d_first)
    d_branch = spread_grads(d_mixed.astype(jnp.bfloat16))
    grad_out_w = jnp.einsum("rc,rd->cd", attended_low, d_branch, preferred_element_type=jnp.float32)
    d_attended = (
        jnp.einsum("rd,cd->rc", d_branch, out_w, preferred_element_type=jnp.float32)
        .astype(jnp.bfloat16)
        .reshape(queries.shape)
    )
    d_queries, d_keys, d_values = attend_backward(
        queries, keys_rot, values, d_attended, log_total, segments
    )
    flat_shape = (-1, queries.shape[2] * queries.shape[3])
    d_query_low = unrotate(d_queries, cosine, sine_table).astype(jnp.bfloat16).reshape(flat_shape)
    d_key_low = unrotate(d_keys, cosine, sine_table).astype(jnp.bfloat16).reshape(flat_shape)
    d_value_low = d_values.astype(jnp.bfloat16).reshape(flat_shape)
    grad_parts = (d_query_low, d_key_low, d_value_low)
    grad_qkv = jnp.stack(
        [
            jnp.einsum("rd,rc->dc", inputs, grad_part, preferred_element_type=jnp.float32)
            for grad_part in grad_parts
        ]
    )
    d_inputs = jnp.einsum("rc,dc->rd", d_query_low, qkv_w[0], preferred_element_type=jnp.float32)
    d_inputs = d_inputs + jnp.einsum(
        "rc,dc->rd", d_key_low, qkv_w[1], preferred_element_type=jnp.float32
    )
    d_inputs = d_inputs + jnp.einsum(
        "rc,dc->rd", d_value_low, qkv_w[2], preferred_element_type=jnp.float32
    )
    d_stream = d_mixed + collect_grads(d_inputs)
    weight_grads = (
        grad_qkv,
        grad_out_w,
        grad_gate_up,
        grad_down,
        jnp.stack([d_gain_one, d_gain_two]),
        jnp.stack([d_shift_one, d_shift_two]),
    )
    return (d_stream, weight_grads)


def on_device(
    tokens,
    segments,
    qkv_weight,
    out_weight,
    gate_up_weight,
    down_weight,
    norm_gain,
    norm_shift,
    cotangent,
):
    arrays = (qkv_weight, out_weight, gate_up_weight, down_weight, norm_gain, norm_shift)
    layer_total = qkv_weight.shape[0]
    tables = rope_tables(segments.shape[1])
    stream = tokens.astype(jnp.float32)
    kept_weights = []
    layer_index = 0
    weights = lax.all_gather(
        for_sending(layer_shards(arrays, layer_index)), "fsdp", axis=1, tiled=True
    )
    stream, saved_state = layer_forward(stream, segments, weights, tables)
    kept_weights.append(weights)
    saved_states = [saved_state]
    activations = stream.astype(jnp.bfloat16)
    grad_stream = cotangent.astype(jnp.float32)
    grad_layers = [None] * layer_total
    for layer_index in reversed(range(layer_total)):
        weights = lax.all_gather(
            for_sending(layer_shards(arrays, layer_index)), "fsdp", axis=1, tiled=True
        )
        grad_stream, weight_grads = layer_backward(
            grad_stream, saved_states[layer_index], segments, weights, tables
        )
        grad_layers[layer_index] = (
            lax.psum_scatter(weight_grads[0], "fsdp", scatter_dimension=1, tiled=True),
            lax.psum_scatter(weight_grads[1], "fsdp", scatter_dimension=1, tiled=True),
            lax.psum_scatter(weight_grads[2], "fsdp", scatter_dimension=1, tiled=True),
            lax.psum_scatter(weight_grads[3], "fsdp", scatter_dimension=1, tiled=True),
            lax.psum_scatter(weight_grads[4], "fsdp", scatter_dimension=1, tiled=True),
            lax.psum_scatter(weight_grads[5], "fsdp", scatter_dimension=1, tiled=True),
        )
    stacked = [jnp.stack([grad_layers[0][member]]) for member in range(6)]
    gain_sum, shift_sum = lax.psum((stacked[4], stacked[5]), "tp")
    return (
        activations,
        grad_stream,
        stacked[0],
        stacked[1],
        stacked[2],
        stacked[3],
        gain_sum,
        shift_sum,
    )


MESH_ID = pl.DeviceIdType.MESH
BF = jnp.bfloat16
F32 = jnp.float32
NZ, NY = 4, 2
PQ, PK, PV, PO, PG = range(5)
NG_PARTS = 6
PD = PG + NG_PARTS
NPARTS = PD + 3
PAIRS = 3
NEG = -1e30


def nt(a, b):
    return lax.dot_general(a, b, (((1,), (1,)), ((), ())), preferred_element_type=F32)


def nn(a, b):
    return jnp.dot(a, b, preferred_element_type=F32)


def rope_numpy(length):
    half = HEAD_DIM // 2
    inv = 1000.0 ** (-np.arange(half, dtype=np.float64) * 2.0 / HEAD_DIM)
    angles = np.arange(length, dtype=np.float64)[:, None] * inv[None, :]
    cosine, sine = np.cos(angles), np.sin(angles)
    cos_rows = np.concatenate([cosine, cosine, cosine, cosine], axis=1)
    sin_rows = np.concatenate([-sine, sine, -sine, sine], axis=1)
    return cos_rows.astype(np.float32), sin_rows.astype(np.float32)


def layer_kernel(
    dims,
    tok_ref, cot_ref, seg_ref, cos_ref, sin_ref, qkv_in, out_ref, gu_in, down_ref, gain_ref, shift_ref,
    act_out, gtok_out, gq_out, go_out, ggu_out, gd_out,
    W, G, Ly, Lz, Lx, F, X, XT, Q, K, V, A, M, MT, DT, GT, UP, H, R, C, N1, N2, RS1,
    DQT, LSE, LST, DEL, DLT, SEGR, SEGC, NV, NG, NGR, NGT, GL, LD, OWN_N, N8,
    sLC, sCR, rCR, sA, sB, rB, sY, rY, sZ, rZ, sX, rX, sXF, rXF, sF, rF, sO, sM, rM, cred,
):
    LEN, D, HC, FC = dims
    HALF = LEN // 2
    SH = D // 16
    BR = 2 * SH
    CH = FC // 3
    GH = FC // NG_PARTS
    OW = HC + 128
    cols = {}
    at = 0
    for p in range(NPARTS):
        n = HC if p in (PQ, PK, PV) else OW if p == PO else 2 * GH if p < PD else CH
        cols[p] = (at, n)
        at += n

    f = lax.axis_index("fsdp")
    t = lax.axis_index("tp")
    c = lax.rem(f, 2)
    y = lax.rem(f // 2, 2)
    z = f // 4
    oc = 1 - c
    native = c == t
    away = c != t
    dev_x = (f, 1 - t)
    dev_y = ((z * 2 + (1 - y)) * 2 + c, t)
    dev_c = ((z * 2 + y) * 2 + oc, t)
    dev_d = ((z * 2 + y) * 2 + oc, 1 - t)

    def zof(d):
        return lax.rem(z + d, NZ)

    def dev_z(d):
        return ((zof(d) * 2 + y) * 2 + c, t)

    def rows_of(zz, yy):
        return pl.ds(pl.multiple_of((zz * 2 + yy) * BR, 16), BR)

    def cslice(p):
        return pl.ds(cols[p][0], cols[p][1])

    def blk(ref, p, zz, yy):
        return ref.at[rows_of(zz, yy), cslice(p)]

    def bid(zz, yy):
        return zz * 2 + yy

    def crosses_first(p, zz, yy):
        return lax.rem(zz + yy + p, 2) == 0

    def both(*conds):
        out = conds[0]
        for cond in conds[1:]:
            out = jnp.logical_and(out, cond)
        return out

    def when(cond, fn):
        pl.when(cond)(fn)

    def rc(src, dst, ss, rs, dev):
        return pltpu.make_async_remote_copy(
            src_ref=src, dst_ref=dst, send_sem=ss, recv_sem=rs, device_id=dev, device_id_type=MESH_ID
        )

    def wait_bytes(p, blocks, sem):
        ref = Ly.at[0, :, pl.ds(0, blocks * cols[p][1])]
        pltpu.make_async_copy(ref, ref, sem).wait()

    own_r = pl.multiple_of(c * HALF, HALF)
    oth_r = pl.multiple_of(oc * HALF, HALF)
    own_rows = pl.ds(own_r, HALF)
    oth_rows = pl.ds(oth_r, HALF)

    bar = pltpu.get_barrier_semaphore()
    partners = [dev_x, dev_y, dev_c, dev_d, dev_z(1), dev_z(2), dev_z(3)]
    for dev in partners:
        pl.semaphore_signal(bar, inc=1, device_id=dev, device_id_type=MESH_ID)
    pl.semaphore_wait(bar, len(partners))

    def shard_pieces(p):
        c0, n = cols[p]
        if p in (PQ, PK, PV):
            return [(qkv_in.at[0, p], c0, n)]
        if p == PO:
            return [(out_ref.at[0], c0, HC), (OWN_N, c0 + HC, 128)]
        if p < PD:
            j = p - PG
            return [(gu_in.at[0, i, :, pl.ds(j * GH, GH)], c0 + i * GH, GH) for i in range(2)]
        j = p - PD
        return [(down_ref.at[0, :, pl.ds(j * CH, CH)], c0, CH)]

    shard_rows = pl.ds(pl.multiple_of((z * 2 + y) * BR + c * SH, 16), SH)
    oshard_rows = pl.ds(pl.multiple_of((z * 2 + y) * BR + oc * SH, 16), SH)

    def start_shards(p):
        @pl.when(native)
        def _():
            for src, c0, n in shard_pieces(p):
                pltpu.make_async_copy(src, W.at[shard_rows, pl.ds(c0, n)], sLC.at[p]).start()

        @pl.when(away)
        def _():
            for src, c0, n in shard_pieces(p):
                rc(src, W.at[shard_rows, pl.ds(c0, n)], sCR.at[p], rCR.at[p], dev_c).start()

    def own_whole(p):
        return W.at[shard_rows, cslice(p)]

    tok_home = pltpu.make_async_copy(tok_ref, X.at[own_rows], sM.at[2])
    tok_core = rc(tok_ref, X.at[own_rows], sM.at[3], rM.at[3], dev_c)
    tok_away = rc(tok_ref, X.at[oth_rows], sM.at[4], rM.at[4], dev_d)
    tok_pass = rc(X.at[own_rows], X.at[own_rows], sM.at[3], rM.at[3], dev_c)
    seg_send = rc(SEGR, SEGR, sM.at[1], rM.at[1], dev_c)
    cot_home = pltpu.make_async_copy(cot_ref, C, sM.at[5])
    cot_away = rc(cot_ref, C, sM.at[5], rM.at[5], dev_d)

    start_shards(PQ)
    start_shards(PK)

    @pl.when(native)
    def _():
        tok_home.start()
        tok_core.start()
        cot_home.start()
        SEGR[...] = jnp.broadcast_to(seg_ref[...].astype(F32), SEGR.shape)
        seg_send.start()

    @pl.when(away)
    def _():
        tok_away.start()

    for p in range(2, NPARTS):
        if p != PO:
            start_shards(p)

    def ag_copy(p, zz, yy, dev, sem):
        b = blk(W, p, zz, yy)
        return rc(b, b, sem.at[p], rB.at[p, bid(zz, yy)], dev)

    def got(p, zz, yy):
        b = blk(W, p, zz, yy)
        rc(b, b, sA.at[p], rB.at[p, bid(zz, yy)], dev_x).wait_recv()

    def ag1(p):
        def spread_own():
            for d in (2, 1, 3):
                ag_copy(p, z, y, dev_z(d), sA).start()
            ag_copy(p, z, y, dev_y, sA).start()

        @pl.when(native)
        def _():
            pltpu.make_async_copy(own_whole(p), own_whole(p), sLC.at[p]).wait()
            o = W.at[oshard_rows, cslice(p)]
            rc(o, o, sCR.at[p], rCR.at[p], dev_c).wait_recv()
            ag_copy(p, z, y, dev_x, sA).start()
            spread_own()

        @pl.when(both(away, crosses_first(p, z, y)))
        def _():
            got(p, z, y)
            spread_own()

    def ag2(p, d):
        zz = zof(d)
        first = crosses_first(p, zz, y)

        def work():
            got(p, zz, y)
            ag_copy(p, zz, y, dev_y, sB).start()

            @pl.when(jnp.logical_not(first))
            def _():
                ag_copy(p, zz, y, dev_x, sB).start()

        when(both(d > 0, jnp.logical_or(native, first)), work)

    def ag3(p, d):
        zz = zof(d)
        first = crosses_first(p, zz, 1 - y)

        @pl.when(jnp.logical_or(native, first))
        def _():
            got(p, zz, 1 - y)

            @pl.when(jnp.logical_not(first))
            def _():
                ag_copy(p, zz, 1 - y, dev_x, sB).start()

    def ag4(p, d):
        zz = zof(d)
        yy = lax.rem(zz + p + 1, 2)

        @pl.when(away)
        def _():
            got(p, zz, yy)

    def ag_sent(p):
        own_first = crosses_first(p, z, y)

        @pl.when(native)
        def _():
            wait_bytes(p, 5, sA.at[p])
            when(own_first, lambda: wait_bytes(p, 7, sB.at[p]))
            when(jnp.logical_not(own_first), lambda: wait_bytes(p, 6, sB.at[p]))

        @pl.when(away)
        def _():
            @pl.when(own_first)
            def _():
                wait_bytes(p, 4, sA.at[p])
                wait_bytes(p, 1, sB.at[p])
            when(jnp.logical_not(own_first), lambda: wait_bytes(p, 2, sB.at[p]))
            pltpu.make_async_copy(own_whole(p), own_whole(p), sCR.at[p]).wait()

    def loop(n, body, *events):
        for ev in events:
            assert ev in queue and n == 4
            queue.remove(ev)

        def go(i, carry):
            body(i)
            for name, p in events:
                kinds[name](p, i)
            return carry
        lax.fori_loop(0, n, go, 0)

    queue = []
    for i in range(-2, NPARTS + 2):
        for name, lag in (("ag1", -2), ("ag2", 0), ("ag3", 1), ("ag4", 2)):
            if 0 <= i - lag < NPARTS:
                queue.append((name, i - lag))
    kinds = {"ag1": ag1, "ag2": ag2, "ag3": ag3, "ag4": ag4}
    whole = ("ag1", "rs1", "rs3", "rs4")

    def step():
        name, p = queue.pop(0)
        if name in whole:
            kinds[name](p)
        else:
            def go(i, carry):
                kinds[name](p, i)
                return carry
            lax.fori_loop(0, 4, go, 0)

    def until(name, p):
        while (name, p) in queue:
            step()

    def ready(p):
        until("ag3", p)
        if ("ag4", p) in queue:
            queue.remove(("ag4", p))
            queue.insert(0, ("ag4", p))
            step()

    lane = lax.broadcasted_iota(jnp.int32, (1, 128), 1)
    low_half = lax.rem(lane, HEAD_DIM) < HEAD_DIM // 2
    head0 = lane < HEAD_DIM

    def swap(v):
        return jnp.where(low_half, pltpu.roll(v, 128 - HEAD_DIM // 2, 1), pltpu.roll(v, HEAD_DIM // 2, 1))

    def rot(v, r, n):
        return v * cos_ref[pl.ds(r, n), :] + swap(v) * sin_ref[pl.ds(r, n), :]

    def unrot(v, r, n):
        return v * cos_ref[pl.ds(r, n), :] - swap(v) * sin_ref[pl.ds(r, n), :]

    def wcols(p, a=0, n=None):
        c0, m = cols[p]
        return pl.ds(c0 + a, m if n is None else n)

    TR = 256

    def transpose_into(src, dst, *events):
        def body(i):
            r = pl.multiple_of(i * TR, TR)
            dst[:, pl.ds(r, TR)] = src[pl.ds(r, TR), :].T
        loop(LEN // TR, body, *events)

    def core_send(src, dst, k):
        return rc(src, dst, sM.at[k], rM.at[k], dev_c)

    until("ag1", PK)

    eye = (
        lax.broadcasted_iota(jnp.int32, (SH, SH), 0) == lax.broadcasted_iota(jnp.int32, (SH, SH), 1)
    ).astype(BF)
    N8[...] = jnp.zeros(N8.shape, F32)
    N8[0:2, :] = gain_ref[0].astype(F32)
    N8[2:4, :] = shift_ref[0].astype(F32)
    OWN_N[...] = jnp.zeros(OWN_N.shape, BF)
    OWN_N[:, 0:8] = nt(eye, N8[...].astype(BF)).astype(BF)
    start_shards(PO)

    @pl.when(native)
    def _():
        tok_home.wait()

    @pl.when(away)
    def _():
        rc(SEGR, SEGR, sM.at[1], rM.at[1], dev_c).wait_recv()
    until("ag2", PQ)

    @pl.when(away)
    def _():
        rc(tok_ref, X.at[own_rows], sM.at[4], rM.at[4], dev_d).wait_recv()
        tok_pass.start()
    until("ag3", PQ)
    rc(X.at[oth_rows], X.at[oth_rows], sM.at[3], rM.at[3], dev_c).wait_recv()

    def seg_cols(i):
        r = pl.multiple_of(i * 128, 128)
        SEGC[pl.ds(r, 128), :] = jnp.broadcast_to(SEGR[0:1, pl.ds(r, 128)], (128, 128)).T
    loop(LEN // 128, seg_cols)

    def project(p, dst, turn, *events):
        def body(i):
            r = pl.multiple_of(i * TR, TR)
            v = nn(X[pl.ds(r, TR), :], W[:, wcols(p)])
            for k in range(PAIRS):
                part = v[:, 128 * k : 128 * (k + 1)]
                if turn:
                    part = rot(part, r, TR)
                dst[pl.ds(r, TR), 128 * k : 128 * (k + 1)] = part.astype(BF)
        loop(LEN // TR, body, *events)

    transpose_into(X, XT)
    ready(PQ)
    project(PQ, Q, True)
    ready(PK)
    project(PK, K, True)
    when(away, lambda: cot_away.start())
    ready(PV)
    project(PV, V, False)

    scale = HEAD_DIM ** -0.5
    LSE[...] = jnp.zeros(LSE.shape, F32)

    def attend_pair(k, *events):
        def body(i):
            r = pl.multiple_of(i * TR, TR)
            rows = pl.ds(r, TR)
            pair = slice(128 * k, 128 * (k + 1))
            q = Q[rows, pair]
            keys = K[:, pair]
            vals = V[:, pair]
            same = SEGC[rows, 0:1] == SEGR[0:1, :]
            outs, lses = [], []
            for s in range(2):
                mine = head0 if s == 0 else jnp.logical_not(head0)
                qm = jnp.where(mine, q.astype(F32) * scale, 0.0).astype(BF)
                sc = jnp.where(same, nt(qm, keys), NEG)
                top = jnp.max(sc, axis=1, keepdims=True)
                e = jnp.exp(sc - top)
                total = jnp.sum(e, axis=1, keepdims=True)
                outs.append(nn(e.astype(BF), vals) / total)
                lses.append(top + jnp.log(total))
            A[rows, pair] = jnp.where(head0, outs[0], outs[1]).astype(BF)
            LSE[rows, :] = jnp.where(lane == 2 * k, lses[0], jnp.where(lane == 2 * k + 1, lses[1], LSE[rows, :]))
        loop(LEN // TR, body, *events)

    for k in range(PAIRS):
        until("ag1", PO + 3 + k)
        attend_pair(k, ("ag2", PO + 1 + k), ("ag3", PO + k))

    ready(PO)
    norm_cols = pl.ds(cols[PO][0] + HC, 128)
    NV[...] = W[:, norm_cols].astype(F32).T[0:8, :]

    @pl.when(native)
    def _():
        tok_core.wait_send()

    @pl.when(away)
    def _():
        tok_pass.wait_send()

    def partial(lhs, dst_rows_at, finish):
        def body(i):
            r = pl.multiple_of(i * TR, TR)
            acc = None
            for ref, a, n, w0 in lhs:
                term = nt(ref[pl.ds(dst_rows_at + r, TR), pl.ds(a, n)], W[:, pl.ds(w0, n)])
                acc = term if acc is None else acc + term
            finish(r, acc)
        loop(HALF // TR, body)

    def to_x(r, acc):
        X[pl.ds(oth_r + r, TR), :] = acc.astype(BF)

    def to_n2(r, acc):
        N2[pl.ds(r, TR), :] = acc

    out_terms = [(A, 0, HC, cols[PO][0])]
    partial(out_terms, oth_r, to_x)
    part0 = core_send(X.at[oth_rows], R, 6)
    part0.start()
    partial(out_terms, own_r, to_n2)
    until("ag1", PG + 5)
    part0.wait_recv()

    TN = 64
    inv_d = 1.0 / D

    def norm1(i):
        r = pl.multiple_of(i * TN, TN)
        rows = pl.ds(r, TN)
        mix = X[pl.ds(own_r + r, TN), :].astype(F32) + N2[rows, :] + R[rows, :].astype(F32)
        mean = jnp.sum(mix, axis=1, keepdims=True) * inv_d
        cen = mix - mean
        var = jnp.sum(cen * cen, axis=1, keepdims=True) * inv_d
        rs = lax.rsqrt(var + epsilon)
        n = cen * rs
        N1[rows, :] = n
        RS1[rows, :] = jnp.broadcast_to(rs, (TN, 128))
        M[pl.ds(own_r + r, TN), :] = (n * NV[0:1, :] + NV[2:3, :]).astype(BF)
    loop(HALF // TN, norm1)
    mid = core_send(M.at[own_rows], M.at[own_rows], 7)
    mid.start()
    until("ag2", PG + 3)
    rc(M.at[oth_rows], M.at[oth_rows], sM.at[7], rM.at[7], dev_c).wait_recv()

    def sigmoid(v):
        return 1.0 / (1.0 + jnp.exp(-v))

    def hidden_chunk(g, *events):
        def body(i):
            r = pl.multiple_of(i * TR, TR)
            rows = pl.ds(r, TR)
            pre = nn(M[rows, :], W[:, wcols(PG + g)])
            gate, up = pre[:, :GH], pre[:, GH:]
            GT[rows, pl.ds(g * GH, GH)] = gate.astype(BF)
            UP[rows, pl.ds(g * GH, GH)] = up.astype(BF)
            H[rows, pl.ds(g * GH, GH)] = (gate * sigmoid(gate) * up).astype(BF)
        loop(LEN // TR, body, *events)

    for g in range(NG_PARTS):
        ready(PG + g)
        if g == 1:
            transpose_into(M, MT)
        hidden_chunk(g)
    for p in range(PD, NPARTS):
        ready(p)
    part0.wait_send()
    mid.wait_send()

    down_terms = [(H, j * CH, CH, cols[PD + j][0]) for j in range(3)]
    partial(down_terms, oth_r, to_x)
    part1 = core_send(X.at[oth_rows], R, 8)
    part1.start()
    partial(down_terms, own_r, to_n2)

    @pl.when(native)
    def _():
        cot_home.wait()

    @pl.when(away)
    def _():
        rc(cot_ref, C, sM.at[5], rM.at[5], dev_d).wait_recv()

    part1.wait_recv()

    def norm2(i, carry):
        dg, db = carry
        r = pl.multiple_of(i * TN, TN)
        rows = pl.ds(r, TN)
        first = N1[rows, :] * NV[0:1, :] + NV[2:3, :]
        v = first + N2[rows, :] + R[rows, :].astype(F32)
        mean = jnp.sum(v, axis=1, keepdims=True) * inv_d
        cen = v - mean
        var = jnp.sum(cen * cen, axis=1, keepdims=True) * inv_d
        rs = lax.rsqrt(var + epsilon)
        n = cen * rs
        e = C[rows, :].astype(F32)
        C[rows, :] = (n * NV[1:2, :] + NV[3:4, :]).astype(BF)
        eg = e * NV[1:2, :]
        m1 = jnp.sum(eg, axis=1, keepdims=True) * inv_d
        m2 = jnp.sum(eg * n, axis=1, keepdims=True) * inv_d
        d = rs * (eg - m1 - n * m2)
        N2[rows, :] = d
        M[pl.ds(own_r + r, TN), :] = d.astype(BF)
        return dg + jnp.sum(e * n, axis=0, keepdims=True), db + jnp.sum(e, axis=0, keepdims=True)

    zero_row = jnp.zeros((1, D), F32)
    dg1, db1 = lax.fori_loop(0, HALF // TN, norm2, (zero_row, zero_row))
    d2 = core_send(M.at[own_rows], M.at[own_rows], 9)
    d2.start()
    NG[...] = jnp.zeros(NG.shape, F32)
    NG[1:2, :] = dg1
    NG[3:4, :] = db1

    for p in range(NPARTS):
        ag_sent(p)

    act_home = pltpu.make_async_copy(C, act_out, sM.at[10])
    act_away = rc(C, act_out, sM.at[10], rM.at[10], dev_d)

    @pl.when(native)
    def _():
        act_home.start()

    @pl.when(away)
    def _():
        act_away.start()

    land = {p: p for p in range(NPARTS)}
    land[PG + 2] = PD + 1
    land[PG + 3] = PD
    land[PQ] = PG + 3
    land[PK] = PG + 2
    land[PO] = PG + 4
    land[PV] = PG + 5
    credits = {PD: [PD, PG + 3], PD + 1: [PG + 2], PD + 2: [PD + 2]}
    credits["mid"] = [PG, PG + 1, PG + 4, PG + 5, PQ, PK, PO, PV]

    def wland(p, zz, yy):
        if p == PD + 1:
            return LD.at[zz]
        return W.at[rows_of(zz, yy), pl.ds(cols[land[p]][0], cols[p][1])]

    def credit(k):
        @pl.when(native)
        def _():
            for p in credits[k]:
                pl.semaphore_signal(cred.at[p], inc=1, device_id=dev_x, device_id_type=MESH_ID)

    def x_block(p, d):
        zz = zof(d)
        yy = lax.rem(zz + p + 1, 2)
        return rc(blk(G, p, zz, yy), wland(p, zz, yy), sX.at[p], rX.at[p, d], dev_x)

    def y_block(p, d):
        return rc(blk(G, p, zof(d), 1 - y), Ly.at[zof(d), :, cslice(p)], sY.at[p], rY.at[p, d], dev_y)

    def y_arrival(p, d):
        return rc(blk(G, p, zof(d), y), Ly.at[zof(d), :, cslice(p)], sY.at[p], rY.at[p, d], dev_y)

    def z_block(p, d):
        return rc(blk(G, p, zof(d), y), Lz.at[d - 1, :, cslice(p)], sZ.at[p], rZ.at[p], dev_z(d))

    def x_final(p):
        return rc(blk(G, p, z, y), Lx.at[:, cslice(p)], sXF.at[p], rXF.at[p], dev_x)

    def out_copies(p):
        lo = pl.multiple_of(c * SH, 16)
        c0, n = cols[p]
        if p in (PQ, PK, PV):
            pieces = [(c0, n, gq_out.at[p])]
        elif p == PO:
            pieces = [(c0, n, go_out)]
        elif p < PD:
            j = p - PG
            pieces = [(c0 + i * GH, GH, ggu_out.at[i, :, pl.ds(j * GH, GH)]) for i in range(2)]
        else:
            pieces = [(c0, n, gd_out.at[:, pl.ds((p - PD) * CH, CH)])]
        return [
            pltpu.make_async_copy(F.at[pl.ds(lo, SH), pl.ds(a, m)], dst, sO.at[p])
            for a, m, dst in pieces
        ]

    def f_rows(core):
        return pl.ds(pl.multiple_of(core * SH, 16), SH)

    def f_send(p):
        part = F.at[f_rows(oc), cslice(p)]
        return rc(part, part, sF.at[p], rF.at[p], dev_c)

    def f_arrival(p):
        part = F.at[f_rows(c), cslice(p)]
        return rc(part, part, sF.at[p], rF.at[p], dev_c)

    def rs1(p):
        def gy(d, carry):
            when(crosses_first(p, zof(d), 1 - y), lambda: y_block(p, d).start())
            return carry
        lax.fori_loop(0, 4, gy, 0)

        @pl.when(away)
        def _():
            if p != PD + 1:
                pl.semaphore_wait(cred.at[p], 1)

            def go(d, carry):
                x_block(p, d).start()
                return carry
            lax.fori_loop(0, 4, go, 0)

    def rs1n(p, d):
        zz = zof(d)

        @pl.when(both(native, jnp.logical_not(crosses_first(p, zz, 1 - y))))
        def _():
            x_block(p, d).wait_recv()
            rows = rows_of(zz, 1 - y)
            G[rows, cslice(p)] = (G[rows, cslice(p)].astype(F32) + wland(p, zz, 1 - y)[...].astype(F32)).astype(BF)
            y_block(p, d).start()

    def rs2(p, i):
        d = lax.rem(i + 1, 4)
        zz = zof(d)
        rows = rows_of(zz, y)
        first = crosses_first(p, zz, y)

        def finish(total):
            G[rows, cslice(p)] = total.astype(BF)
            when(d > 0, lambda: z_block(p, d).start())

        @pl.when(both(native, jnp.logical_not(first)))
        def _():
            x_block(p, d).wait_recv()
            y_arrival(p, d).wait_recv()
            finish(G[rows, cslice(p)].astype(F32) + Ly[zz, :, cslice(p)].astype(F32) + wland(p, zz, y)[...].astype(F32))

        @pl.when(first)
        def _():
            y_arrival(p, d).wait_recv()
            finish(G[rows, cslice(p)].astype(F32) + Ly[zz, :, cslice(p)].astype(F32))

    def rs3(p):
        own_first = crosses_first(p, z, y)

        def total():
            three = Lz.at[:, :, cslice(p)]
            pltpu.make_async_copy(three, three, rZ.at[p]).wait()
            out = G[rows_of(z, y), cslice(p)].astype(F32)
            for k in range(3):
                out = out + Lz[k, :, cslice(p)].astype(F32)
            return out

        @pl.when(native)
        def _():
            F[:, cslice(p)] = total()

        @pl.when(both(away, own_first))
        def _():
            G[rows_of(z, y), cslice(p)] = total().astype(BF)
            x_final(p).start()

    def rs4(p):
        @pl.when(native)
        def _():
            @pl.when(crosses_first(p, z, y))
            def _():
                x_final(p).wait_recv()
                F[:, cslice(p)] = F[:, cslice(p)] + Lx[:, cslice(p)].astype(F32)
            f_send(p).start()

        when(away, lambda: f_arrival(p).wait_recv())
        for cp in out_copies(p):
            cp.start()

    def rs_sent(p):
        own_first = crosses_first(p, z, y)

        @pl.when(native)
        def _():
            wait_bytes(p, 4, sY.at[p])
            wait_bytes(p, 3, sZ.at[p])
            f_send(p).wait_send()

        @pl.when(away)
        def _():
            wait_bytes(p, 4, sX.at[p])
            wait_bytes(p, 2, sY.at[p])

            @pl.when(own_first)
            def _():
                wait_bytes(p, 1, sZ.at[p])
                x_final(p).wait_send()
            when(jnp.logical_not(own_first), lambda: wait_bytes(p, 2, sZ.at[p]))

        part = F.at[f_rows(c), cslice(p)]
        pltpu.make_async_copy(part, part, sO.at[p]).wait()

    kinds.update({"rs1": rs1, "rs1n": rs1n, "rs2": rs2, "rs3": rs3, "rs4": rs4})
    order = [PD + 1, PG + 2, PD, PG + 3, PD + 2, PG, PG + 1, PG + 4, PG + 5, PO, PV, PQ, PK]
    assert not queue
    for i in range(NPARTS + 9):
        for name, lag in (("rs1n", 1), ("rs2", 2), ("rs3", 5), ("rs4", 9)):
            if 0 <= i - lag < NPARTS:
                queue.append((name, order[i - lag]))

    def transpose_half(src, dst, first_row):
        def body(i):
            r = pl.multiple_of(first_row + i * TR, TR)
            dst[:, pl.ds(r, TR)] = src[pl.ds(r, TR), :].T
        loop(HALF // TR, body)

    transpose_half(M, DT, own_r)
    rc(M.at[oth_rows], M.at[oth_rows], sM.at[9], rM.at[9], dev_c).wait_recv()
    transpose_half(M, DT, oth_r)

    def back_chunk(j, *events):
        hc = pl.ds(j * CH, CH)

        def body(i):
            r = pl.multiple_of(i * TR, TR)
            rows = pl.ds(r, TR)
            dh = nn(M[rows, :], W[:, wcols(PD + j)]).astype(BF).astype(F32)
            gate = GT[rows, hc].astype(F32)
            up = UP[rows, hc].astype(F32)
            sg = sigmoid(gate)
            GT[rows, hc] = (dh * up * (sg * (1.0 + gate * (1.0 - sg)))).astype(BF)
            UP[rows, hc] = (dh * gate * sg).astype(BF)
        loop(LEN // TR, body, *events)

    WR = D // 4

    def weight_grad(left, pieces, *events):
        def body(i):
            r = pl.multiple_of(i * WR, 64)
            for right, a, n, c0 in pieces:
                G[pl.ds(r, WR), pl.ds(c0, n)] = nn(left[pl.ds(r, WR), :], right[:, pl.ds(a, n)]).astype(BF)
        loop(4, body, *events)

    def grads_down(j, *events):
        weight_grad(DT, [(H, j * CH, CH, cols[PD + j][0])], *events)

    def grads_gate_up(g, *events):
        c0 = cols[PG + g][0]
        weight_grad(MT, [(GT, g * GH, GH, c0), (UP, g * GH, GH, c0 + GH)], *events)

    def now(p):
        rs1(p)

    def take(name, p):
        queue.remove((name, p))
        queue.insert(0, (name, p))
        step()

    grads_down(1)
    now(PD + 1)
    back_chunk(1)
    credit(PD + 1)
    grads_gate_up(2)
    now(PG + 2)
    grads_gate_up(3)
    back_chunk(0, ("rs1n", PD + 1))
    credit(PD)
    grads_down(0)
    now(PD)
    grads_gate_up(0, ("rs1n", PG + 2))
    grads_gate_up(1, ("rs2", PD + 1))
    now(PG + 3)
    back_chunk(2, ("rs1n", PD))
    credit(PD + 2)
    grads_down(2, ("rs2", PG + 2))
    now(PD + 2)
    grads_gate_up(4, ("rs1n", PG + 3))
    grads_gate_up(5, ("rs2", PD))

    mid_terms = []
    for g in range(NG_PARTS):
        mid_terms.append((GT, g * GH, GH, cols[PG + g][0]))
        mid_terms.append((UP, g * GH, GH, cols[PG + g][0] + GH))
    part1.wait_send()
    partial(mid_terms, oth_r, to_x)
    part2 = core_send(X.at[oth_rows], R, 11)
    part2.start()

    def to_n2_add(r, acc):
        N2[pl.ds(r, TR), :] = N2[pl.ds(r, TR), :] + acc
    partial(mid_terms, own_r, to_n2_add)
    credit("mid")
    now(PG)
    d2.wait_send()
    part2.wait_recv()

    def norm1_back(i, carry):
        dg, db = carry
        r = pl.multiple_of(i * TN, TN)
        rows = pl.ds(r, TN)
        e = N2[rows, :] + R[rows, :].astype(F32)
        n = N1[rows, :]
        rs = RS1[rows, 0:1]
        eg = e * NV[0:1, :]
        m1 = jnp.sum(eg, axis=1, keepdims=True) * inv_d
        m2 = jnp.sum(eg * n, axis=1, keepdims=True) * inv_d
        d = rs * (eg - m1 - n * m2)
        N2[rows, :] = d
        M[pl.ds(own_r + r, TN), :] = d.astype(BF)
        return dg + jnp.sum(e * n, axis=0, keepdims=True), db + jnp.sum(e, axis=0, keepdims=True)

    dg0, db0 = lax.fori_loop(0, HALF // TN, norm1_back, (zero_row, zero_row))
    d1 = core_send(M.at[own_rows], M.at[own_rows], 12)
    d1.start()
    NG[0:1, :] = dg0
    NG[2:3, :] = db0
    ng = core_send(NG, NGR, 13)
    ng.start()
    rc(M.at[oth_rows], M.at[oth_rows], sM.at[12], rM.at[12], dev_c).wait_recv()
    transpose_into(M, DT, ("rs1n", PD + 2))
    ng.wait_recv()
    NGT[...] = jnp.zeros(NGT.shape, F32)
    NGT[0:8, :] = NG[...] + NGR[...]
    G[:, norm_cols] = NGT[...].T.astype(BF)

    def d_att(i):
        r = pl.multiple_of(i * TR, TR)
        rows = pl.ds(r, TR)
        da = nn(M[rows, :], W[:, wcols(PO, 0, HC)]).astype(BF)
        UP[rows, pl.ds(0, HC)] = da
        prod = da.astype(F32) * A[rows, :].astype(F32)
        acc = jnp.zeros((TR, 128), F32)
        for k in range(PAIRS):
            piece = prod[:, 128 * k : 128 * (k + 1)]
            d0 = jnp.sum(jnp.where(head0, piece, 0.0), axis=1, keepdims=True)
            dall = jnp.sum(piece, axis=1, keepdims=True)
            acc = jnp.where(lane == 2 * k, d0, jnp.where(lane == 2 * k + 1, dall - d0, acc))
        DEL[rows, :] = acc
    loop(LEN // TR, d_att, ("rs2", PG + 3))
    weight_grad(DT, [(A, 0, HC, cols[PO][0])])
    now(PG + 1)
    take("rs3", PD + 1)
    LST[...] = LSE[...].T[0:8, :]
    DLT[...] = DEL[...].T[0:8, :]

    def attend_back(k, *events):
        pair = slice(128 * k, 128 * (k + 1))
        DQT[...] = jnp.zeros(DQT.shape, F32)

        def body(i):
            r = pl.multiple_of(i * TR, TR)
            rows = pl.ds(r, TR)
            keys = K[rows, pair].astype(F32) * scale
            vals = V[rows, pair]
            qp = Q[:, pair]
            da = UP[:, pair]
            same = SEGC[rows, 0:1] == SEGR[0:1, :]
            dv, dk = [], []
            for s in range(2):
                h = 2 * k + s
                mine = head0 if s == 0 else jnp.logical_not(head0)
                km = jnp.where(mine, keys, 0.0)
                vm = jnp.where(mine, vals.astype(F32), 0.0).astype(BF)
                sc = nt(km.astype(BF), qp)
                pr = jnp.where(same, jnp.exp(sc - LST[h : h + 1, :]), 0.0)
                dp = nt(vm, da)
                ds = (pr * (dp - DLT[h : h + 1, :])).astype(BF)
                dv.append(nn(pr.astype(BF), da))
                dk.append(nn(ds, qp))
                DQT[...] = DQT[...] + nn(km.T.astype(BF), ds)
            GT[rows, 2 * HC + 128 * k : 2 * HC + 128 * (k + 1)] = jnp.where(head0, dv[0], dv[1]).astype(BF)
            GT[rows, HC + 128 * k : HC + 128 * (k + 1)] = unrot(jnp.where(head0, dk[0], dk[1]) * scale, r, TR).astype(BF)
        loop(LEN // TR, body, *events)

        def finish(i):
            r = pl.multiple_of(i * 128, 128)
            GT[pl.ds(r, 128), pair] = unrot(DQT[:, pl.ds(r, 128)].T, r, 128).astype(BF)
        loop(LEN // 128, finish)

    attend_back(0, ("rs1n", PG), ("rs2", PD + 2))
    take("rs3", PG + 2)
    now(PG + 4)
    attend_back(1, ("rs1n", PG + 1), ("rs2", PG))
    take("rs3", PD)
    now(PG + 5)
    attend_back(2, ("rs1n", PG + 4), ("rs2", PG + 1))
    take("rs3", PG + 3)
    now(PO)

    weight_grad(XT, [(GT, 2 * HC, HC, cols[PV][0])], ("rs1n", PG + 5))
    now(PV)
    weight_grad(XT, [(GT, 0, HC, cols[PQ][0])], ("rs2", PG + 4))
    now(PQ)
    weight_grad(XT, [(GT, HC, HC, cols[PK][0])], ("rs1n", PO))
    now(PK)

    in_terms = [(GT, 0, 3 * HC, 0)]
    part2.wait_send()
    partial(in_terms, oth_r, to_x)
    part3 = core_send(X.at[oth_rows], R, 14)
    part3.start()
    partial(in_terms, own_r, to_n2_add)

    @pl.when(native)
    def _():
        act_home.wait()

    @pl.when(away)
    def _():
        act_away.wait_send()

    part3.wait_recv()

    gtok_home = pltpu.make_async_copy(N2, gtok_out, sM.at[15])
    gtok_away = rc(C, GL, sM.at[15], rM.at[15], dev_d)

    def add_rows(i):
        r = pl.multiple_of(i * TN, TN)
        rows = pl.ds(r, TN)
        total = N2[rows, :] + R[rows, :].astype(F32)
        N2[rows, :] = total
        C[rows, :] = total.astype(BF)
    loop(HALF // TN, add_rows)

    @pl.when(native)
    def _():
        gtok_home.start()

    @pl.when(away)
    def _():
        gtok_away.start()

    while queue:
        step()

    @pl.when(away)
    def _():
        rc(C, GL, sM.at[15], rM.at[15], dev_d).wait_recv()
        N1[...] = GL[...].astype(F32)
        out = pltpu.make_async_copy(N1, gtok_out, sM.at[16])
        out.start()
        out.wait()
        gtok_away.wait_send()
        rc(C, act_out, sM.at[10], rM.at[10], dev_d).wait_recv()
        tok_away.wait_send()
        cot_away.wait_send()

    @pl.when(native)
    def _():
        gtok_home.wait()
        seg_send.wait_send()

    d1.wait_send()
    ng.wait_send()
    part3.wait_send()
    for p in range(NPARTS):
        rs_sent(p)


def on_device_fused(
    tokens, segments, qkv_weight, out_weight, gate_up_weight, down_weight, norm_gain, norm_shift, cotangent
):
    length, width = segments.shape[1], tokens.shape[1]
    half = tokens.shape[0]
    hc, fc = qkv_weight.shape[3], gate_up_weight.shape[3]
    sh = qkv_weight.shape[2]
    nc = 4 * hc + 128 + 3 * fc
    cosine, sine = rope_numpy(length)
    vm = pl.BlockSpec(memory_space=pltpu.VMEM)
    anyspec = pl.BlockSpec(memory_space=pl.ANY)
    V_ = pltpu.VMEM
    br = 2 * sh
    dma = pltpu.SemaphoreType.DMA
    scratch = [
        V_((width, nc), BF),
        V_((width, nc), BF),
        V_((NZ, br, nc), BF),
        V_((NZ - 1, br, nc), BF),
        V_((br, nc), BF),
        V_((br, nc), F32),
        V_((length, width), BF),
        V_((width, length), BF),
        V_((length, hc), BF),
        V_((length, hc), BF),
        V_((length, hc), BF),
        V_((length, hc), BF),
        V_((length, width), BF),
        V_((width, length), BF),
        V_((width, length), BF),
        V_((length, fc), BF),
        V_((length, fc), BF),
        V_((length, fc), BF),
        V_((half, width), BF),
        V_((half, width), BF),
        V_((half, width), F32),
        V_((half, width), F32),
        V_((half, 128), F32),
        V_((128, length), F32),
        V_((length, 128), F32),
        V_((8, length), F32),
        V_((length, 128), F32),
        V_((8, length), F32),
        V_((8, length), F32),
        V_((length, 128), F32),
        V_((8, width), F32),
        V_((8, width), F32),
        V_((8, width), F32),
        V_((128, width), F32),
        V_((half, width), BF),
        V_((NZ, br, fc // 3), BF),
        V_((sh, 128), BF),
        V_((8, sh), F32),
        dma((NPARTS,)), dma((NPARTS,)), dma((NPARTS,)), dma((NPARTS,)), dma((NPARTS,)), dma((NPARTS, 8)),
        dma((NPARTS,)), dma((NPARTS, 4)), dma((NPARTS,)), dma((NPARTS,)), dma((NPARTS,)), dma((NPARTS, 4)),
        dma((NPARTS,)), dma((NPARTS,)), dma((NPARTS,)), dma((NPARTS,)), dma((NPARTS,)),
        dma((17,)), dma((17,)),
        pltpu.SemaphoreType.REGULAR((NPARTS,)),
    ]
    act, gtok, gq, go, ggu, gd = pl.pallas_call(
        functools.partial(layer_kernel, (length, width, hc, fc)),
        out_shape=(
            jax.ShapeDtypeStruct((half, width), BF),
            jax.ShapeDtypeStruct((half, width), F32),
            jax.ShapeDtypeStruct((3, sh, hc), F32),
            jax.ShapeDtypeStruct((sh, hc + 128), F32),
            jax.ShapeDtypeStruct((2, sh, fc), F32),
            jax.ShapeDtypeStruct((sh, fc), F32),
        ),
        in_specs=[anyspec, anyspec, vm, vm, vm, anyspec, anyspec, anyspec, anyspec, vm, vm],
        out_specs=tuple([anyspec] * 6),
        scratch_shapes=scratch,
        compiler_params=pltpu.CompilerParams(
            collective_id=1, has_side_effects=True, vmem_limit_bytes=VMEM_LIMIT
        ),
        name="layer",
    )(
        tokens, cotangent, segments, jnp.asarray(cosine), jnp.asarray(sine),
        qkv_weight, jnp.swapaxes(out_weight, 1, 2), gate_up_weight, jnp.swapaxes(down_weight, 1, 2), norm_gain, norm_shift,
    )
    act, gtok, gq, out_t, ggu, down_t, gain, shift = pl.pallas_call(
        functools.partial(finish_kernel, hc),
        out_shape=(
            jax.ShapeDtypeStruct((half, width), BF),
            jax.ShapeDtypeStruct((half, width), F32),
            jax.ShapeDtypeStruct((1, 3, sh, hc), F32),
            jax.ShapeDtypeStruct((1, sh, hc), F32),
            jax.ShapeDtypeStruct((1, 2, sh, fc), F32),
            jax.ShapeDtypeStruct((1, sh, fc), F32),
            jax.ShapeDtypeStruct((1, 2, sh), F32),
            jax.ShapeDtypeStruct((1, 2, sh), F32),
        ),
        in_specs=[anyspec, anyspec, anyspec, vm, anyspec, anyspec],
        out_specs=tuple([vm] * 8),
        scratch_shapes=[dma((5,))],
        name="finish",
    )(act, gtok, gq, go, ggu, gd)
    return act, gtok, gq, jnp.swapaxes(out_t, 1, 2), ggu, jnp.swapaxes(down_t, 1, 2), gain, shift


def finish_kernel(
    hc, act, gtok, gq, go, ggu, gd, act_out, gtok_out, gq_out, out_out, ggu_out, down_out, gain_out, shift_out, sem
):
    copies = [
        pltpu.make_async_copy(gtok, gtok_out, sem.at[0]),
        pltpu.make_async_copy(act, act_out, sem.at[1]),
        pltpu.make_async_copy(ggu, ggu_out.at[0], sem.at[2]),
        pltpu.make_async_copy(gq, gq_out.at[0], sem.at[3]),
        pltpu.make_async_copy(gd, down_out.at[0], sem.at[4]),
    ]
    for cp in copies:
        cp.start()
    sh = go.shape[0]
    out_out[0] = go[:, 0:hc]
    norms = jnp.concatenate([go[:, hc : hc + 128], jnp.zeros((128 - sh, 128), F32)], axis=0).T[:, 0:sh]
    gain_out[0] = norms[0:2, :]
    shift_out[0] = norms[2:4, :]
    for cp in copies:
        cp.wait()


VMEM_LIMIT = 64 * 1024 * 1024


def solution(mesh):
    body = on_device_fused if dict(mesh.shape) == {"fsdp": 16, "tp": 2} else on_device
    placed = (
        P(("fsdp", "tp"), None),
        P("fsdp", None),
        P(None, None, "fsdp", "tp"),
        P(None, "tp", "fsdp"),
        P(None, None, "fsdp", "tp"),
        P(None, "tp", "fsdp"),
        P(None, None, "fsdp"),
        P(None, None, "fsdp"),
        P(("fsdp", "tp"), None),
    )
    return jax.shard_map(
        body,
        mesh=mesh,
        in_specs=placed,
        out_specs=(
            P(("fsdp", "tp"), None),
            P(("fsdp", "tp"), None),
            P(None, None, "fsdp", "tp"),
            P(None, "tp", "fsdp"),
            P(None, None, "fsdp", "tp"),
            P(None, "tp", "fsdp"),
            P(None, None, "fsdp"),
            P(None, None, "fsdp"),
        ),
        check_vma=False,
    )
```

```python
import functools

import jax
import jax.numpy as jnp
import numpy as np
from jax import lax
from jax.experimental import pallas as pl
from jax.experimental.pallas import tpu as pltpu
from jax.sharding import PartitionSpec as P

HEAD_DIM = 64


epsilon = 1e-05


def for_sending(value):

    def short(part):
        return part.astype(jnp.bfloat16) if part.dtype == jnp.float32 else part

    return jax.tree.map(short, value)


def rope_tables(length):
    half_dim = HEAD_DIM // 2
    inv_freq = 1000.0 ** (-jnp.arange(half_dim, dtype=jnp.float32) * 2.0 / HEAD_DIM)
    angles = jnp.arange(length, dtype=jnp.float32)[:, None] * inv_freq[None, :]
    cosine = jnp.concatenate([jnp.cos(angles), jnp.cos(angles)], axis=-1)[:, None, :]
    sine_table = jnp.concatenate([jnp.sin(angles), jnp.sin(angles)], axis=-1)[:, None, :]
    return (cosine, sine_table)


def rotate(values_in, cosine, sine_table):
    half_dim = values_in.shape[-1] // 2
    turned = jnp.concatenate([-values_in[..., half_dim:], values_in[..., :half_dim]], axis=-1)
    return values_in * cosine + turned * sine_table


def unrotate(grads_in, cosine, sine_table):
    half_dim = grads_in.shape[-1] // 2
    moved_part = grads_in * sine_table
    return grads_in * cosine + jnp.concatenate(
        [moved_part[..., half_dim:], -moved_part[..., :half_dim]], axis=-1
    )


def norm_rows(stream, scale_vec, shift_vec):
    row_mean = jnp.mean(stream, axis=-1, keepdims=True)
    centred = stream - row_mean
    row_var = jnp.mean(centred * centred, axis=-1, keepdims=True)
    return centred * lax.rsqrt(row_var + epsilon) * scale_vec + shift_vec


def swiglu(gate_pre, up_proj):
    return jax.nn.silu(gate_pre) * up_proj


def spread(stream_low):
    return lax.all_gather(stream_low, "tp", axis=0, tiled=True)


def collect(partial_rows):
    return lax.psum_scatter(
        partial_rows.astype(jnp.bfloat16), "tp", scatter_dimension=0, tiled=True
    ).astype(jnp.float32)


def spread_grads(grads_low):
    return lax.all_gather(grads_low, "tp", axis=0, tiled=True)


def collect_grads(partial_rows):
    return lax.psum_scatter(
        partial_rows.astype(jnp.bfloat16), "tp", scatter_dimension=0, tiled=True
    ).astype(jnp.float32)


def layer_shards(arrays, layer_index):
    return tuple((weight_part[layer_index] for weight_part in arrays))


def block_scores(query_blk, keys_seq, seg_blk, seg_seq):
    scores = jnp.einsum(
        "qhd,khd->hqk", query_blk, keys_seq, preferred_element_type=jnp.float32
    ) * HEAD_DIM ** (-0.5)
    joined = seg_blk[:, None] == seg_seq[None, :]
    return jnp.where(joined[None], scores, -1e30)


def attend_forward(queries, keys_rot, values, segments):
    seq_count, length = segments.shape
    block_rows = min(512, length)
    block_count = length // block_rows

    def attend_one_block(flat_index):
        sequence = flat_index // block_count
        row_start = flat_index % block_count * block_rows
        query_seq = lax.dynamic_index_in_dim(queries, sequence, 0, False)
        keys_seq = lax.dynamic_index_in_dim(keys_rot, sequence, 0, False)
        values_seq = lax.dynamic_index_in_dim(values, sequence, 0, False)
        seg_seq = lax.dynamic_index_in_dim(segments, sequence, 0, False)
        query_blk = lax.dynamic_slice_in_dim(query_seq, row_start, block_rows, 0)
        seg_blk = lax.dynamic_slice_in_dim(seg_seq, row_start, block_rows, 0)
        scores = block_scores(query_blk, keys_seq, seg_blk, seg_seq)
        row_max = jnp.max(scores, axis=-1, keepdims=True)
        exp_terms = jnp.exp(scores - row_max)
        row_total = jnp.sum(exp_terms, axis=-1, keepdims=True)
        probs_low = (exp_terms / row_total).astype(jnp.bfloat16)
        attended = jnp.einsum(
            "hqk,khd->qhd", probs_low, values_seq, preferred_element_type=jnp.float32
        )
        return (attended, row_max + jnp.log(row_total))

    attended, log_total = lax.map(
        attend_one_block, jnp.arange(seq_count * block_count, dtype=jnp.int32)
    )
    return (attended.reshape(seq_count * length, -1), log_total)


def attend_backward(queries, keys_rot, values, d_attended, log_total, segments):
    seq_count, length = segments.shape
    block_rows = min(512, length)
    block_count = length // block_rows
    scale_value = HEAD_DIM ** (-0.5)

    def one_sequence(sequence):
        query_seq = lax.dynamic_index_in_dim(queries, sequence, 0, False)
        keys_seq = lax.dynamic_index_in_dim(keys_rot, sequence, 0, False)
        values_seq = lax.dynamic_index_in_dim(values, sequence, 0, False)
        d_out_seq = lax.dynamic_index_in_dim(d_attended, sequence, 0, False)
        seg_seq = lax.dynamic_index_in_dim(segments, sequence, 0, False)

        def one_one_block(running, block_index):
            row_start = block_index * block_rows
            query_blk = lax.dynamic_slice_in_dim(query_seq, row_start, block_rows, 0)
            d_out_blk = lax.dynamic_slice_in_dim(d_out_seq, row_start, block_rows, 0)
            seg_blk = lax.dynamic_slice_in_dim(seg_seq, row_start, block_rows, 0)
            block_total = lax.dynamic_index_in_dim(
                log_total, sequence * block_count + block_index, 0, False
            )
            scores = block_scores(query_blk, keys_seq, seg_blk, seg_seq)
            attn_probs = jnp.exp(scores - block_total)
            probs_low = attn_probs.astype(jnp.bfloat16)
            d_probs = jnp.einsum(
                "qhd,khd->hqk", d_out_blk, values_seq, preferred_element_type=jnp.float32
            )
            inner_sum = jnp.sum(attn_probs * d_probs, axis=-1, keepdims=True)
            d_scores = (attn_probs * (d_probs - inner_sum)).astype(jnp.bfloat16)
            d_query = (
                jnp.einsum("hqk,khd->qhd", d_scores, keys_seq, preferred_element_type=jnp.float32)
                * scale_value
            )
            d_key = (
                running[0]
                + jnp.einsum(
                    "hqk,qhd->khd", d_scores, query_blk, preferred_element_type=jnp.float32
                )
                * scale_value
            )
            d_value = running[1] + jnp.einsum(
                "hqk,qhd->khd", probs_low, d_out_blk, preferred_element_type=jnp.float32
            )
            return ((d_key, d_value), d_query)

        zero_keys = jnp.zeros(keys_seq.shape, jnp.float32)
        (d_keys, d_values), d_queries = lax.scan(
            one_one_block, (zero_keys, zero_keys), jnp.arange(block_count, dtype=jnp.int32)
        )
        return (d_queries.reshape(keys_seq.shape), d_keys, d_values)

    return lax.map(one_sequence, jnp.arange(seq_count, dtype=jnp.int32))


def layer_forward(stream, segments, weights, tables):
    qkv_w, out_w, gate_up_w, down_w, gain_rows, shift_rows = weights
    cosine, sine_table = tables
    seq_count, length = segments.shape
    head_count = qkv_w.shape[2] // HEAD_DIM
    shaped = (seq_count, length, head_count, HEAD_DIM)
    gain_vals = gain_rows.astype(jnp.float32)
    shift_vals = shift_rows.astype(jnp.float32)
    inputs = spread(stream.astype(jnp.bfloat16))
    query_pre = jnp.dot(inputs, qkv_w[0], preferred_element_type=jnp.float32).reshape(shaped)
    key_pre = jnp.dot(inputs, qkv_w[1], preferred_element_type=jnp.float32).reshape(shaped)
    queries = rotate(query_pre, cosine, sine_table).astype(jnp.bfloat16)
    keys_rot = rotate(key_pre, cosine, sine_table).astype(jnp.bfloat16)
    values = (
        jnp.dot(inputs, qkv_w[2], preferred_element_type=jnp.float32)
        .astype(jnp.bfloat16)
        .reshape(shaped)
    )
    attended, log_total = attend_forward(queries, keys_rot, values, segments)
    attended_low = attended.astype(jnp.bfloat16)
    branch = collect(jnp.dot(attended_low, out_w, preferred_element_type=jnp.float32))
    mixed = stream + branch
    first_norm = norm_rows(mixed, gain_vals[0], shift_vals[0])
    middle = spread(first_norm.astype(jnp.bfloat16))
    gate_pre = jnp.dot(middle, gate_up_w[0], preferred_element_type=jnp.float32)
    up_proj = jnp.dot(middle, gate_up_w[1], preferred_element_type=jnp.float32)
    hidden = swiglu(gate_pre, up_proj).astype(jnp.bfloat16)
    branch_two = collect(jnp.dot(hidden, down_w, preferred_element_type=jnp.float32))
    second_in = first_norm + branch_two
    saved_state = (
        inputs,
        queries,
        keys_rot,
        values,
        log_total,
        attended_low,
        mixed,
        middle,
        gate_pre,
        up_proj,
        hidden,
        second_in,
    )
    return (norm_rows(second_in, gain_vals[1], shift_vals[1]), saved_state)


def layer_backward(grad_out, saved_state, segments, weights, tables):
    qkv_w, out_w, gate_up_w, down_w, gain_rows, shift_rows = weights
    (
        inputs,
        queries,
        keys_rot,
        values,
        log_total,
        attended_low,
        mixed,
        middle,
        gate_pre,
        up_proj,
        hidden,
        second_in,
    ) = saved_state
    cosine, sine_table = tables
    gain_vals = gain_rows.astype(jnp.float32)
    shift_vals = shift_rows.astype(jnp.float32)
    unused_two, norm_two_back = jax.vjp(norm_rows, second_in, gain_vals[1], shift_vals[1])
    d_second, d_gain_two, d_shift_two = norm_two_back(grad_out)
    d_branch_two = spread_grads(d_second.astype(jnp.bfloat16))
    grad_down = jnp.einsum("rf,rd->fd", hidden, d_branch_two, preferred_element_type=jnp.float32)
    d_hidden_low = jnp.einsum(
        "rd,fd->rf", d_branch_two, down_w, preferred_element_type=jnp.float32
    ).astype(jnp.bfloat16)
    d_hidden = lax.optimization_barrier(d_hidden_low).astype(jnp.float32)
    unused_swish, swish_back = jax.vjp(swiglu, gate_pre, up_proj)
    d_gate, d_up = swish_back(d_hidden)
    d_gate_low = d_gate.astype(jnp.bfloat16)
    d_up_low = d_up.astype(jnp.bfloat16)
    grad_gate_up = jnp.stack(
        [
            jnp.einsum("rd,rf->df", middle, d_gate_low, preferred_element_type=jnp.float32),
            jnp.einsum("rd,rf->df", middle, d_up_low, preferred_element_type=jnp.float32),
        ]
    )
    d_middle = jnp.einsum("rf,df->rd", d_gate_low, gate_up_w[0], preferred_element_type=jnp.float32)
    d_middle = d_middle + jnp.einsum(
        "rf,df->rd", d_up_low, gate_up_w[1], preferred_element_type=jnp.float32
    )
    d_first = d_second + collect_grads(d_middle)
    unused_one, norm_one_back = jax.vjp(norm_rows, mixed, gain_vals[0], shift_vals[0])
    d_mixed, d_gain_one, d_shift_one = norm_one_back(d_first)
    d_branch = spread_grads(d_mixed.astype(jnp.bfloat16))
    grad_out_w = jnp.einsum("rc,rd->cd", attended_low, d_branch, preferred_element_type=jnp.float32)
    d_attended = (
        jnp.einsum("rd,cd->rc", d_branch, out_w, preferred_element_type=jnp.float32)
        .astype(jnp.bfloat16)
        .reshape(queries.shape)
    )
    d_queries, d_keys, d_values = attend_backward(
        queries, keys_rot, values, d_attended, log_total, segments
    )
    flat_shape = (-1, queries.shape[2] * queries.shape[3])
    d_query_low = unrotate(d_queries, cosine, sine_table).astype(jnp.bfloat16).reshape(flat_shape)
    d_key_low = unrotate(d_keys, cosine, sine_table).astype(jnp.bfloat16).reshape(flat_shape)
    d_value_low = d_values.astype(jnp.bfloat16).reshape(flat_shape)
    grad_parts = (d_query_low, d_key_low, d_value_low)
    grad_qkv = jnp.stack(
        [
            jnp.einsum("rd,rc->dc", inputs, grad_part, preferred_element_type=jnp.float32)
            for grad_part in grad_parts
        ]
    )
    d_inputs = jnp.einsum("rc,dc->rd", d_query_low, qkv_w[0], preferred_element_type=jnp.float32)
    d_inputs = d_inputs + jnp.einsum(
        "rc,dc->rd", d_key_low, qkv_w[1], preferred_element_type=jnp.float32
    )
    d_inputs = d_inputs + jnp.einsum(
        "rc,dc->rd", d_value_low, qkv_w[2], preferred_element_type=jnp.float32
    )
    d_stream = d_mixed + collect_grads(d_inputs)
    weight_grads = (
        grad_qkv,
        grad_out_w,
        grad_gate_up,
        grad_down,
        jnp.stack([d_gain_one, d_gain_two]),
        jnp.stack([d_shift_one, d_shift_two]),
    )
    return (d_stream, weight_grads)


def on_device(
    tokens,
    segments,
    qkv_weight,
    out_weight,
    gate_up_weight,
    down_weight,
    norm_gain,
    norm_shift,
    cotangent,
):
    arrays = (qkv_weight, out_weight, gate_up_weight, down_weight, norm_gain, norm_shift)
    layer_total = qkv_weight.shape[0]
    tables = rope_tables(segments.shape[1])
    stream = tokens.astype(jnp.float32)
    kept_weights = []
    layer_index = 0
    weights = lax.all_gather(
        for_sending(layer_shards(arrays, layer_index)), "fsdp", axis=1, tiled=True
    )
    stream, saved_state = layer_forward(stream, segments, weights, tables)
    kept_weights.append(weights)
    saved_states = [saved_state]
    activations = stream.astype(jnp.bfloat16)
    grad_stream = cotangent.astype(jnp.float32)
    grad_layers = [None] * layer_total
    for layer_index in reversed(range(layer_total)):
        weights = lax.all_gather(
            for_sending(layer_shards(arrays, layer_index)), "fsdp", axis=1, tiled=True
        )
        grad_stream, weight_grads = layer_backward(
            grad_stream, saved_states[layer_index], segments, weights, tables
        )
        grad_layers[layer_index] = (
            lax.psum_scatter(weight_grads[0], "fsdp", scatter_dimension=1, tiled=True),
            lax.psum_scatter(weight_grads[1], "fsdp", scatter_dimension=1, tiled=True),
            lax.psum_scatter(weight_grads[2], "fsdp", scatter_dimension=1, tiled=True),
            lax.psum_scatter(weight_grads[3], "fsdp", scatter_dimension=1, tiled=True),
            lax.psum_scatter(weight_grads[4], "fsdp", scatter_dimension=1, tiled=True),
            lax.psum_scatter(weight_grads[5], "fsdp", scatter_dimension=1, tiled=True),
        )
    stacked = [jnp.stack([grad_layers[0][member]]) for member in range(6)]
    gain_sum, shift_sum = lax.psum((stacked[4], stacked[5]), "tp")
    return (
        activations,
        grad_stream,
        stacked[0],
        stacked[1],
        stacked[2],
        stacked[3],
        gain_sum,
        shift_sum,
    )


MESH_ID = pl.DeviceIdType.MESH
BF = jnp.bfloat16
F32 = jnp.float32
NZ, NY = 4, 2
PQ, PK, PV, PO, PG = range(5)
NG_PARTS = 6
PD = PG + NG_PARTS
NPARTS = PD + 3
PAIRS = 3
NEG = -1e30


def nt(a, b):
    return lax.dot_general(a, b, (((1,), (1,)), ((), ())), preferred_element_type=F32)


def nn(a, b):
    return jnp.dot(a, b, preferred_element_type=F32)


def rope_numpy(length):
    half = HEAD_DIM // 2
    inv = 1000.0 ** (-np.arange(half, dtype=np.float64) * 2.0 / HEAD_DIM)
    angles = np.arange(length, dtype=np.float64)[:, None] * inv[None, :]
    cosine, sine = np.cos(angles), np.sin(angles)
    cos_rows = np.concatenate([cosine, cosine, cosine, cosine], axis=1)
    sin_rows = np.concatenate([-sine, sine, -sine, sine], axis=1)
    return cos_rows.astype(np.float32), sin_rows.astype(np.float32)


def layer_kernel(
    dims,
    tok_ref, cot_ref, seg_ref, cos_in, sin_in, qkv_in, out_ref, gu_in, down_ref, gain_ref, shift_ref,
    act_out, gtok_out, gq_out, go_out, ggu_out, gd_out,
    W, G, Ly, Lz, Lx, F, X, XT, Q, K, V, A, M, MT, DT, GT, UP, H, R, C, N1, N2, RS1,
    DQT, LSE, LST, DEL, DLT, SEGR, SEGC, NV, NG, NGR, NGT, GL, LD, OWN_N, N8, cos_ref, sin_ref,
    sLC, sCR, rCR, sA, sB, rB, sY, rY, sZ, rZ, sX, rX, sXF, rXF, sF, rF, sO, sM, rM, cred,
):
    LEN, D, HC, FC = dims
    HALF = LEN // 2
    SH = D // 16
    BR = 2 * SH
    CH = FC // 3
    GH = FC // NG_PARTS
    OW = HC + 128
    cols = {}
    at = 0
    for p in range(NPARTS):
        n = HC if p in (PQ, PK, PV) else OW if p == PO else 2 * GH if p < PD else CH
        cols[p] = (at, n)
        at += n

    f = lax.axis_index("fsdp")
    t = lax.axis_index("tp")
    c = lax.rem(f, 2)
    y = lax.rem(f // 2, 2)
    z = f // 4
    oc = 1 - c
    native = c == t
    away = c != t
    dev_x = (f, 1 - t)
    dev_y = ((z * 2 + (1 - y)) * 2 + c, t)
    dev_c = ((z * 2 + y) * 2 + oc, t)
    dev_d = ((z * 2 + y) * 2 + oc, 1 - t)

    def zof(d):
        return lax.rem(z + d, NZ)

    def dev_z(d):
        return ((zof(d) * 2 + y) * 2 + c, t)

    def rows_of(zz, yy):
        return pl.ds(pl.multiple_of((zz * 2 + yy) * BR, 16), BR)

    def cslice(p):
        return pl.ds(cols[p][0], cols[p][1])

    def blk(ref, p, zz, yy):
        return ref.at[rows_of(zz, yy), cslice(p)]

    def bid(zz, yy):
        return zz * 2 + yy

    def crosses_first(p, zz, yy):
        return lax.rem(zz + yy + p, 2) == 0

    def last_i(p, zz, yy):
        return (lax.rem(zz + 2 * yy + 3 * p, 7) // 3 + 1) // 2

    def ag_first(p, zz, yy):
        return last_i(p, zz, yy) == 0

    def both(*conds):
        out = conds[0]
        for cond in conds[1:]:
            out = jnp.logical_and(out, cond)
        return out

    def when(cond, fn):
        pl.when(cond)(fn)

    def rc(src, dst, ss, rs, dev):
        return pltpu.make_async_remote_copy(
            src_ref=src, dst_ref=dst, send_sem=ss, recv_sem=rs, device_id=dev, device_id_type=MESH_ID
        )

    def wait_bytes(p, blocks, sem):
        ref = Ly.at[0, :, pl.ds(0, blocks * cols[p][1])]
        pltpu.make_async_copy(ref, ref, sem).wait()

    own_r = pl.multiple_of(c * HALF, HALF)
    oth_r = pl.multiple_of(oc * HALF, HALF)
    own_rows = pl.ds(own_r, HALF)
    oth_rows = pl.ds(oth_r, HALF)

    bar = pltpu.get_barrier_semaphore()
    partners = [dev_x, dev_y, dev_c, dev_d, dev_z(1), dev_z(2), dev_z(3)]
    for dev in partners:
        pl.semaphore_signal(bar, inc=1, device_id=dev, device_id_type=MESH_ID)
    pl.semaphore_wait(bar, len(partners))

    def shard_pieces(p):
        c0, n = cols[p]
        if p in (PQ, PK, PV):
            return [(qkv_in.at[0, p], c0, n)]
        if p == PO:
            return [(out_ref.at[0], c0, HC), (OWN_N, c0 + HC, 128)]
        if p < PD:
            j = p - PG
            return [(gu_in.at[0, i, :, pl.ds(j * GH, GH)], c0 + i * GH, GH) for i in range(2)]
        j = p - PD
        return [(down_ref.at[0, :, pl.ds(j * CH, CH)], c0, CH)]

    shard_rows = pl.ds(pl.multiple_of((z * 2 + y) * BR + c * SH, 16), SH)
    oshard_rows = pl.ds(pl.multiple_of((z * 2 + y) * BR + oc * SH, 16), SH)

    def start_shards(p):
        @pl.when(native)
        def _():
            for src, c0, n in shard_pieces(p):
                pltpu.make_async_copy(src, W.at[shard_rows, pl.ds(c0, n)], sLC.at[p]).start()

        @pl.when(away)
        def _():
            for src, c0, n in shard_pieces(p):
                rc(src, W.at[shard_rows, pl.ds(c0, n)], sCR.at[p], rCR.at[p], dev_c).start()

    def own_whole(p):
        return W.at[shard_rows, cslice(p)]

    tok_home = pltpu.make_async_copy(tok_ref, X.at[own_rows], sM.at[2])
    tok_core = rc(tok_ref, X.at[own_rows], sM.at[3], rM.at[3], dev_c)
    tok_away = rc(tok_ref, X.at[oth_rows], sM.at[4], rM.at[4], dev_d)
    tok_pass = rc(X.at[own_rows], X.at[own_rows], sM.at[3], rM.at[3], dev_c)
    seg_send = rc(SEGR, SEGR, sM.at[1], rM.at[1], dev_c)
    cot_home = pltpu.make_async_copy(cot_ref, C, sM.at[5])
    cot_away = rc(cot_ref, C, sM.at[5], rM.at[5], dev_d)

    turns = [
        pltpu.make_async_copy(cos_in, cos_ref, sM.at[17]),
        pltpu.make_async_copy(sin_in, sin_ref, sM.at[18]),
    ]
    start_shards(PQ)
    start_shards(PK)
    for cp in turns:
        cp.start()

    @pl.when(native)
    def _():
        tok_home.start()
        tok_core.start()
        cot_home.start()
        SEGR[...] = jnp.broadcast_to(seg_ref[...].astype(F32), SEGR.shape)
        seg_send.start()

    @pl.when(away)
    def _():
        tok_away.start()
        cot_away.start()

    for p in range(2, NPARTS):
        if p != PO:
            start_shards(p)

    def ag_copy(p, zz, yy, dev, sem):
        b = blk(W, p, zz, yy)
        return rc(b, b, sem.at[p], rB.at[p, bid(zz, yy)], dev)

    def got(p, zz, yy):
        b = blk(W, p, zz, yy)
        rc(b, b, sA.at[p], rB.at[p, bid(zz, yy)], dev_x).wait_recv()

    def ag1(p):
        def spread_own():
            for d in (2, 1, 3):
                ag_copy(p, z, y, dev_z(d), sA).start()
            ag_copy(p, z, y, dev_y, sA).start()

        @pl.when(native)
        def _():
            pltpu.make_async_copy(own_whole(p), own_whole(p), sLC.at[p]).wait()
            o = W.at[oshard_rows, cslice(p)]
            rc(o, o, sCR.at[p], rCR.at[p], dev_c).wait_recv()
            ag_copy(p, z, y, dev_x, sA).start()
            spread_own()

        @pl.when(both(away, ag_first(p, z, y)))
        def _():
            got(p, z, y)
            spread_own()

    def ag2(p, d):
        zz = zof(d)
        first = ag_first(p, zz, y)

        def work():
            got(p, zz, y)
            ag_copy(p, zz, y, dev_y, sB).start()

            @pl.when(jnp.logical_not(first))
            def _():
                ag_copy(p, zz, y, dev_x, sB).start()

        when(both(d > 0, jnp.logical_or(native, first)), work)

    def ag3(p, d):
        zz = zof(d)
        first = ag_first(p, zz, 1 - y)

        @pl.when(jnp.logical_or(native, first))
        def _():
            got(p, zz, 1 - y)

            @pl.when(jnp.logical_not(first))
            def _():
                ag_copy(p, zz, 1 - y, dev_x, sB).start()

    def ag4(p, d):
        zz = zof(d)
        for yy in (y, 1 - y):
            when(both(away, jnp.logical_not(ag_first(p, zz, yy))), functools.partial(got, p, zz, yy))

    def ag_sent(p):
        own_first = ag_first(p, z, y)
        when(native, lambda: wait_bytes(p, 5, sA.at[p]))
        when(both(away, own_first), lambda: wait_bytes(p, 4, sA.at[p]))
        nat = 1 - lax.rem(c + t, 2)
        count = 0
        for d in range(4):
            if d:
                mine = last_i(p, zof(d), y)
                count = count + nat * (1 + mine) + (1 - nat) * (1 - mine)
            count = count + nat * last_i(p, zof(d), 1 - y)
        for n in range(1, 11):
            when(count == n, functools.partial(wait_bytes, p, n, sB.at[p]))

        @pl.when(away)
        def _():
            pltpu.make_async_copy(own_whole(p), own_whole(p), sCR.at[p]).wait()

    def loop(n, body, *events):
        for ev in events:
            assert ev in queue and n == 4
            queue.remove(ev)

        def go(i, carry):
            body(i)
            for name, p in events:
                kinds[name](p, i)
            return carry
        lax.fori_loop(0, n, go, 0)

    queue = []
    for i in range(-2, NPARTS + 2):
        for name, lag in (("ag1", -2), ("ag2", 0), ("ag3", 1), ("ag4", 2)):
            if 0 <= i - lag < NPARTS:
                queue.append((name, i - lag))
    kinds = {"ag1": ag1, "ag2": ag2, "ag3": ag3, "ag4": ag4}
    whole = ("ag1", "rs1", "rs3", "rs4")

    def step():
        name, p = queue.pop(0)
        if name in whole:
            kinds[name](p)
        else:
            def go(i, carry):
                kinds[name](p, i)
                return carry
            lax.fori_loop(0, 4, go, 0)

    def until(name, p):
        while (name, p) in queue:
            step()

    def ready(p):
        until("ag3", p)
        if ("ag4", p) in queue:
            queue.remove(("ag4", p))
            queue.insert(0, ("ag4", p))
            step()

    lane = lax.broadcasted_iota(jnp.int32, (1, 128), 1)
    low_half = lax.rem(lane, HEAD_DIM) < HEAD_DIM // 2
    head0 = lane < HEAD_DIM

    def swap(v):
        return jnp.where(low_half, pltpu.roll(v, 128 - HEAD_DIM // 2, 1), pltpu.roll(v, HEAD_DIM // 2, 1))

    def rot(v, r, n):
        return v * cos_ref[pl.ds(r, n), :] + swap(v) * sin_ref[pl.ds(r, n), :]

    def unrot(v, r, n):
        return v * cos_ref[pl.ds(r, n), :] - swap(v) * sin_ref[pl.ds(r, n), :]

    def wcols(p, a=0, n=None):
        c0, m = cols[p]
        return pl.ds(c0 + a, m if n is None else n)

    TR = 256

    def transpose_into(src, dst, *events):
        def body(i):
            r = pl.multiple_of(i * TR, TR)
            dst[:, pl.ds(r, TR)] = src[pl.ds(r, TR), :].T
        loop(LEN // TR, body, *events)

    def core_send(src, dst, k):
        return rc(src, dst, sM.at[k], rM.at[k], dev_c)

    until("ag1", PK)

    eye = (
        lax.broadcasted_iota(jnp.int32, (SH, SH), 0) == lax.broadcasted_iota(jnp.int32, (SH, SH), 1)
    ).astype(BF)
    N8[...] = jnp.zeros(N8.shape, F32)
    N8[0:2, :] = gain_ref[0].astype(F32)
    N8[2:4, :] = shift_ref[0].astype(F32)
    OWN_N[...] = jnp.zeros(OWN_N.shape, BF)
    OWN_N[:, 0:8] = nt(eye, N8[...].astype(BF)).astype(BF)
    start_shards(PO)

    @pl.when(native)
    def _():
        tok_home.wait()

    @pl.when(away)
    def _():
        rc(SEGR, SEGR, sM.at[1], rM.at[1], dev_c).wait_recv()
    until("ag2", PQ)

    @pl.when(away)
    def _():
        rc(tok_ref, X.at[own_rows], sM.at[4], rM.at[4], dev_d).wait_recv()
        tok_pass.start()
    until("ag3", PQ)
    rc(X.at[oth_rows], X.at[oth_rows], sM.at[3], rM.at[3], dev_c).wait_recv()

    def seg_cols(i):
        r = pl.multiple_of(i * 128, 128)
        SEGC[pl.ds(r, 128), :] = jnp.broadcast_to(SEGR[0:1, pl.ds(r, 128)], (128, 128)).T
    loop(LEN // 128, seg_cols)

    def project(p, dst, turn, *events):
        def body(i):
            r = pl.multiple_of(i * TR, TR)
            v = nn(X[pl.ds(r, TR), :], W[:, wcols(p)])
            for k in range(PAIRS):
                part = v[:, 128 * k : 128 * (k + 1)]
                if turn:
                    part = rot(part, r, TR)
                dst[pl.ds(r, TR), 128 * k : 128 * (k + 1)] = part.astype(BF)
        loop(LEN // TR, body, *events)

    transpose_into(X, XT)
    for cp in turns:
        cp.wait()
    ready(PQ)
    project(PQ, Q, True)
    ready(PK)
    project(PK, K, True)
    ready(PV)
    project(PV, V, False)

    scale = HEAD_DIM ** -0.5
    LSE[...] = jnp.zeros(LSE.shape, F32)

    def attend_pair(k, *events):
        def body(i):
            r = pl.multiple_of(i * TR, TR)
            rows = pl.ds(r, TR)
            pair = slice(128 * k, 128 * (k + 1))
            q = Q[rows, pair]
            keys = K[:, pair]
            vals = V[:, pair]
            same = SEGC[rows, 0:1] == SEGR[0:1, :]
            outs, lses = [], []
            for s in range(2):
                mine = head0 if s == 0 else jnp.logical_not(head0)
                qm = jnp.where(mine, q.astype(F32) * scale, 0.0).astype(BF)
                sc = jnp.where(same, nt(qm, keys), NEG)
                top = jnp.max(sc, axis=1, keepdims=True)
                e = jnp.exp(sc - top)
                total = jnp.sum(e, axis=1, keepdims=True)
                outs.append(nn(e.astype(BF), vals) / total)
                lses.append(top + jnp.log(total))
            A[rows, pair] = jnp.where(head0, outs[0], outs[1]).astype(BF)
            LSE[rows, :] = jnp.where(lane == 2 * k, lses[0], jnp.where(lane == 2 * k + 1, lses[1], LSE[rows, :]))
        loop(LEN // TR, body, *events)

    for k in range(PAIRS):
        until("ag1", PO + 3 + k)
        attend_pair(k, ("ag2", PO + 1 + k), ("ag3", PO + k))

    ready(PO)
    norm_cols = pl.ds(cols[PO][0] + HC, 128)
    NV[...] = W[:, norm_cols].astype(F32).T[0:8, :]

    @pl.when(native)
    def _():
        tok_core.wait_send()

    @pl.when(away)
    def _():
        tok_pass.wait_send()

    def partial(lhs, dst_rows_at, finish):
        def body(i):
            r = pl.multiple_of(i * TR, TR)
            acc = None
            for ref, a, n, w0 in lhs:
                term = nt(ref[pl.ds(dst_rows_at + r, TR), pl.ds(a, n)], W[:, pl.ds(w0, n)])
                acc = term if acc is None else acc + term
            finish(r, acc)
        loop(HALF // TR, body)

    def to_x(r, acc):
        X[pl.ds(oth_r + r, TR), :] = acc.astype(BF)

    def to_n2(r, acc):
        N2[pl.ds(r, TR), :] = acc

    out_terms = [(A, 0, HC, cols[PO][0])]
    partial(out_terms, oth_r, to_x)
    part0 = core_send(X.at[oth_rows], R, 6)
    part0.start()
    partial(out_terms, own_r, to_n2)
    until("ag1", PG + 5)
    part0.wait_recv()

    TN = 64
    inv_d = 1.0 / D

    def norm1(i):
        r = pl.multiple_of(i * TN, TN)
        rows = pl.ds(r, TN)
        mix = X[pl.ds(own_r + r, TN), :].astype(F32) + N2[rows, :] + R[rows, :].astype(F32)
        mean = jnp.sum(mix, axis=1, keepdims=True) * inv_d
        cen = mix - mean
        var = jnp.sum(cen * cen, axis=1, keepdims=True) * inv_d
        rs = lax.rsqrt(var + epsilon)
        n = cen * rs
        N1[rows, :] = n
        RS1[rows, :] = jnp.broadcast_to(rs, (TN, 128))
        M[pl.ds(own_r + r, TN), :] = (n * NV[0:1, :] + NV[2:3, :]).astype(BF)
    loop(HALF // TN, norm1)
    mid = core_send(M.at[own_rows], M.at[own_rows], 7)
    mid.start()
    until("ag2", PG + 3)
    rc(M.at[oth_rows], M.at[oth_rows], sM.at[7], rM.at[7], dev_c).wait_recv()

    def sigmoid(v):
        return 1.0 / (1.0 + jnp.exp(-v))

    def hidden_chunk(g, *events):
        def body(i):
            r = pl.multiple_of(i * TR, TR)
            rows = pl.ds(r, TR)
            pre = nn(M[rows, :], W[:, wcols(PG + g)])
            gate, up = pre[:, :GH], pre[:, GH:]
            GT[rows, pl.ds(g * GH, GH)] = gate.astype(BF)
            UP[rows, pl.ds(g * GH, GH)] = up.astype(BF)
            H[rows, pl.ds(g * GH, GH)] = (gate * sigmoid(gate) * up).astype(BF)
        loop(LEN // TR, body, *events)

    for g in range(NG_PARTS):
        ready(PG + g)
        if g == 1:
            transpose_into(M, MT)
        hidden_chunk(g)
    for p in range(PD, NPARTS):
        ready(p)
    part0.wait_send()
    mid.wait_send()

    down_terms = [(H, j * CH, CH, cols[PD + j][0]) for j in range(3)]
    partial(down_terms, oth_r, to_x)
    part1 = core_send(X.at[oth_rows], R, 8)
    part1.start()
    partial(down_terms, own_r, to_n2)

    @pl.when(native)
    def _():
        cot_home.wait()

    @pl.when(away)
    def _():
        rc(cot_ref, C, sM.at[5], rM.at[5], dev_d).wait_recv()

    part1.wait_recv()

    def norm2(i, carry):
        dg, db = carry
        r = pl.multiple_of(i * TN, TN)
        rows = pl.ds(r, TN)
        first = N1[rows, :] * NV[0:1, :] + NV[2:3, :]
        v = first + N2[rows, :] + R[rows, :].astype(F32)
        mean = jnp.sum(v, axis=1, keepdims=True) * inv_d
        cen = v - mean
        var = jnp.sum(cen * cen, axis=1, keepdims=True) * inv_d
        rs = lax.rsqrt(var + epsilon)
        n = cen * rs
        e = C[rows, :].astype(F32)
        C[rows, :] = (n * NV[1:2, :] + NV[3:4, :]).astype(BF)
        eg = e * NV[1:2, :]
        m1 = jnp.sum(eg, axis=1, keepdims=True) * inv_d
        m2 = jnp.sum(eg * n, axis=1, keepdims=True) * inv_d
        d = rs * (eg - m1 - n * m2)
        N2[rows, :] = d
        M[pl.ds(own_r + r, TN), :] = d.astype(BF)
        return dg + jnp.sum(e * n, axis=0, keepdims=True), db + jnp.sum(e, axis=0, keepdims=True)

    zero_row = jnp.zeros((1, D), F32)
    dg1, db1 = lax.fori_loop(0, HALF // TN, norm2, (zero_row, zero_row))
    d2 = core_send(M.at[own_rows], M.at[own_rows], 9)
    d2.start()
    NG[...] = jnp.zeros(NG.shape, F32)
    NG[1:2, :] = dg1
    NG[3:4, :] = db1

    for p in range(NPARTS):
        ag_sent(p)

    act_home = pltpu.make_async_copy(C, act_out, sM.at[10])
    act_away = rc(C, act_out, sM.at[10], rM.at[10], dev_d)

    @pl.when(native)
    def _():
        act_home.start()

    @pl.when(away)
    def _():
        act_away.start()

    land = {p: p for p in range(NPARTS)}
    land[PG + 2] = PD + 1
    land[PG + 3] = PD
    land[PQ] = PG + 3
    land[PK] = PG + 2
    land[PO] = PG + 4
    land[PV] = PG + 5
    credits = {PD: [PD, PG + 3], PD + 1: [PG + 2], PD + 2: [PD + 2]}
    credits["mid"] = [PG, PG + 1, PG + 4, PG + 5, PQ, PK, PO, PV]

    def wland(p, zz, yy):
        if p == PD + 1:
            return LD.at[zz]
        return W.at[rows_of(zz, yy), pl.ds(cols[land[p]][0], cols[p][1])]

    def credit(k):
        @pl.when(native)
        def _():
            for p in credits[k]:
                pl.semaphore_signal(cred.at[p], inc=1, device_id=dev_x, device_id_type=MESH_ID)

    def x_block(p, d):
        zz = zof(d)
        yy = lax.rem(zz + p + 1, 2)
        return rc(blk(G, p, zz, yy), wland(p, zz, yy), sX.at[p], rX.at[p, d], dev_x)

    def y_block(p, d):
        return rc(blk(G, p, zof(d), 1 - y), Ly.at[zof(d), :, cslice(p)], sY.at[p], rY.at[p, d], dev_y)

    def y_arrival(p, d):
        return rc(blk(G, p, zof(d), y), Ly.at[zof(d), :, cslice(p)], sY.at[p], rY.at[p, d], dev_y)

    def z_block(p, d):
        return rc(blk(G, p, zof(d), y), Lz.at[d - 1, :, cslice(p)], sZ.at[p], rZ.at[p], dev_z(d))

    def x_final(p):
        return rc(blk(G, p, z, y), Lx.at[:, cslice(p)], sXF.at[p], rXF.at[p], dev_x)

    def out_copies(p):
        lo = pl.multiple_of(c * SH, 16)
        c0, n = cols[p]
        if p in (PQ, PK, PV):
            pieces = [(c0, n, gq_out.at[p])]
        elif p == PO:
            pieces = [(c0, n, go_out)]
        elif p < PD:
            j = p - PG
            pieces = [(c0 + i * GH, GH, ggu_out.at[i, :, pl.ds(j * GH, GH)]) for i in range(2)]
        else:
            pieces = [(c0, n, gd_out.at[:, pl.ds((p - PD) * CH, CH)])]
        return [
            pltpu.make_async_copy(F.at[pl.ds(lo, SH), pl.ds(a, m)], dst, sO.at[p])
            for a, m, dst in pieces
        ]

    def f_rows(core):
        return pl.ds(pl.multiple_of(core * SH, 16), SH)

    def f_send(p):
        part = F.at[f_rows(oc), cslice(p)]
        return rc(part, part, sF.at[p], rF.at[p], dev_c)

    def f_arrival(p):
        part = F.at[f_rows(c), cslice(p)]
        return rc(part, part, sF.at[p], rF.at[p], dev_c)

    def rs1(p):
        def gy(d, carry):
            when(crosses_first(p, zof(d), 1 - y), lambda: y_block(p, d).start())
            return carry
        lax.fori_loop(0, 4, gy, 0)

        @pl.when(away)
        def _():
            if p != PD + 1:
                pl.semaphore_wait(cred.at[p], 1)

            def go(d, carry):
                x_block(p, d).start()
                return carry
            lax.fori_loop(0, 4, go, 0)

    def rs1n(p, d):
        zz = zof(d)

        @pl.when(both(native, jnp.logical_not(crosses_first(p, zz, 1 - y))))
        def _():
            x_block(p, d).wait_recv()
            rows = rows_of(zz, 1 - y)
            G[rows, cslice(p)] = (G[rows, cslice(p)].astype(F32) + wland(p, zz, 1 - y)[...].astype(F32)).astype(BF)
            y_block(p, d).start()

    def rs2(p, i):
        d = lax.rem(i + 1, 4)
        zz = zof(d)
        rows = rows_of(zz, y)
        first = crosses_first(p, zz, y)

        def finish(total):
            G[rows, cslice(p)] = total.astype(BF)
            when(d > 0, lambda: z_block(p, d).start())

        @pl.when(both(native, jnp.logical_not(first)))
        def _():
            x_block(p, d).wait_recv()
            y_arrival(p, d).wait_recv()
            finish(G[rows, cslice(p)].astype(F32) + Ly[zz, :, cslice(p)].astype(F32) + wland(p, zz, y)[...].astype(F32))

        @pl.when(first)
        def _():
            y_arrival(p, d).wait_recv()
            finish(G[rows, cslice(p)].astype(F32) + Ly[zz, :, cslice(p)].astype(F32))

    def rs3(p):
        own_first = crosses_first(p, z, y)

        def total():
            three = Lz.at[:, :, cslice(p)]
            pltpu.make_async_copy(three, three, rZ.at[p]).wait()
            out = G[rows_of(z, y), cslice(p)].astype(F32)
            for k in range(3):
                out = out + Lz[k, :, cslice(p)].astype(F32)
            return out

        @pl.when(native)
        def _():
            F[:, cslice(p)] = total()

        @pl.when(both(away, own_first))
        def _():
            G[rows_of(z, y), cslice(p)] = total().astype(BF)
            x_final(p).start()

    def rs4(p):
        @pl.when(native)
        def _():
            @pl.when(crosses_first(p, z, y))
            def _():
                x_final(p).wait_recv()
                F[:, cslice(p)] = F[:, cslice(p)] + Lx[:, cslice(p)].astype(F32)
            f_send(p).start()

        when(away, lambda: f_arrival(p).wait_recv())
        for cp in out_copies(p):
            cp.start()

    def rs_sent(p):
        own_first = crosses_first(p, z, y)

        @pl.when(native)
        def _():
            wait_bytes(p, 4, sY.at[p])
            wait_bytes(p, 3, sZ.at[p])
            f_send(p).wait_send()

        @pl.when(away)
        def _():
            wait_bytes(p, 4, sX.at[p])
            wait_bytes(p, 2, sY.at[p])

            @pl.when(own_first)
            def _():
                wait_bytes(p, 1, sZ.at[p])
                x_final(p).wait_send()
            when(jnp.logical_not(own_first), lambda: wait_bytes(p, 2, sZ.at[p]))

        part = F.at[f_rows(c), cslice(p)]
        pltpu.make_async_copy(part, part, sO.at[p]).wait()

    kinds.update({"rs1": rs1, "rs1n": rs1n, "rs2": rs2, "rs3": rs3, "rs4": rs4})
    order = [PD + 1, PG + 2, PD, PG + 3, PD + 2, PG, PG + 1, PG + 4, PG + 5, PO, PV, PQ, PK]
    assert not queue
    for i in range(NPARTS + 9):
        for name, lag in (("rs1n", 1), ("rs2", 2), ("rs3", 5), ("rs4", 9)):
            if 0 <= i - lag < NPARTS:
                queue.append((name, order[i - lag]))

    def transpose_half(src, dst, first_row):
        def body(i):
            r = pl.multiple_of(first_row + i * TR, TR)
            dst[:, pl.ds(r, TR)] = src[pl.ds(r, TR), :].T
        loop(HALF // TR, body)

    transpose_half(M, DT, own_r)
    rc(M.at[oth_rows], M.at[oth_rows], sM.at[9], rM.at[9], dev_c).wait_recv()
    transpose_half(M, DT, oth_r)

    def back_chunk(j, *events):
        hc = pl.ds(j * CH, CH)

        def body(i):
            r = pl.multiple_of(i * TR, TR)
            rows = pl.ds(r, TR)
            dh = nn(M[rows, :], W[:, wcols(PD + j)]).astype(BF).astype(F32)
            gate = GT[rows, hc].astype(F32)
            up = UP[rows, hc].astype(F32)
            sg = sigmoid(gate)
            GT[rows, hc] = (dh * up * (sg * (1.0 + gate * (1.0 - sg)))).astype(BF)
            UP[rows, hc] = (dh * gate * sg).astype(BF)
        loop(LEN // TR, body, *events)

    WR = D // 4

    def weight_grad(left, pieces, *events):
        def body(i):
            r = pl.multiple_of(i * WR, 64)
            for right, a, n, c0 in pieces:
                G[pl.ds(r, WR), pl.ds(c0, n)] = nn(left[pl.ds(r, WR), :], right[:, pl.ds(a, n)]).astype(BF)
        loop(4, body, *events)

    def grads_down(j, *events):
        weight_grad(DT, [(H, j * CH, CH, cols[PD + j][0])], *events)

    def grads_gate_up(g, *events):
        c0 = cols[PG + g][0]
        weight_grad(MT, [(GT, g * GH, GH, c0), (UP, g * GH, GH, c0 + GH)], *events)

    def now(p):
        rs1(p)

    def take(name, p):
        queue.remove((name, p))
        queue.insert(0, (name, p))
        step()

    grads_down(1)
    now(PD + 1)
    back_chunk(1)
    credit(PD + 1)
    grads_gate_up(2)
    now(PG + 2)
    grads_gate_up(3)
    back_chunk(0, ("rs1n", PD + 1))
    credit(PD)
    grads_down(0)
    now(PD)
    grads_gate_up(0, ("rs1n", PG + 2))
    grads_gate_up(1, ("rs2", PD + 1))
    now(PG + 3)
    back_chunk(2, ("rs1n", PD))
    credit(PD + 2)
    grads_down(2, ("rs2", PG + 2))
    now(PD + 2)
    grads_gate_up(4, ("rs1n", PG + 3))
    grads_gate_up(5, ("rs2", PD))

    mid_terms = []
    for g in range(NG_PARTS):
        mid_terms.append((GT, g * GH, GH, cols[PG + g][0]))
        mid_terms.append((UP, g * GH, GH, cols[PG + g][0] + GH))
    part1.wait_send()
    partial(mid_terms, oth_r, to_x)
    part2 = core_send(X.at[oth_rows], R, 11)
    part2.start()

    def to_n2_add(r, acc):
        N2[pl.ds(r, TR), :] = N2[pl.ds(r, TR), :] + acc
    partial(mid_terms, own_r, to_n2_add)
    credit("mid")
    now(PG)
    d2.wait_send()
    part2.wait_recv()

    def norm1_back(i, carry):
        dg, db = carry
        r = pl.multiple_of(i * TN, TN)
        rows = pl.ds(r, TN)
        e = N2[rows, :] + R[rows, :].astype(F32)
        n = N1[rows, :]
        rs = RS1[rows, 0:1]
        eg = e * NV[0:1, :]
        m1 = jnp.sum(eg, axis=1, keepdims=True) * inv_d
        m2 = jnp.sum(eg * n, axis=1, keepdims=True) * inv_d
        d = rs * (eg - m1 - n * m2)
        N2[rows, :] = d
        M[pl.ds(own_r + r, TN), :] = d.astype(BF)
        return dg + jnp.sum(e * n, axis=0, keepdims=True), db + jnp.sum(e, axis=0, keepdims=True)

    dg0, db0 = lax.fori_loop(0, HALF // TN, norm1_back, (zero_row, zero_row))
    d1 = core_send(M.at[own_rows], M.at[own_rows], 12)
    d1.start()
    NG[0:1, :] = dg0
    NG[2:3, :] = db0
    ng = core_send(NG, NGR, 13)
    ng.start()
    rc(M.at[oth_rows], M.at[oth_rows], sM.at[12], rM.at[12], dev_c).wait_recv()
    transpose_into(M, DT, ("rs1n", PD + 2))
    ng.wait_recv()
    NGT[...] = jnp.zeros(NGT.shape, F32)
    NGT[0:8, :] = NG[...] + NGR[...]
    G[:, norm_cols] = NGT[...].T.astype(BF)

    def d_att(i):
        r = pl.multiple_of(i * TR, TR)
        rows = pl.ds(r, TR)
        da = nn(M[rows, :], W[:, wcols(PO, 0, HC)]).astype(BF)
        UP[rows, pl.ds(0, HC)] = da
        prod = da.astype(F32) * A[rows, :].astype(F32)
        acc = jnp.zeros((TR, 128), F32)
        for k in range(PAIRS):
            piece = prod[:, 128 * k : 128 * (k + 1)]
            d0 = jnp.sum(jnp.where(head0, piece, 0.0), axis=1, keepdims=True)
            dall = jnp.sum(piece, axis=1, keepdims=True)
            acc = jnp.where(lane == 2 * k, d0, jnp.where(lane == 2 * k + 1, dall - d0, acc))
        DEL[rows, :] = acc
    loop(LEN // TR, d_att, ("rs2", PG + 3))
    weight_grad(DT, [(A, 0, HC, cols[PO][0])])
    now(PG + 1)
    take("rs3", PD + 1)
    LST[...] = LSE[...].T[0:8, :]
    DLT[...] = DEL[...].T[0:8, :]

    def attend_back(k, *events):
        pair = slice(128 * k, 128 * (k + 1))
        DQT[...] = jnp.zeros(DQT.shape, F32)

        def body(i):
            r = pl.multiple_of(i * TR, TR)
            rows = pl.ds(r, TR)
            keys = K[rows, pair].astype(F32) * scale
            vals = V[rows, pair]
            qp = Q[:, pair]
            da = UP[:, pair]
            same = SEGC[rows, 0:1] == SEGR[0:1, :]
            dv, dk = [], []
            for s in range(2):
                h = 2 * k + s
                mine = head0 if s == 0 else jnp.logical_not(head0)
                km = jnp.where(mine, keys, 0.0)
                vm = jnp.where(mine, vals.astype(F32), 0.0).astype(BF)
                sc = nt(km.astype(BF), qp)
                pr = jnp.where(same, jnp.exp(sc - LST[h : h + 1, :]), 0.0)
                dp = nt(vm, da)
                ds = (pr * (dp - DLT[h : h + 1, :])).astype(BF)
                dv.append(nn(pr.astype(BF), da))
                dk.append(nn(ds, qp))
                DQT[...] = DQT[...] + nn(km.T.astype(BF), ds)
            GT[rows, 2 * HC + 128 * k : 2 * HC + 128 * (k + 1)] = jnp.where(head0, dv[0], dv[1]).astype(BF)
            GT[rows, HC + 128 * k : HC + 128 * (k + 1)] = unrot(jnp.where(head0, dk[0], dk[1]) * scale, r, TR).astype(BF)
        loop(LEN // TR, body, *events)

        def finish(i):
            r = pl.multiple_of(i * 128, 128)
            GT[pl.ds(r, 128), pair] = unrot(DQT[:, pl.ds(r, 128)].T, r, 128).astype(BF)
        loop(LEN // 128, finish)

    now(PG + 4)
    attend_back(0, ("rs1n", PG), ("rs2", PD + 2))
    take("rs3", PG + 2)
    now(PG + 5)
    attend_back(1, ("rs1n", PG + 1), ("rs2", PG), ("rs1n", PG + 4))
    take("rs3", PD)
    now(PO)
    attend_back(2, ("rs2", PG + 1), ("rs1n", PG + 5), ("rs2", PG + 4))
    take("rs3", PG + 3)

    weight_grad(XT, [(GT, 2 * HC, HC, cols[PV][0])], ("rs1n", PO))
    now(PV)
    weight_grad(XT, [(GT, 0, HC, cols[PQ][0])], ("rs2", PG + 5))
    now(PQ)
    weight_grad(XT, [(GT, HC, HC, cols[PK][0])])
    now(PK)

    in_terms = [(GT, 0, 3 * HC, 0)]
    part2.wait_send()
    partial(in_terms, oth_r, to_x)
    part3 = core_send(X.at[oth_rows], R, 14)
    part3.start()
    partial(in_terms, own_r, to_n2_add)

    @pl.when(native)
    def _():
        act_home.wait()

    @pl.when(away)
    def _():
        act_away.wait_send()

    part3.wait_recv()

    gtok_home = pltpu.make_async_copy(N2, gtok_out, sM.at[15])
    gtok_away = rc(C, GL, sM.at[15], rM.at[15], dev_d)

    def add_rows(i):
        r = pl.multiple_of(i * TN, TN)
        rows = pl.ds(r, TN)
        total = N2[rows, :] + R[rows, :].astype(F32)
        N2[rows, :] = total
        C[rows, :] = total.astype(BF)
    loop(HALF // TN, add_rows)

    @pl.when(native)
    def _():
        gtok_home.start()

    @pl.when(away)
    def _():
        gtok_away.start()

    while queue:
        step()

    @pl.when(away)
    def _():
        rc(C, GL, sM.at[15], rM.at[15], dev_d).wait_recv()
        N1[...] = GL[...].astype(F32)
        out = pltpu.make_async_copy(N1, gtok_out, sM.at[16])
        out.start()
        out.wait()
        gtok_away.wait_send()
        rc(C, act_out, sM.at[10], rM.at[10], dev_d).wait_recv()
        tok_away.wait_send()
        cot_away.wait_send()

    @pl.when(native)
    def _():
        gtok_home.wait()
        seg_send.wait_send()

    d1.wait_send()
    ng.wait_send()
    part3.wait_send()
    for p in range(NPARTS):
        rs_sent(p)


def on_device_fused(
    tokens, segments, qkv_weight, out_weight, gate_up_weight, down_weight, norm_gain, norm_shift, cotangent
):
    length, width = segments.shape[1], tokens.shape[1]
    half = tokens.shape[0]
    hc, fc = qkv_weight.shape[3], gate_up_weight.shape[3]
    sh = qkv_weight.shape[2]
    nc = 4 * hc + 128 + 3 * fc
    cosine, sine = rope_numpy(length)
    vm = pl.BlockSpec(memory_space=pltpu.VMEM)
    anyspec = pl.BlockSpec(memory_space=pl.ANY)
    V_ = pltpu.VMEM
    br = 2 * sh
    dma = pltpu.SemaphoreType.DMA
    scratch = [
        V_((width, nc), BF),
        V_((width, nc), BF),
        V_((NZ, br, nc), BF),
        V_((NZ - 1, br, nc), BF),
        V_((br, nc), BF),
        V_((br, nc), F32),
        V_((length, width), BF),
        V_((width, length), BF),
        V_((length, hc), BF),
        V_((length, hc), BF),
        V_((length, hc), BF),
        V_((length, hc), BF),
        V_((length, width), BF),
        V_((width, length), BF),
        V_((width, length), BF),
        V_((length, fc), BF),
        V_((length, fc), BF),
        V_((length, fc), BF),
        V_((half, width), BF),
        V_((half, width), BF),
        V_((half, width), F32),
        V_((half, width), F32),
        V_((half, 128), F32),
        V_((128, length), F32),
        V_((length, 128), F32),
        V_((8, length), F32),
        V_((length, 128), F32),
        V_((8, length), F32),
        V_((8, length), F32),
        V_((length, 128), F32),
        V_((8, width), F32),
        V_((8, width), F32),
        V_((8, width), F32),
        V_((128, width), F32),
        V_((half, width), BF),
        V_((NZ, br, fc // 3), BF),
        V_((sh, 128), BF),
        V_((8, sh), F32),
        V_((length, 128), F32),
        V_((length, 128), F32),
        dma((NPARTS,)), dma((NPARTS,)), dma((NPARTS,)), dma((NPARTS,)), dma((NPARTS,)), dma((NPARTS, 8)),
        dma((NPARTS,)), dma((NPARTS, 4)), dma((NPARTS,)), dma((NPARTS,)), dma((NPARTS,)), dma((NPARTS, 4)),
        dma((NPARTS,)), dma((NPARTS,)), dma((NPARTS,)), dma((NPARTS,)), dma((NPARTS,)),
        dma((19,)), dma((17,)),
        pltpu.SemaphoreType.REGULAR((NPARTS,)),
    ]
    act, gtok, gq, go, ggu, gd = pl.pallas_call(
        functools.partial(layer_kernel, (length, width, hc, fc)),
        out_shape=(
            jax.ShapeDtypeStruct((half, width), BF),
            jax.ShapeDtypeStruct((half, width), F32),
            jax.ShapeDtypeStruct((3, sh, hc), F32),
            jax.ShapeDtypeStruct((sh, hc + 128), F32),
            jax.ShapeDtypeStruct((2, sh, fc), F32),
            jax.ShapeDtypeStruct((sh, fc), F32),
        ),
        in_specs=[anyspec, anyspec, vm, anyspec, anyspec, anyspec, anyspec, anyspec, anyspec, vm, vm],
        out_specs=tuple([anyspec] * 6),
        scratch_shapes=scratch,
        compiler_params=pltpu.CompilerParams(
            collective_id=1, has_side_effects=True, vmem_limit_bytes=VMEM_LIMIT
        ),
        name="layer",
    )(
        tokens, cotangent, segments, jnp.asarray(cosine), jnp.asarray(sine),
        qkv_weight, jnp.swapaxes(out_weight, 1, 2), gate_up_weight, jnp.swapaxes(down_weight, 1, 2), norm_gain, norm_shift,
    )
    act, gtok, gq, out_t, ggu, down_t, gain, shift = pl.pallas_call(
        functools.partial(finish_kernel, hc),
        out_shape=(
            jax.ShapeDtypeStruct((half, width), BF),
            jax.ShapeDtypeStruct((half, width), F32),
            jax.ShapeDtypeStruct((1, 3, sh, hc), F32),
            jax.ShapeDtypeStruct((1, sh, hc), F32),
            jax.ShapeDtypeStruct((1, 2, sh, fc), F32),
            jax.ShapeDtypeStruct((1, sh, fc), F32),
            jax.ShapeDtypeStruct((1, 2, sh), F32),
            jax.ShapeDtypeStruct((1, 2, sh), F32),
        ),
        in_specs=[anyspec, anyspec, anyspec, vm, anyspec, anyspec],
        out_specs=tuple([vm] * 8),
        scratch_shapes=[dma((5,))],
        name="finish",
    )(act, gtok, gq, go, ggu, gd)
    return act, gtok, gq, jnp.swapaxes(out_t, 1, 2), ggu, jnp.swapaxes(down_t, 1, 2), gain, shift


def finish_kernel(
    hc, act, gtok, gq, go, ggu, gd, act_out, gtok_out, gq_out, out_out, ggu_out, down_out, gain_out, shift_out, sem
):
    copies = [
        pltpu.make_async_copy(gtok, gtok_out, sem.at[0]),
        pltpu.make_async_copy(act, act_out, sem.at[1]),
        pltpu.make_async_copy(ggu, ggu_out.at[0], sem.at[2]),
        pltpu.make_async_copy(gq, gq_out.at[0], sem.at[3]),
        pltpu.make_async_copy(gd, down_out.at[0], sem.at[4]),
    ]
    for cp in copies:
        cp.start()
    sh = go.shape[0]
    out_out[0] = go[:, 0:hc]
    norms = jnp.concatenate([go[:, hc : hc + 128], jnp.zeros((128 - sh, 128), F32)], axis=0).T[:, 0:sh]
    gain_out[0] = norms[0:2, :]
    shift_out[0] = norms[2:4, :]
    for cp in copies:
        cp.wait()


VMEM_LIMIT = 64 * 1024 * 1024


def solution(mesh):
    body = on_device_fused if dict(mesh.shape) == {"fsdp": 16, "tp": 2} else on_device
    placed = (
        P(("fsdp", "tp"), None),
        P("fsdp", None),
        P(None, None, "fsdp", "tp"),
        P(None, "tp", "fsdp"),
        P(None, None, "fsdp", "tp"),
        P(None, "tp", "fsdp"),
        P(None, None, "fsdp"),
        P(None, None, "fsdp"),
        P(("fsdp", "tp"), None),
    )
    return jax.shard_map(
        body,
        mesh=mesh,
        in_specs=placed,
        out_specs=(
            P(("fsdp", "tp"), None),
            P(("fsdp", "tp"), None),
            P(None, None, "fsdp", "tp"),
            P(None, "tp", "fsdp"),
            P(None, None, "fsdp", "tp"),
            P(None, "tp", "fsdp"),
            P(None, None, "fsdp"),
            P(None, None, "fsdp"),
        ),
        check_vma=False,
    )
```

```python
import functools

import jax
import jax.numpy as jnp
import numpy as np
from jax import lax
from jax.experimental import pallas as pl
from jax.experimental.pallas import tpu as pltpu
from jax.sharding import PartitionSpec as P

HEAD_DIM = 64


epsilon = 1e-05


def for_sending(value):

    def short(part):
        return part.astype(jnp.bfloat16) if part.dtype == jnp.float32 else part

    return jax.tree.map(short, value)


def rope_tables(length):
    half_dim = HEAD_DIM // 2
    inv_freq = 1000.0 ** (-jnp.arange(half_dim, dtype=jnp.float32) * 2.0 / HEAD_DIM)
    angles = jnp.arange(length, dtype=jnp.float32)[:, None] * inv_freq[None, :]
    cosine = jnp.concatenate([jnp.cos(angles), jnp.cos(angles)], axis=-1)[:, None, :]
    sine_table = jnp.concatenate([jnp.sin(angles), jnp.sin(angles)], axis=-1)[:, None, :]
    return (cosine, sine_table)


def rotate(values_in, cosine, sine_table):
    half_dim = values_in.shape[-1] // 2
    turned = jnp.concatenate([-values_in[..., half_dim:], values_in[..., :half_dim]], axis=-1)
    return values_in * cosine + turned * sine_table


def unrotate(grads_in, cosine, sine_table):
    half_dim = grads_in.shape[-1] // 2
    moved_part = grads_in * sine_table
    return grads_in * cosine + jnp.concatenate(
        [moved_part[..., half_dim:], -moved_part[..., :half_dim]], axis=-1
    )


def norm_rows(stream, scale_vec, shift_vec):
    row_mean = jnp.mean(stream, axis=-1, keepdims=True)
    centred = stream - row_mean
    row_var = jnp.mean(centred * centred, axis=-1, keepdims=True)
    return centred * lax.rsqrt(row_var + epsilon) * scale_vec + shift_vec


def swiglu(gate_pre, up_proj):
    return jax.nn.silu(gate_pre) * up_proj


def spread(stream_low):
    return lax.all_gather(stream_low, "tp", axis=0, tiled=True)


def collect(partial_rows):
    return lax.psum_scatter(
        partial_rows.astype(jnp.bfloat16), "tp", scatter_dimension=0, tiled=True
    ).astype(jnp.float32)


def spread_grads(grads_low):
    return lax.all_gather(grads_low, "tp", axis=0, tiled=True)


def collect_grads(partial_rows):
    return lax.psum_scatter(
        partial_rows.astype(jnp.bfloat16), "tp", scatter_dimension=0, tiled=True
    ).astype(jnp.float32)


def layer_shards(arrays, layer_index):
    return tuple((weight_part[layer_index] for weight_part in arrays))


def block_scores(query_blk, keys_seq, seg_blk, seg_seq):
    scores = jnp.einsum(
        "qhd,khd->hqk", query_blk, keys_seq, preferred_element_type=jnp.float32
    ) * HEAD_DIM ** (-0.5)
    joined = seg_blk[:, None] == seg_seq[None, :]
    return jnp.where(joined[None], scores, -1e30)


def attend_forward(queries, keys_rot, values, segments):
    seq_count, length = segments.shape
    block_rows = min(512, length)
    block_count = length // block_rows

    def attend_one_block(flat_index):
        sequence = flat_index // block_count
        row_start = flat_index % block_count * block_rows
        query_seq = lax.dynamic_index_in_dim(queries, sequence, 0, False)
        keys_seq = lax.dynamic_index_in_dim(keys_rot, sequence, 0, False)
        values_seq = lax.dynamic_index_in_dim(values, sequence, 0, False)
        seg_seq = lax.dynamic_index_in_dim(segments, sequence, 0, False)
        query_blk = lax.dynamic_slice_in_dim(query_seq, row_start, block_rows, 0)
        seg_blk = lax.dynamic_slice_in_dim(seg_seq, row_start, block_rows, 0)
        scores = block_scores(query_blk, keys_seq, seg_blk, seg_seq)
        row_max = jnp.max(scores, axis=-1, keepdims=True)
        exp_terms = jnp.exp(scores - row_max)
        row_total = jnp.sum(exp_terms, axis=-1, keepdims=True)
        probs_low = (exp_terms / row_total).astype(jnp.bfloat16)
        attended = jnp.einsum(
            "hqk,khd->qhd", probs_low, values_seq, preferred_element_type=jnp.float32
        )
        return (attended, row_max + jnp.log(row_total))

    attended, log_total = lax.map(
        attend_one_block, jnp.arange(seq_count * block_count, dtype=jnp.int32)
    )
    return (attended.reshape(seq_count * length, -1), log_total)


def attend_backward(queries, keys_rot, values, d_attended, log_total, segments):
    seq_count, length = segments.shape
    block_rows = min(512, length)
    block_count = length // block_rows
    scale_value = HEAD_DIM ** (-0.5)

    def one_sequence(sequence):
        query_seq = lax.dynamic_index_in_dim(queries, sequence, 0, False)
        keys_seq = lax.dynamic_index_in_dim(keys_rot, sequence, 0, False)
        values_seq = lax.dynamic_index_in_dim(values, sequence, 0, False)
        d_out_seq = lax.dynamic_index_in_dim(d_attended, sequence, 0, False)
        seg_seq = lax.dynamic_index_in_dim(segments, sequence, 0, False)

        def one_one_block(running, block_index):
            row_start = block_index * block_rows
            query_blk = lax.dynamic_slice_in_dim(query_seq, row_start, block_rows, 0)
            d_out_blk = lax.dynamic_slice_in_dim(d_out_seq, row_start, block_rows, 0)
            seg_blk = lax.dynamic_slice_in_dim(seg_seq, row_start, block_rows, 0)
            block_total = lax.dynamic_index_in_dim(
                log_total, sequence * block_count + block_index, 0, False
            )
            scores = block_scores(query_blk, keys_seq, seg_blk, seg_seq)
            attn_probs = jnp.exp(scores - block_total)
            probs_low = attn_probs.astype(jnp.bfloat16)
            d_probs = jnp.einsum(
                "qhd,khd->hqk", d_out_blk, values_seq, preferred_element_type=jnp.float32
            )
            inner_sum = jnp.sum(attn_probs * d_probs, axis=-1, keepdims=True)
            d_scores = (attn_probs * (d_probs - inner_sum)).astype(jnp.bfloat16)
            d_query = (
                jnp.einsum("hqk,khd->qhd", d_scores, keys_seq, preferred_element_type=jnp.float32)
                * scale_value
            )
            d_key = (
                running[0]
                + jnp.einsum(
                    "hqk,qhd->khd", d_scores, query_blk, preferred_element_type=jnp.float32
                )
                * scale_value
            )
            d_value = running[1] + jnp.einsum(
                "hqk,qhd->khd", probs_low, d_out_blk, preferred_element_type=jnp.float32
            )
            return ((d_key, d_value), d_query)

        zero_keys = jnp.zeros(keys_seq.shape, jnp.float32)
        (d_keys, d_values), d_queries = lax.scan(
            one_one_block, (zero_keys, zero_keys), jnp.arange(block_count, dtype=jnp.int32)
        )
        return (d_queries.reshape(keys_seq.shape), d_keys, d_values)

    return lax.map(one_sequence, jnp.arange(seq_count, dtype=jnp.int32))


def layer_forward(stream, segments, weights, tables):
    qkv_w, out_w, gate_up_w, down_w, gain_rows, shift_rows = weights
    cosine, sine_table = tables
    seq_count, length = segments.shape
    head_count = qkv_w.shape[2] // HEAD_DIM
    shaped = (seq_count, length, head_count, HEAD_DIM)
    gain_vals = gain_rows.astype(jnp.float32)
    shift_vals = shift_rows.astype(jnp.float32)
    inputs = spread(stream.astype(jnp.bfloat16))
    query_pre = jnp.dot(inputs, qkv_w[0], preferred_element_type=jnp.float32).reshape(shaped)
    key_pre = jnp.dot(inputs, qkv_w[1], preferred_element_type=jnp.float32).reshape(shaped)
    queries = rotate(query_pre, cosine, sine_table).astype(jnp.bfloat16)
    keys_rot = rotate(key_pre, cosine, sine_table).astype(jnp.bfloat16)
    values = (
        jnp.dot(inputs, qkv_w[2], preferred_element_type=jnp.float32)
        .astype(jnp.bfloat16)
        .reshape(shaped)
    )
    attended, log_total = attend_forward(queries, keys_rot, values, segments)
    attended_low = attended.astype(jnp.bfloat16)
    branch = collect(jnp.dot(attended_low, out_w, preferred_element_type=jnp.float32))
    mixed = stream + branch
    first_norm = norm_rows(mixed, gain_vals[0], shift_vals[0])
    middle = spread(first_norm.astype(jnp.bfloat16))
    gate_pre = jnp.dot(middle, gate_up_w[0], preferred_element_type=jnp.float32)
    up_proj = jnp.dot(middle, gate_up_w[1], preferred_element_type=jnp.float32)
    hidden = swiglu(gate_pre, up_proj).astype(jnp.bfloat16)
    branch_two = collect(jnp.dot(hidden, down_w, preferred_element_type=jnp.float32))
    second_in = first_norm + branch_two
    saved_state = (
        inputs,
        queries,
        keys_rot,
        values,
        log_total,
        attended_low,
        mixed,
        middle,
        gate_pre,
        up_proj,
        hidden,
        second_in,
    )
    return (norm_rows(second_in, gain_vals[1], shift_vals[1]), saved_state)


def layer_backward(grad_out, saved_state, segments, weights, tables):
    qkv_w, out_w, gate_up_w, down_w, gain_rows, shift_rows = weights
    (
        inputs,
        queries,
        keys_rot,
        values,
        log_total,
        attended_low,
        mixed,
        middle,
        gate_pre,
        up_proj,
        hidden,
        second_in,
    ) = saved_state
    cosine, sine_table = tables
    gain_vals = gain_rows.astype(jnp.float32)
    shift_vals = shift_rows.astype(jnp.float32)
    unused_two, norm_two_back = jax.vjp(norm_rows, second_in, gain_vals[1], shift_vals[1])
    d_second, d_gain_two, d_shift_two = norm_two_back(grad_out)
    d_branch_two = spread_grads(d_second.astype(jnp.bfloat16))
    grad_down = jnp.einsum("rf,rd->fd", hidden, d_branch_two, preferred_element_type=jnp.float32)
    d_hidden_low = jnp.einsum(
        "rd,fd->rf", d_branch_two, down_w, preferred_element_type=jnp.float32
    ).astype(jnp.bfloat16)
    d_hidden = lax.optimization_barrier(d_hidden_low).astype(jnp.float32)
    unused_swish, swish_back = jax.vjp(swiglu, gate_pre, up_proj)
    d_gate, d_up = swish_back(d_hidden)
    d_gate_low = d_gate.astype(jnp.bfloat16)
    d_up_low = d_up.astype(jnp.bfloat16)
    grad_gate_up = jnp.stack(
        [
            jnp.einsum("rd,rf->df", middle, d_gate_low, preferred_element_type=jnp.float32),
            jnp.einsum("rd,rf->df", middle, d_up_low, preferred_element_type=jnp.float32),
        ]
    )
    d_middle = jnp.einsum("rf,df->rd", d_gate_low, gate_up_w[0], preferred_element_type=jnp.float32)
    d_middle = d_middle + jnp.einsum(
        "rf,df->rd", d_up_low, gate_up_w[1], preferred_element_type=jnp.float32
    )
    d_first = d_second + collect_grads(d_middle)
    unused_one, norm_one_back = jax.vjp(norm_rows, mixed, gain_vals[0], shift_vals[0])
    d_mixed, d_gain_one, d_shift_one = norm_one_back(d_first)
    d_branch = spread_grads(d_mixed.astype(jnp.bfloat16))
    grad_out_w = jnp.einsum("rc,rd->cd", attended_low, d_branch, preferred_element_type=jnp.float32)
    d_attended = (
        jnp.einsum("rd,cd->rc", d_branch, out_w, preferred_element_type=jnp.float32)
        .astype(jnp.bfloat16)
        .reshape(queries.shape)
    )
    d_queries, d_keys, d_values = attend_backward(
        queries, keys_rot, values, d_attended, log_total, segments
    )
    flat_shape = (-1, queries.shape[2] * queries.shape[3])
    d_query_low = unrotate(d_queries, cosine, sine_table).astype(jnp.bfloat16).reshape(flat_shape)
    d_key_low = unrotate(d_keys, cosine, sine_table).astype(jnp.bfloat16).reshape(flat_shape)
    d_value_low = d_values.astype(jnp.bfloat16).reshape(flat_shape)
    grad_parts = (d_query_low, d_key_low, d_value_low)
    grad_qkv = jnp.stack(
        [
            jnp.einsum("rd,rc->dc", inputs, grad_part, preferred_element_type=jnp.float32)
            for grad_part in grad_parts
        ]
    )
    d_inputs = jnp.einsum("rc,dc->rd", d_query_low, qkv_w[0], preferred_element_type=jnp.float32)
    d_inputs = d_inputs + jnp.einsum(
        "rc,dc->rd", d_key_low, qkv_w[1], preferred_element_type=jnp.float32
    )
    d_inputs = d_inputs + jnp.einsum(
        "rc,dc->rd", d_value_low, qkv_w[2], preferred_element_type=jnp.float32
    )
    d_stream = d_mixed + collect_grads(d_inputs)
    weight_grads = (
        grad_qkv,
        grad_out_w,
        grad_gate_up,
        grad_down,
        jnp.stack([d_gain_one, d_gain_two]),
        jnp.stack([d_shift_one, d_shift_two]),
    )
    return (d_stream, weight_grads)


def on_device(
    tokens,
    segments,
    qkv_weight,
    out_weight,
    gate_up_weight,
    down_weight,
    norm_gain,
    norm_shift,
    cotangent,
):
    arrays = (qkv_weight, out_weight, gate_up_weight, down_weight, norm_gain, norm_shift)
    layer_total = qkv_weight.shape[0]
    tables = rope_tables(segments.shape[1])
    stream = tokens.astype(jnp.float32)
    kept_weights = []
    layer_index = 0
    weights = lax.all_gather(
        for_sending(layer_shards(arrays, layer_index)), "fsdp", axis=1, tiled=True
    )
    stream, saved_state = layer_forward(stream, segments, weights, tables)
    kept_weights.append(weights)
    saved_states = [saved_state]
    activations = stream.astype(jnp.bfloat16)
    grad_stream = cotangent.astype(jnp.float32)
    grad_layers = [None] * layer_total
    for layer_index in reversed(range(layer_total)):
        weights = lax.all_gather(
            for_sending(layer_shards(arrays, layer_index)), "fsdp", axis=1, tiled=True
        )
        grad_stream, weight_grads = layer_backward(
            grad_stream, saved_states[layer_index], segments, weights, tables
        )
        grad_layers[layer_index] = (
            lax.psum_scatter(weight_grads[0], "fsdp", scatter_dimension=1, tiled=True),
            lax.psum_scatter(weight_grads[1], "fsdp", scatter_dimension=1, tiled=True),
            lax.psum_scatter(weight_grads[2], "fsdp", scatter_dimension=1, tiled=True),
            lax.psum_scatter(weight_grads[3], "fsdp", scatter_dimension=1, tiled=True),
            lax.psum_scatter(weight_grads[4], "fsdp", scatter_dimension=1, tiled=True),
            lax.psum_scatter(weight_grads[5], "fsdp", scatter_dimension=1, tiled=True),
        )
    stacked = [jnp.stack([grad_layers[0][member]]) for member in range(6)]
    gain_sum, shift_sum = lax.psum((stacked[4], stacked[5]), "tp")
    return (
        activations,
        grad_stream,
        stacked[0],
        stacked[1],
        stacked[2],
        stacked[3],
        gain_sum,
        shift_sum,
    )


MESH_ID = pl.DeviceIdType.MESH
BF = jnp.bfloat16
F32 = jnp.float32
NZ, NY = 4, 2
PQ, PK, PV, PO, PG = range(5)
NG_PARTS = 6
PD = PG + NG_PARTS
NPARTS = PD + 3
PAIRS = 3
NEG = -1e30


def nt(a, b):
    return lax.dot_general(a, b, (((1,), (1,)), ((), ())), preferred_element_type=F32)


def nn(a, b):
    return jnp.dot(a, b, preferred_element_type=F32)


def rope_numpy(length):
    half = HEAD_DIM // 2
    inv = 1000.0 ** (-np.arange(half, dtype=np.float64) * 2.0 / HEAD_DIM)
    angles = np.arange(length, dtype=np.float64)[:, None] * inv[None, :]
    cosine, sine = np.cos(angles), np.sin(angles)
    cos_rows = np.concatenate([cosine, cosine, cosine, cosine], axis=1)
    sin_rows = np.concatenate([-sine, sine, -sine, sine], axis=1)
    return cos_rows.astype(np.float32), sin_rows.astype(np.float32)


def layer_kernel(
    dims,
    tok_ref, cot_ref, seg_ref, cos_in, sin_in, qkv_in, out_ref, gu_in, down_ref, gain_ref, shift_ref,
    act_out, gtok_out, gq_out, go_out, ggu_out, gd_out,
    W, G, Ly, Lz, Lx, F, X, XT, Q, K, V, A, M, MT, DT, GT, UP, H, R, C, N1, N2, RS1,
    DQT, LSE, LST, DEL, DLT, SEGR, SEGC, NV, NG, NGR, NGT, GL, LD, OWN_N, N8, cos_ref, sin_ref,
    sLC, sCR, rCR, sA, sB, rB, sY, rY, sZ, rZ, sX, rX, sXF, rXF, sF, rF, sO, sM, rM, cred,
):
    LEN, D, HC, FC = dims
    HALF = LEN // 2
    SH = D // 16
    BR = 2 * SH
    CH = FC // 3
    GH = FC // NG_PARTS
    OW = HC + 128
    cols = {}
    at = 0
    for p in range(NPARTS):
        n = HC if p in (PQ, PK, PV) else OW if p == PO else 2 * GH if p < PD else CH
        cols[p] = (at, n)
        at += n

    f = lax.axis_index("fsdp")
    t = lax.axis_index("tp")
    c = lax.rem(f, 2)
    y = lax.rem(f // 2, 2)
    z = f // 4
    oc = 1 - c
    native = c == t
    away = c != t
    dev_x = (f, 1 - t)
    dev_y = ((z * 2 + (1 - y)) * 2 + c, t)
    dev_c = ((z * 2 + y) * 2 + oc, t)
    dev_d = ((z * 2 + y) * 2 + oc, 1 - t)

    def zof(d):
        return lax.rem(z + d, NZ)

    def dev_z(d):
        return ((zof(d) * 2 + y) * 2 + c, t)

    def rows_of(zz, yy):
        return pl.ds(pl.multiple_of((zz * 2 + yy) * BR, 16), BR)

    def cslice(p):
        return pl.ds(cols[p][0], cols[p][1])

    def blk(ref, p, zz, yy):
        return ref.at[rows_of(zz, yy), cslice(p)]

    def bid(zz, yy):
        return zz * 2 + yy

    def crosses_first(p, zz, yy):
        return lax.rem(zz + yy + p, 2) == 0

    def last_i(p, zz, yy):
        return (lax.rem(zz + 2 * yy + 3 * p, 7) // 3 + 1) // 2

    def ag_first(p, zz, yy):
        return last_i(p, zz, yy) == 0

    def both(*conds):
        out = conds[0]
        for cond in conds[1:]:
            out = jnp.logical_and(out, cond)
        return out

    def when(cond, fn):
        pl.when(cond)(fn)

    def rc(src, dst, ss, rs, dev):
        return pltpu.make_async_remote_copy(
            src_ref=src, dst_ref=dst, send_sem=ss, recv_sem=rs, device_id=dev, device_id_type=MESH_ID
        )

    def wait_bytes(p, blocks, sem):
        ref = Ly.at[0, :, pl.ds(0, blocks * cols[p][1])]
        pltpu.make_async_copy(ref, ref, sem).wait()

    own_r = pl.multiple_of(c * HALF, HALF)
    oth_r = pl.multiple_of(oc * HALF, HALF)
    own_rows = pl.ds(own_r, HALF)
    oth_rows = pl.ds(oth_r, HALF)

    bar = pltpu.get_barrier_semaphore()
    partners = [dev_x, dev_y, dev_c, dev_d, dev_z(1), dev_z(2), dev_z(3)]
    for dev in partners:
        pl.semaphore_signal(bar, inc=1, device_id=dev, device_id_type=MESH_ID)
    pl.semaphore_wait(bar, len(partners))

    def shard_pieces(p):
        c0, n = cols[p]
        if p in (PQ, PK, PV):
            return [(qkv_in.at[0, p], c0, n)]
        if p == PO:
            return [(out_ref.at[0], c0, HC), (OWN_N, c0 + HC, 128)]
        if p < PD:
            j = p - PG
            return [(gu_in.at[0, i, :, pl.ds(j * GH, GH)], c0 + i * GH, GH) for i in range(2)]
        j = p - PD
        return [(down_ref.at[0, :, pl.ds(j * CH, CH)], c0, CH)]

    shard_rows = pl.ds(pl.multiple_of((z * 2 + y) * BR + c * SH, 16), SH)
    oshard_rows = pl.ds(pl.multiple_of((z * 2 + y) * BR + oc * SH, 16), SH)

    def start_shards(p):
        @pl.when(native)
        def _():
            for src, c0, n in shard_pieces(p):
                pltpu.make_async_copy(src, W.at[shard_rows, pl.ds(c0, n)], sLC.at[p]).start()

        @pl.when(away)
        def _():
            for src, c0, n in shard_pieces(p):
                rc(src, W.at[shard_rows, pl.ds(c0, n)], sCR.at[p], rCR.at[p], dev_c).start()

    def own_whole(p):
        return W.at[shard_rows, cslice(p)]

    tok_home = pltpu.make_async_copy(tok_ref, X.at[own_rows], sM.at[2])
    tok_core = rc(tok_ref, X.at[own_rows], sM.at[3], rM.at[3], dev_c)
    tok_away = rc(tok_ref, X.at[oth_rows], sM.at[4], rM.at[4], dev_d)
    tok_pass = rc(X.at[own_rows], X.at[own_rows], sM.at[3], rM.at[3], dev_c)
    seg_send = rc(SEGR, SEGR, sM.at[1], rM.at[1], dev_c)
    cot_home = pltpu.make_async_copy(cot_ref, C, sM.at[5])
    cot_away = rc(cot_ref, C, sM.at[5], rM.at[5], dev_d)

    turns = [
        pltpu.make_async_copy(cos_in, cos_ref, sM.at[17]),
        pltpu.make_async_copy(sin_in, sin_ref, sM.at[18]),
    ]
    start_shards(PQ)
    start_shards(PK)
    for cp in turns:
        cp.start()

    @pl.when(native)
    def _():
        tok_home.start()
        tok_core.start()
        cot_home.start()
        SEGR[...] = jnp.broadcast_to(seg_ref[...].astype(F32), SEGR.shape)
        seg_send.start()

    @pl.when(away)
    def _():
        tok_away.start()
        cot_away.start()

    for p in range(2, NPARTS):
        if p != PO:
            start_shards(p)

    def ag_copy(p, zz, yy, dev, sem):
        b = blk(W, p, zz, yy)
        return rc(b, b, sem.at[p], rB.at[p, bid(zz, yy)], dev)

    def got(p, zz, yy):
        b = blk(W, p, zz, yy)
        rc(b, b, sA.at[p], rB.at[p, bid(zz, yy)], dev_x).wait_recv()

    def ag1(p):
        def spread_own():
            for d in (2, 1, 3):
                ag_copy(p, z, y, dev_z(d), sA).start()
            ag_copy(p, z, y, dev_y, sA).start()

        @pl.when(native)
        def _():
            pltpu.make_async_copy(own_whole(p), own_whole(p), sLC.at[p]).wait()
            o = W.at[oshard_rows, cslice(p)]
            rc(o, o, sCR.at[p], rCR.at[p], dev_c).wait_recv()
            ag_copy(p, z, y, dev_x, sA).start()
            spread_own()

        @pl.when(both(away, ag_first(p, z, y)))
        def _():
            got(p, z, y)
            spread_own()

    def ag2(p, d):
        zz = zof(d)
        first = ag_first(p, zz, y)

        def work():
            got(p, zz, y)
            ag_copy(p, zz, y, dev_y, sB).start()

            @pl.when(jnp.logical_not(first))
            def _():
                ag_copy(p, zz, y, dev_x, sB).start()

        when(both(d > 0, jnp.logical_or(native, first)), work)

    def ag3(p, d):
        zz = zof(d)
        first = ag_first(p, zz, 1 - y)

        @pl.when(jnp.logical_or(native, first))
        def _():
            got(p, zz, 1 - y)

            @pl.when(jnp.logical_not(first))
            def _():
                ag_copy(p, zz, 1 - y, dev_x, sB).start()

    def ag4(p, d):
        zz = zof(d)
        for yy in (y, 1 - y):
            when(both(away, jnp.logical_not(ag_first(p, zz, yy))), functools.partial(got, p, zz, yy))

    def ag_sent(p):
        own_first = ag_first(p, z, y)
        when(native, lambda: wait_bytes(p, 5, sA.at[p]))
        when(both(away, own_first), lambda: wait_bytes(p, 4, sA.at[p]))
        nat = 1 - lax.rem(c + t, 2)
        count = 0
        for d in range(4):
            if d:
                mine = last_i(p, zof(d), y)
                count = count + nat * (1 + mine) + (1 - nat) * (1 - mine)
            count = count + nat * last_i(p, zof(d), 1 - y)
        for n in range(1, 11):
            when(count == n, functools.partial(wait_bytes, p, n, sB.at[p]))

        @pl.when(away)
        def _():
            pltpu.make_async_copy(own_whole(p), own_whole(p), sCR.at[p]).wait()

    def loop(n, body, *events):
        for ev in events:
            assert ev in queue and n == 4
            queue.remove(ev)

        def go(i, carry):
            body(i)
            for name, p in events:
                kinds[name](p, i)
            return carry
        lax.fori_loop(0, n, go, 0)

    queue = []
    for i in range(-2, NPARTS + 2):
        for name, lag in (("ag1", -2), ("ag2", 0), ("ag3", 1), ("ag4", 2)):
            if 0 <= i - lag < NPARTS:
                queue.append((name, i - lag))
    kinds = {"ag1": ag1, "ag2": ag2, "ag3": ag3, "ag4": ag4}
    whole = ("ag1", "rs1", "rs3", "rs4")

    def step():
        name, p = queue.pop(0)
        if name in whole:
            kinds[name](p)
        else:
            def go(i, carry):
                kinds[name](p, i)
                return carry
            lax.fori_loop(0, 4, go, 0)

    def until(name, p):
        while (name, p) in queue:
            step()

    def ready(p):
        until("ag3", p)
        if ("ag4", p) in queue:
            queue.remove(("ag4", p))
            queue.insert(0, ("ag4", p))
            step()

    lane = lax.broadcasted_iota(jnp.int32, (1, 128), 1)
    low_half = lax.rem(lane, HEAD_DIM) < HEAD_DIM // 2
    head0 = lane < HEAD_DIM

    def swap(v):
        return jnp.where(low_half, pltpu.roll(v, 128 - HEAD_DIM // 2, 1), pltpu.roll(v, HEAD_DIM // 2, 1))

    def rot(v, r, n):
        return v * cos_ref[pl.ds(r, n), :] + swap(v) * sin_ref[pl.ds(r, n), :]

    def unrot(v, r, n):
        return v * cos_ref[pl.ds(r, n), :] - swap(v) * sin_ref[pl.ds(r, n), :]

    def wcols(p, a=0, n=None):
        c0, m = cols[p]
        return pl.ds(c0 + a, m if n is None else n)

    TR = 256

    def transpose_into(src, dst, *events):
        def body(i):
            r = pl.multiple_of(i * TR, TR)
            dst[:, pl.ds(r, TR)] = src[pl.ds(r, TR), :].T
        loop(LEN // TR, body, *events)

    def core_send(src, dst, k):
        return rc(src, dst, sM.at[k], rM.at[k], dev_c)

    until("ag1", PK)

    eye = (
        lax.broadcasted_iota(jnp.int32, (SH, SH), 0) == lax.broadcasted_iota(jnp.int32, (SH, SH), 1)
    ).astype(BF)
    N8[...] = jnp.zeros(N8.shape, F32)
    N8[0:2, :] = gain_ref[0].astype(F32)
    N8[2:4, :] = shift_ref[0].astype(F32)
    OWN_N[...] = jnp.zeros(OWN_N.shape, BF)
    OWN_N[:, 0:8] = nt(eye, N8[...].astype(BF)).astype(BF)
    start_shards(PO)

    @pl.when(native)
    def _():
        tok_home.wait()

    @pl.when(away)
    def _():
        rc(SEGR, SEGR, sM.at[1], rM.at[1], dev_c).wait_recv()
    until("ag2", PQ)

    @pl.when(away)
    def _():
        rc(tok_ref, X.at[own_rows], sM.at[4], rM.at[4], dev_d).wait_recv()
        tok_pass.start()
    until("ag3", PQ)
    rc(X.at[oth_rows], X.at[oth_rows], sM.at[3], rM.at[3], dev_c).wait_recv()

    def seg_cols(i):
        r = pl.multiple_of(i * 128, 128)
        SEGC[pl.ds(r, 128), :] = jnp.broadcast_to(SEGR[0:1, pl.ds(r, 128)], (128, 128)).T
    loop(LEN // 128, seg_cols)

    def project(p, dst, turn, *events):
        def body(i):
            r = pl.multiple_of(i * TR, TR)
            v = nn(X[pl.ds(r, TR), :], W[:, wcols(p)])
            for k in range(PAIRS):
                part = v[:, 128 * k : 128 * (k + 1)]
                if turn:
                    part = rot(part, r, TR)
                dst[pl.ds(r, TR), 128 * k : 128 * (k + 1)] = part.astype(BF)
        loop(LEN // TR, body, *events)

    transpose_into(X, XT)
    for cp in turns:
        cp.wait()
    ready(PQ)
    project(PQ, Q, True)
    ready(PK)
    project(PK, K, True)
    ready(PV)
    project(PV, V, False)

    scale = HEAD_DIM ** -0.5
    LSE[...] = jnp.zeros(LSE.shape, F32)

    def attend_pair(k, *events):
        def body(i):
            r = pl.multiple_of(i * TR, TR)
            rows = pl.ds(r, TR)
            pair = slice(128 * k, 128 * (k + 1))
            q = Q[rows, pair]
            keys = K[:, pair]
            vals = V[:, pair]
            same = SEGC[rows, 0:1] == SEGR[0:1, :]
            outs, lses = [], []
            for s in range(2):
                mine = head0 if s == 0 else jnp.logical_not(head0)
                qm = jnp.where(mine, q.astype(F32) * scale, 0.0).astype(BF)
                sc = jnp.where(same, nt(qm, keys), NEG)
                top = jnp.max(sc, axis=1, keepdims=True)
                e = jnp.exp(sc - top)
                total = jnp.sum(e, axis=1, keepdims=True)
                outs.append(nn(e.astype(BF), vals) / total)
                lses.append(top + jnp.log(total))
            A[rows, pair] = jnp.where(head0, outs[0], outs[1]).astype(BF)
            LSE[rows, :] = jnp.where(lane == 2 * k, lses[0], jnp.where(lane == 2 * k + 1, lses[1], LSE[rows, :]))
        loop(LEN // TR, body, *events)

    for k in range(PAIRS):
        until("ag1", PO + 3 + k)
        attend_pair(k, ("ag2", PO + 1 + k), ("ag3", PO + k))

    ready(PO)
    norm_cols = pl.ds(cols[PO][0] + HC, 128)
    NV[...] = W[:, norm_cols].astype(F32).T[0:8, :]

    @pl.when(native)
    def _():
        tok_core.wait_send()

    @pl.when(away)
    def _():
        tok_pass.wait_send()

    def partial(lhs, dst_rows_at, finish):
        def body(i):
            r = pl.multiple_of(i * TR, TR)
            acc = None
            for ref, a, n, w0 in lhs:
                term = nt(ref[pl.ds(dst_rows_at + r, TR), pl.ds(a, n)], W[:, pl.ds(w0, n)])
                acc = term if acc is None else acc + term
            finish(r, acc)
        loop(HALF // TR, body)

    def to_x(r, acc):
        X[pl.ds(oth_r + r, TR), :] = acc.astype(BF)

    def to_n2(r, acc):
        N2[pl.ds(r, TR), :] = acc

    out_terms = [(A, 0, HC, cols[PO][0])]
    partial(out_terms, oth_r, to_x)
    part0 = core_send(X.at[oth_rows], R, 6)
    part0.start()
    partial(out_terms, own_r, to_n2)
    until("ag1", PG + 5)
    part0.wait_recv()

    TN = 128
    inv_d = 1.0 / D

    def norm1(i):
        r = pl.multiple_of(i * TN, TN)
        rows = pl.ds(r, TN)
        mix = X[pl.ds(own_r + r, TN), :].astype(F32) + N2[rows, :] + R[rows, :].astype(F32)
        mean = jnp.sum(mix, axis=1, keepdims=True) * inv_d
        cen = mix - mean
        var = jnp.sum(cen * cen, axis=1, keepdims=True) * inv_d
        rs = lax.rsqrt(var + epsilon)
        n = cen * rs
        N1[rows, :] = n
        RS1[rows, :] = jnp.broadcast_to(rs, (TN, 128))
        M[pl.ds(own_r + r, TN), :] = (n * NV[0:1, :] + NV[2:3, :]).astype(BF)
    loop(HALF // TN, norm1)
    mid = core_send(M.at[own_rows], M.at[own_rows], 7)
    mid.start()
    until("ag2", PG + 3)
    rc(M.at[oth_rows], M.at[oth_rows], sM.at[7], rM.at[7], dev_c).wait_recv()

    def sigmoid(v):
        return 1.0 / (1.0 + jnp.exp(-v))

    def hidden_chunk(g, *events):
        def body(i):
            r = pl.multiple_of(i * TR, TR)
            rows = pl.ds(r, TR)
            pre = nn(M[rows, :], W[:, wcols(PG + g)])
            gate, up = pre[:, :GH], pre[:, GH:]
            GT[rows, pl.ds(g * GH, GH)] = gate.astype(BF)
            UP[rows, pl.ds(g * GH, GH)] = up.astype(BF)
            H[rows, pl.ds(g * GH, GH)] = (gate * sigmoid(gate) * up).astype(BF)
        loop(LEN // TR, body, *events)

    for g in range(NG_PARTS):
        ready(PG + g)
        if g == 1:
            transpose_into(M, MT)
        hidden_chunk(g)
    for p in range(PD, NPARTS):
        ready(p)
    part0.wait_send()
    mid.wait_send()

    down_terms = [(H, j * CH, CH, cols[PD + j][0]) for j in range(3)]
    partial(down_terms, oth_r, to_x)
    part1 = core_send(X.at[oth_rows], R, 8)
    part1.start()
    partial(down_terms, own_r, to_n2)

    @pl.when(native)
    def _():
        cot_home.wait()

    @pl.when(away)
    def _():
        rc(cot_ref, C, sM.at[5], rM.at[5], dev_d).wait_recv()

    part1.wait_recv()

    def norm2(i, carry):
        dg, db = carry
        r = pl.multiple_of(i * TN, TN)
        rows = pl.ds(r, TN)
        first = N1[rows, :] * NV[0:1, :] + NV[2:3, :]
        v = first + N2[rows, :] + R[rows, :].astype(F32)
        mean = jnp.sum(v, axis=1, keepdims=True) * inv_d
        cen = v - mean
        var = jnp.sum(cen * cen, axis=1, keepdims=True) * inv_d
        rs = lax.rsqrt(var + epsilon)
        n = cen * rs
        e = C[rows, :].astype(F32)
        C[rows, :] = (n * NV[1:2, :] + NV[3:4, :]).astype(BF)
        eg = e * NV[1:2, :]
        m1 = jnp.sum(eg, axis=1, keepdims=True) * inv_d
        m2 = jnp.sum(eg * n, axis=1, keepdims=True) * inv_d
        d = rs * (eg - m1 - n * m2)
        N2[rows, :] = d
        M[pl.ds(own_r + r, TN), :] = d.astype(BF)
        return dg + jnp.sum(e * n, axis=0, keepdims=True), db + jnp.sum(e, axis=0, keepdims=True)

    zero_row = jnp.zeros((1, D), F32)
    dg1, db1 = lax.fori_loop(0, HALF // TN, norm2, (zero_row, zero_row))
    d2 = core_send(M.at[own_rows], M.at[own_rows], 9)
    d2.start()
    NG[...] = jnp.zeros(NG.shape, F32)
    NG[1:2, :] = dg1
    NG[3:4, :] = db1

    for p in range(NPARTS):
        ag_sent(p)

    act_home = pltpu.make_async_copy(C, act_out, sM.at[10])
    act_away = rc(C, act_out, sM.at[10], rM.at[10], dev_d)

    @pl.when(native)
    def _():
        act_home.start()

    @pl.when(away)
    def _():
        act_away.start()

    land = {p: p for p in range(NPARTS)}
    land[PG + 2] = PD + 1
    land[PG + 3] = PD
    land[PQ] = PG + 3
    land[PK] = PG + 2
    land[PO] = PG + 4
    land[PV] = PG + 5
    credits = {PD: [PD, PG + 3], PD + 1: [PG + 2], PD + 2: [PD + 2]}
    credits["mid"] = [PG, PG + 1, PG + 4, PG + 5, PQ, PK, PO, PV]

    def wland(p, zz, yy):
        if p == PD + 1:
            return LD.at[zz]
        return W.at[rows_of(zz, yy), pl.ds(cols[land[p]][0], cols[p][1])]

    def credit(k):
        @pl.when(native)
        def _():
            for p in credits[k]:
                pl.semaphore_signal(cred.at[p], inc=1, device_id=dev_x, device_id_type=MESH_ID)

    def x_block(p, d):
        zz = zof(d)
        yy = lax.rem(zz + p + 1, 2)
        return rc(blk(G, p, zz, yy), wland(p, zz, yy), sX.at[p], rX.at[p, d], dev_x)

    def y_block(p, d):
        return rc(blk(G, p, zof(d), 1 - y), Ly.at[zof(d), :, cslice(p)], sY.at[p], rY.at[p, d], dev_y)

    def y_arrival(p, d):
        return rc(blk(G, p, zof(d), y), Ly.at[zof(d), :, cslice(p)], sY.at[p], rY.at[p, d], dev_y)

    def z_block(p, d):
        return rc(blk(G, p, zof(d), y), Lz.at[d - 1, :, cslice(p)], sZ.at[p], rZ.at[p], dev_z(d))

    def x_final(p):
        return rc(blk(G, p, z, y), Lx.at[:, cslice(p)], sXF.at[p], rXF.at[p], dev_x)

    def out_copies(p):
        lo = pl.multiple_of(c * SH, 16)
        c0, n = cols[p]
        if p in (PQ, PK, PV):
            pieces = [(c0, n, gq_out.at[p])]
        elif p == PO:
            pieces = [(c0, n, go_out)]
        elif p < PD:
            j = p - PG
            pieces = [(c0 + i * GH, GH, ggu_out.at[i, :, pl.ds(j * GH, GH)]) for i in range(2)]
        else:
            pieces = [(c0, n, gd_out.at[:, pl.ds((p - PD) * CH, CH)])]
        return [
            pltpu.make_async_copy(F.at[pl.ds(lo, SH), pl.ds(a, m)], dst, sO.at[p])
            for a, m, dst in pieces
        ]

    def f_rows(core):
        return pl.ds(pl.multiple_of(core * SH, 16), SH)

    def f_send(p):
        part = F.at[f_rows(oc), cslice(p)]
        return rc(part, part, sF.at[p], rF.at[p], dev_c)

    def f_arrival(p):
        part = F.at[f_rows(c), cslice(p)]
        return rc(part, part, sF.at[p], rF.at[p], dev_c)

    def rs1(p):
        def gy(d, carry):
            when(crosses_first(p, zof(d), 1 - y), lambda: y_block(p, d).start())
            return carry
        lax.fori_loop(0, 4, gy, 0)

        @pl.when(away)
        def _():
            if p != PD + 1:
                pl.semaphore_wait(cred.at[p], 1)

            def go(d, carry):
                x_block(p, d).start()
                return carry
            lax.fori_loop(0, 4, go, 0)

    def rs1n(p, d):
        zz = zof(d)

        @pl.when(both(native, jnp.logical_not(crosses_first(p, zz, 1 - y))))
        def _():
            x_block(p, d).wait_recv()
            rows = rows_of(zz, 1 - y)
            G[rows, cslice(p)] = (G[rows, cslice(p)].astype(F32) + wland(p, zz, 1 - y)[...].astype(F32)).astype(BF)
            y_block(p, d).start()

    def rs2(p, i):
        d = lax.rem(i + 1, 4)
        zz = zof(d)
        rows = rows_of(zz, y)
        first = crosses_first(p, zz, y)

        def finish(total):
            G[rows, cslice(p)] = total.astype(BF)
            when(d > 0, lambda: z_block(p, d).start())

        @pl.when(both(native, jnp.logical_not(first)))
        def _():
            x_block(p, d).wait_recv()
            y_arrival(p, d).wait_recv()
            finish(G[rows, cslice(p)].astype(F32) + Ly[zz, :, cslice(p)].astype(F32) + wland(p, zz, y)[...].astype(F32))

        @pl.when(first)
        def _():
            y_arrival(p, d).wait_recv()
            finish(G[rows, cslice(p)].astype(F32) + Ly[zz, :, cslice(p)].astype(F32))

    def rs3(p):
        own_first = crosses_first(p, z, y)

        def total():
            three = Lz.at[:, :, cslice(p)]
            pltpu.make_async_copy(three, three, rZ.at[p]).wait()
            out = G[rows_of(z, y), cslice(p)].astype(F32)
            for k in range(3):
                out = out + Lz[k, :, cslice(p)].astype(F32)
            return out

        @pl.when(native)
        def _():
            F[:, cslice(p)] = total()

        @pl.when(both(away, own_first))
        def _():
            G[rows_of(z, y), cslice(p)] = total().astype(BF)
            x_final(p).start()

    def rs4(p):
        @pl.when(native)
        def _():
            @pl.when(crosses_first(p, z, y))
            def _():
                x_final(p).wait_recv()
                F[:, cslice(p)] = F[:, cslice(p)] + Lx[:, cslice(p)].astype(F32)
            f_send(p).start()

        when(away, lambda: f_arrival(p).wait_recv())
        for cp in out_copies(p):
            cp.start()

    def rs_sent(p):
        own_first = crosses_first(p, z, y)

        @pl.when(native)
        def _():
            wait_bytes(p, 4, sY.at[p])
            wait_bytes(p, 3, sZ.at[p])
            f_send(p).wait_send()

        @pl.when(away)
        def _():
            wait_bytes(p, 4, sX.at[p])
            wait_bytes(p, 2, sY.at[p])

            @pl.when(own_first)
            def _():
                wait_bytes(p, 1, sZ.at[p])
                x_final(p).wait_send()
            when(jnp.logical_not(own_first), lambda: wait_bytes(p, 2, sZ.at[p]))

        part = F.at[f_rows(c), cslice(p)]
        pltpu.make_async_copy(part, part, sO.at[p]).wait()

    kinds.update({"rs1": rs1, "rs1n": rs1n, "rs2": rs2, "rs3": rs3, "rs4": rs4})
    order = [PD + 1, PG + 2, PD, PG + 3, PD + 2, PG, PG + 1, PG + 4, PG + 5, PO, PV, PQ, PK]
    assert not queue
    for i in range(NPARTS + 9):
        for name, lag in (("rs1n", 1), ("rs2", 2), ("rs3", 5), ("rs4", 9)):
            if 0 <= i - lag < NPARTS:
                queue.append((name, order[i - lag]))

    def transpose_half(src, dst, first_row):
        def body(i):
            r = pl.multiple_of(first_row + i * TR, TR)
            dst[:, pl.ds(r, TR)] = src[pl.ds(r, TR), :].T
        loop(HALF // TR, body)

    transpose_half(M, DT, own_r)
    rc(M.at[oth_rows], M.at[oth_rows], sM.at[9], rM.at[9], dev_c).wait_recv()
    transpose_half(M, DT, oth_r)

    def back_chunk(j, *events):
        hc = pl.ds(j * CH, CH)

        def body(i):
            r = pl.multiple_of(i * TR, TR)
            rows = pl.ds(r, TR)
            dh = nn(M[rows, :], W[:, wcols(PD + j)]).astype(BF).astype(F32)
            gate = GT[rows, hc].astype(F32)
            up = UP[rows, hc].astype(F32)
            sg = sigmoid(gate)
            GT[rows, hc] = (dh * up * (sg * (1.0 + gate * (1.0 - sg)))).astype(BF)
            UP[rows, hc] = (dh * gate * sg).astype(BF)
        loop(LEN // TR, body, *events)

    WR = D // 4

    def weight_grad(left, pieces, *events):
        def body(i):
            r = pl.multiple_of(i * WR, 64)
            for right, a, n, c0 in pieces:
                G[pl.ds(r, WR), pl.ds(c0, n)] = nn(left[pl.ds(r, WR), :], right[:, pl.ds(a, n)]).astype(BF)
        loop(4, body, *events)

    def grads_down(j, *events):
        weight_grad(DT, [(H, j * CH, CH, cols[PD + j][0])], *events)

    def grads_gate_up(g, *events):
        c0 = cols[PG + g][0]
        weight_grad(MT, [(GT, g * GH, GH, c0), (UP, g * GH, GH, c0 + GH)], *events)

    def now(p):
        rs1(p)

    def take(name, p):
        queue.remove((name, p))
        queue.insert(0, (name, p))
        step()

    grads_down(1)
    now(PD + 1)
    back_chunk(1)
    credit(PD + 1)
    grads_gate_up(2)
    now(PG + 2)
    grads_gate_up(3)
    back_chunk(0, ("rs1n", PD + 1))
    credit(PD)
    grads_down(0)
    now(PD)
    grads_gate_up(0, ("rs1n", PG + 2))
    grads_gate_up(1, ("rs2", PD + 1))
    now(PG + 3)
    back_chunk(2, ("rs1n", PD))
    credit(PD + 2)
    grads_down(2, ("rs2", PG + 2))
    now(PD + 2)
    grads_gate_up(4, ("rs1n", PG + 3))
    grads_gate_up(5, ("rs2", PD))

    mid_terms = []
    for g in range(NG_PARTS):
        mid_terms.append((GT, g * GH, GH, cols[PG + g][0]))
        mid_terms.append((UP, g * GH, GH, cols[PG + g][0] + GH))
    part1.wait_send()
    partial(mid_terms, oth_r, to_x)
    part2 = core_send(X.at[oth_rows], R, 11)
    part2.start()

    def to_n2_add(r, acc):
        N2[pl.ds(r, TR), :] = N2[pl.ds(r, TR), :] + acc
    partial(mid_terms, own_r, to_n2_add)
    credit("mid")
    now(PG)
    d2.wait_send()
    part2.wait_recv()

    def norm1_back(i, carry):
        dg, db = carry
        r = pl.multiple_of(i * TN, TN)
        rows = pl.ds(r, TN)
        e = N2[rows, :] + R[rows, :].astype(F32)
        n = N1[rows, :]
        rs = RS1[rows, 0:1]
        eg = e * NV[0:1, :]
        m1 = jnp.sum(eg, axis=1, keepdims=True) * inv_d
        m2 = jnp.sum(eg * n, axis=1, keepdims=True) * inv_d
        d = rs * (eg - m1 - n * m2)
        N2[rows, :] = d
        M[pl.ds(own_r + r, TN), :] = d.astype(BF)
        return dg + jnp.sum(e * n, axis=0, keepdims=True), db + jnp.sum(e, axis=0, keepdims=True)

    dg0, db0 = lax.fori_loop(0, HALF // TN, norm1_back, (zero_row, zero_row))
    d1 = core_send(M.at[own_rows], M.at[own_rows], 12)
    d1.start()
    NG[0:1, :] = dg0
    NG[2:3, :] = db0
    ng = core_send(NG, NGR, 13)
    ng.start()
    rc(M.at[oth_rows], M.at[oth_rows], sM.at[12], rM.at[12], dev_c).wait_recv()
    transpose_into(M, DT, ("rs1n", PD + 2))
    ng.wait_recv()
    NGT[...] = jnp.zeros(NGT.shape, F32)
    NGT[0:8, :] = NG[...] + NGR[...]
    G[:, norm_cols] = NGT[...].T.astype(BF)

    def d_att(i):
        r = pl.multiple_of(i * TR, TR)
        rows = pl.ds(r, TR)
        da = nn(M[rows, :], W[:, wcols(PO, 0, HC)]).astype(BF)
        UP[rows, pl.ds(0, HC)] = da
        prod = da.astype(F32) * A[rows, :].astype(F32)
        acc = jnp.zeros((TR, 128), F32)
        for k in range(PAIRS):
            piece = prod[:, 128 * k : 128 * (k + 1)]
            d0 = jnp.sum(jnp.where(head0, piece, 0.0), axis=1, keepdims=True)
            dall = jnp.sum(piece, axis=1, keepdims=True)
            acc = jnp.where(lane == 2 * k, d0, jnp.where(lane == 2 * k + 1, dall - d0, acc))
        DEL[rows, :] = acc
    loop(LEN // TR, d_att, ("rs2", PG + 3))
    weight_grad(DT, [(A, 0, HC, cols[PO][0])])
    now(PG + 1)
    take("rs3", PD + 1)
    LST[...] = LSE[...].T[0:8, :]
    DLT[...] = DEL[...].T[0:8, :]

    def attend_back(k, *events):
        pair = slice(128 * k, 128 * (k + 1))
        DQT[...] = jnp.zeros(DQT.shape, F32)

        def body(i):
            r = pl.multiple_of(i * TR, TR)
            rows = pl.ds(r, TR)
            keys = K[rows, pair].astype(F32) * scale
            vals = V[rows, pair]
            qp = Q[:, pair]
            da = UP[:, pair]
            same = SEGC[rows, 0:1] == SEGR[0:1, :]
            dv, dk = [], []
            for s in range(2):
                h = 2 * k + s
                mine = head0 if s == 0 else jnp.logical_not(head0)
                km = jnp.where(mine, keys, 0.0)
                vm = jnp.where(mine, vals.astype(F32), 0.0).astype(BF)
                sc = nt(km.astype(BF), qp)
                pr = jnp.where(same, jnp.exp(sc - LST[h : h + 1, :]), 0.0)
                dp = nt(vm, da)
                ds = (pr * (dp - DLT[h : h + 1, :])).astype(BF)
                dv.append(nn(pr.astype(BF), da))
                dk.append(nn(ds, qp))
                DQT[...] = DQT[...] + nn(km.T.astype(BF), ds)
            GT[rows, 2 * HC + 128 * k : 2 * HC + 128 * (k + 1)] = jnp.where(head0, dv[0], dv[1]).astype(BF)
            GT[rows, HC + 128 * k : HC + 128 * (k + 1)] = unrot(jnp.where(head0, dk[0], dk[1]) * scale, r, TR).astype(BF)
        loop(LEN // TR, body, *events)

        def finish(i):
            r = pl.multiple_of(i * 128, 128)
            GT[pl.ds(r, 128), pair] = unrot(DQT[:, pl.ds(r, 128)].T, r, 128).astype(BF)
        loop(LEN // 128, finish)

    now(PG + 4)
    attend_back(0, ("rs1n", PG), ("rs2", PD + 2))
    take("rs3", PG + 2)
    now(PG + 5)
    attend_back(1, ("rs1n", PG + 1), ("rs2", PG), ("rs1n", PG + 4))
    take("rs3", PD)
    now(PO)
    attend_back(2, ("rs2", PG + 1), ("rs1n", PG + 5), ("rs2", PG + 4))
    take("rs3", PG + 3)

    weight_grad(XT, [(GT, 2 * HC, HC, cols[PV][0])], ("rs1n", PO))
    now(PV)
    weight_grad(XT, [(GT, 0, HC, cols[PQ][0])], ("rs2", PG + 5))
    now(PQ)
    weight_grad(XT, [(GT, HC, HC, cols[PK][0])])
    now(PK)

    in_terms = [(GT, 0, 3 * HC, 0)]
    part2.wait_send()
    partial(in_terms, oth_r, to_x)
    part3 = core_send(X.at[oth_rows], R, 14)
    part3.start()
    partial(in_terms, own_r, to_n2_add)

    @pl.when(native)
    def _():
        act_home.wait()

    @pl.when(away)
    def _():
        act_away.wait_send()

    part3.wait_recv()

    gtok_home = pltpu.make_async_copy(N2, gtok_out, sM.at[15])
    gtok_away = rc(C, GL, sM.at[15], rM.at[15], dev_d)

    def add_rows(i):
        r = pl.multiple_of(i * TN, TN)
        rows = pl.ds(r, TN)
        total = N2[rows, :] + R[rows, :].astype(F32)
        N2[rows, :] = total
        C[rows, :] = total.astype(BF)
    loop(HALF // TN, add_rows)

    @pl.when(native)
    def _():
        gtok_home.start()

    @pl.when(away)
    def _():
        gtok_away.start()

    while queue:
        step()

    @pl.when(away)
    def _():
        rc(C, GL, sM.at[15], rM.at[15], dev_d).wait_recv()
        N1[...] = GL[...].astype(F32)
        out = pltpu.make_async_copy(N1, gtok_out, sM.at[16])
        out.start()
        out.wait()
        gtok_away.wait_send()
        rc(C, act_out, sM.at[10], rM.at[10], dev_d).wait_recv()
        tok_away.wait_send()
        cot_away.wait_send()

    @pl.when(native)
    def _():
        gtok_home.wait()
        seg_send.wait_send()

    d1.wait_send()
    ng.wait_send()
    part3.wait_send()
    for p in range(NPARTS):
        rs_sent(p)


def on_device_fused(
    tokens, segments, qkv_weight, out_weight, gate_up_weight, down_weight, norm_gain, norm_shift, cotangent
):
    length, width = segments.shape[1], tokens.shape[1]
    half = tokens.shape[0]
    hc, fc = qkv_weight.shape[3], gate_up_weight.shape[3]
    sh = qkv_weight.shape[2]
    nc = 4 * hc + 128 + 3 * fc
    cosine, sine = rope_numpy(length)
    vm = pl.BlockSpec(memory_space=pltpu.VMEM)
    anyspec = pl.BlockSpec(memory_space=pl.ANY)
    V_ = pltpu.VMEM
    br = 2 * sh
    dma = pltpu.SemaphoreType.DMA
    scratch = [
        V_((width, nc), BF),
        V_((width, nc), BF),
        V_((NZ, br, nc), BF),
        V_((NZ - 1, br, nc), BF),
        V_((br, nc), BF),
        V_((br, nc), F32),
        V_((length, width), BF),
        V_((width, length), BF),
        V_((length, hc), BF),
        V_((length, hc), BF),
        V_((length, hc), BF),
        V_((length, hc), BF),
        V_((length, width), BF),
        V_((width, length), BF),
        V_((width, length), BF),
        V_((length, fc), BF),
        V_((length, fc), BF),
        V_((length, fc), BF),
        V_((half, width), BF),
        V_((half, width), BF),
        V_((half, width), F32),
        V_((half, width), F32),
        V_((half, 128), F32),
        V_((128, length), F32),
        V_((length, 128), F32),
        V_((8, length), F32),
        V_((length, 128), F32),
        V_((8, length), F32),
        V_((8, length), F32),
        V_((length, 128), F32),
        V_((8, width), F32),
        V_((8, width), F32),
        V_((8, width), F32),
        V_((128, width), F32),
        V_((half, width), BF),
        V_((NZ, br, fc // 3), BF),
        V_((sh, 128), BF),
        V_((8, sh), F32),
        V_((length, 128), F32),
        V_((length, 128), F32),
        dma((NPARTS,)), dma((NPARTS,)), dma((NPARTS,)), dma((NPARTS,)), dma((NPARTS,)), dma((NPARTS, 8)),
        dma((NPARTS,)), dma((NPARTS, 4)), dma((NPARTS,)), dma((NPARTS,)), dma((NPARTS,)), dma((NPARTS, 4)),
        dma((NPARTS,)), dma((NPARTS,)), dma((NPARTS,)), dma((NPARTS,)), dma((NPARTS,)),
        dma((19,)), dma((17,)),
        pltpu.SemaphoreType.REGULAR((NPARTS,)),
    ]
    act, gtok, gq, go, ggu, gd = pl.pallas_call(
        functools.partial(layer_kernel, (length, width, hc, fc)),
        out_shape=(
            jax.ShapeDtypeStruct((half, width), BF),
            jax.ShapeDtypeStruct((half, width), F32),
            jax.ShapeDtypeStruct((3, sh, hc), F32),
            jax.ShapeDtypeStruct((sh, hc + 128), F32),
            jax.ShapeDtypeStruct((2, sh, fc), F32),
            jax.ShapeDtypeStruct((sh, fc), F32),
        ),
        in_specs=[anyspec, anyspec, vm, anyspec, anyspec, anyspec, anyspec, anyspec, anyspec, vm, vm],
        out_specs=tuple([anyspec] * 6),
        scratch_shapes=scratch,
        compiler_params=pltpu.CompilerParams(
            collective_id=1, has_side_effects=True, vmem_limit_bytes=VMEM_LIMIT
        ),
        name="layer",
    )(
        tokens, cotangent, segments, jnp.asarray(cosine), jnp.asarray(sine),
        qkv_weight, jnp.swapaxes(out_weight, 1, 2), gate_up_weight, jnp.swapaxes(down_weight, 1, 2), norm_gain, norm_shift,
    )
    act, gtok, gq, out_t, ggu, down_t, gain, shift = pl.pallas_call(
        functools.partial(finish_kernel, hc),
        out_shape=(
            jax.ShapeDtypeStruct((half, width), BF),
            jax.ShapeDtypeStruct((half, width), F32),
            jax.ShapeDtypeStruct((1, 3, sh, hc), F32),
            jax.ShapeDtypeStruct((1, sh, hc), F32),
            jax.ShapeDtypeStruct((1, 2, sh, fc), F32),
            jax.ShapeDtypeStruct((1, sh, fc), F32),
            jax.ShapeDtypeStruct((1, 2, sh), F32),
            jax.ShapeDtypeStruct((1, 2, sh), F32),
        ),
        in_specs=[anyspec, anyspec, anyspec, vm, anyspec, anyspec],
        out_specs=tuple([vm] * 8),
        scratch_shapes=[dma((5,))],
        name="finish",
    )(act, gtok, gq, go, ggu, gd)
    return act, gtok, gq, jnp.swapaxes(out_t, 1, 2), ggu, jnp.swapaxes(down_t, 1, 2), gain, shift


def finish_kernel(
    hc, act, gtok, gq, go, ggu, gd, act_out, gtok_out, gq_out, out_out, ggu_out, down_out, gain_out, shift_out, sem
):
    copies = [
        pltpu.make_async_copy(gtok, gtok_out, sem.at[0]),
        pltpu.make_async_copy(act, act_out, sem.at[1]),
        pltpu.make_async_copy(ggu, ggu_out.at[0], sem.at[2]),
        pltpu.make_async_copy(gq, gq_out.at[0], sem.at[3]),
        pltpu.make_async_copy(gd, down_out.at[0], sem.at[4]),
    ]
    for cp in copies:
        cp.start()
    sh = go.shape[0]
    out_out[0] = go[:, 0:hc]
    norms = jnp.concatenate([go[:, hc : hc + 128], jnp.zeros((128 - sh, 128), F32)], axis=0).T[:, 0:sh]
    gain_out[0] = norms[0:2, :]
    shift_out[0] = norms[2:4, :]
    for cp in copies:
        cp.wait()


VMEM_LIMIT = 64 * 1024 * 1024


def solution(mesh):
    body = on_device_fused if dict(mesh.shape) == {"fsdp": 16, "tp": 2} else on_device
    placed = (
        P(("fsdp", "tp"), None),
        P("fsdp", None),
        P(None, None, "fsdp", "tp"),
        P(None, "tp", "fsdp"),
        P(None, None, "fsdp", "tp"),
        P(None, "tp", "fsdp"),
        P(None, None, "fsdp"),
        P(None, None, "fsdp"),
        P(("fsdp", "tp"), None),
    )
    return jax.shard_map(
        body,
        mesh=mesh,
        in_specs=placed,
        out_specs=(
            P(("fsdp", "tp"), None),
            P(("fsdp", "tp"), None),
            P(None, None, "fsdp", "tp"),
            P(None, "tp", "fsdp"),
            P(None, None, "fsdp", "tp"),
            P(None, "tp", "fsdp"),
            P(None, None, "fsdp"),
            P(None, None, "fsdp"),
        ),
        check_vma=False,
    )
```
